32 devices in a mesh: req: 2 (over y), patch: 16 (over z, x, core).
Axes of the slice: x: 2, y: 2, z: 4, core: 2. Of those that a mesh axis runs over, the one named last changes fastest.
Arguments:
- queries: bfloat16 [8, 128, 4096], P('req', 'patch'), parts along dimension 0, may hold values from -5 to 5
- keys: bfloat16 [8, 128, 4096], P('req', 'patch'), parts along dimension 0, may hold values from -5 to 5
- values: bfloat16 [8, 128, 4096], P('req', 'patch'), parts along dimension 0, may hold values from -6 to 6
- q_gain: float32 [4096], replicated, may hold values from 1.5 to 6
- k_gain: float32 [4096], replicated, may hold values from 1.5 to 6
- stale_cache: bfloat16 [256, 128, 256], P(('req', 'patch')), parts along dimension 0, may hold values from -8 to 8
- coords: int32 [3, 128], P(None, 'patch'), may hold values from 0 to 63
Outputs:
- attended: bfloat16 [8, 128, 4096], P('req', 'patch'), parts along dimension 0
- next_cache: bfloat16 [256, 128, 256], P(('req', 'patch')), parts along dimension 0
The draws below stay inside these ranges and needn't reach their ends.
There are 2 independent parts, one for each index of `req`. The reference program is written for one: setup_inputs(seed, part) draws one part's arguments, and reference() takes and returns one part's arrays. A program takes and returns all parts, laid end to end along the dimension named above; an argument that names none is the same for every part. Nothing has to cross between parts.
All inputs are finite; a program needn't handle non-finite values.
Results may differ from the reference program's by a relative error of at most 0.012.
The reference program's roundings to bfloat16 on the way (of `qn`, `kn` and `probs`) count: a program that leaves them out, or rounds other values in their place, can miss the bound.
Values may be sent and summed in bfloat16 or wider, within the bound.
No kernel may reach another device: no remote copies, remote signals or barrier semaphores. Data moves between devices by JAX's collectives and lax.ppermute only.
A program may use at most 128 MiB of HBM per device.

```python
import math
import jax
import jax.numpy as jnp
from jax import lax

DH = 128
HEADS = 32
VIDEOS = 4
TOK_DEV = 8
TOKENS = 128
WIDTH = 4096


def shared_base(key):
    return jax.random.normal(key, (VIDEOS, TOKENS, HEADS * DH), jnp.float32)


def draw_keys(key, part):
    base = shared_base(key)
    return jnp.clip(base, -5.0, 5.0).astype(jnp.bfloat16)


def draw_queries(key, part):
    key = jax.random.fold_in(key, 23)
    own = jax.random.normal(key, (VIDEOS, TOKENS, HEADS * DH), jnp.float32)
    return jnp.clip(own, -5.0, 5.0).astype(jnp.bfloat16)


def gain_draw(key, lower, upper):
    return jax.random.uniform(key, (HEADS * DH,), jnp.float32, lower, upper)


def draw_q_gain(key, part):
    key = jax.random.fold_in(key, 31)
    return jnp.exp(gain_draw(key, jnp.log(1.5), jnp.log(3.5)))


def draw_k_gain(key, part):
    key = jax.random.fold_in(key, 41)
    return jnp.exp(gain_draw(key, jnp.log(1.5), jnp.log(3.5)))


def with_ends(entries, key, low, largest):
    spot = [jax.random.randint(jax.random.fold_in(key, axis), (), 0, length) for axis, length in enumerate(entries.shape)]
    main_axis = entries.shape.index(max(entries.shape))
    beside = spot[:main_axis] + [(spot[main_axis] + 1) % entries.shape[main_axis]] + spot[main_axis + 1:]
    return entries.at[tuple(spot)].set(low).at[tuple(beside)].set(largest)


def level_of(key, extent, cuts, least, high):
    def one(dim, shards_of):
        steps = jax.random.uniform(jax.random.fold_in(jax.random.fold_in(key, 6), dim), (shards_of,), jnp.float32, least / len(cuts), high / len(cuts))
        return jnp.repeat(jnp.exp(steps), extent[dim] // shards_of).reshape((-1,) + (1,) * (len(extent) - dim - 1))

    level = one(*cuts[0])
    for cut in cuts[1:]:
        level = level * one(*cut)
    return level


def gaussian(rng, dims, scale, bound, cuts=(), kind=jnp.bfloat16):
    level = level_of(rng, dims, cuts, -0.22, 0.18) if cuts else 1.0
    entries = jax.random.normal(rng, dims, jnp.float32) * scale * level
    return jnp.minimum(jnp.maximum(entries, -bound), bound).astype(kind)


def setup_inputs(seed: int = 0, part: int = 0) -> dict:
    arg_keys = jax.random.split(jax.random.key(seed), 8)
    part_keys = jax.random.split(jax.random.fold_in(arg_keys[7], part), 8)
    queries = draw_queries(jax.random.fold_in(jax.random.fold_in(arg_keys[7], part), 71), part)
    keys = draw_keys(jax.random.fold_in(jax.random.fold_in(arg_keys[7], part), 71), part)
    values = gaussian(part_keys[2], (VIDEOS, TOKENS, WIDTH), 1.0, 6.0, ((1, 16),))
    q_gain = draw_q_gain(jax.random.fold_in(arg_keys[7], 71), part)
    k_gain = draw_k_gain(jax.random.fold_in(arg_keys[7], 71), part)
    stale_cache = gaussian(part_keys[5], (VIDEOS * HEADS, TOKENS, 2 * DH), 1.5, 8.0, ((0, 16),))
    coords = with_ends(jax.random.randint(arg_keys[6], (3, TOKENS), 0, 64), jax.random.fold_in(arg_keys[6], 1), 0, 63).astype(jnp.int32)
    return {"queries": queries, "keys": keys, "values": values, "q_gain": q_gain, "k_gain": k_gain, "stale_cache": stale_cache, "coords": coords}


def rotate(field, coords):
    videos, rows, width = field.shape
    half = DH // 2
    side = DH // 6
    first = half - 2 * side
    place = coords.astype(jnp.float32)

    def freqs(count):
        return 10000.0 ** (-jnp.arange(count, dtype=jnp.float32) / count)
    angle = jnp.concatenate([place[0][:, None] * freqs(first), place[1][:, None] * freqs(side), place[2][:, None] * freqs(side)], axis=1)
    cosine = jnp.cos(angle)[None, :, None, :]
    sine = jnp.sin(angle)[None, :, None, :]
    split = field.reshape(videos, rows, width // DH, half, 2)
    real_part = split[..., 0]
    imag_part = split[..., 1]
    turned = jnp.stack([real_part * cosine - imag_part * sine, real_part * sine + imag_part * cosine], axis=-1)
    return turned.reshape(videos, rows, width)

def prepare(field, gain, coords):
    wide = field.astype(jnp.float32)
    meansq = lax.optimization_barrier(jnp.mean(wide * wide, axis=-1, keepdims=True))
    normed = wide * lax.rsqrt(meansq + 1e-06) * gain
    return rotate(normed, coords).astype(jnp.bfloat16)

def to_pairs(field):
    videos, rows, width = field.shape
    return field.reshape(videos, rows, HEADS, DH).transpose(0, 2, 1, 3).reshape(videos * HEADS, rows, DH)

def reference(queries, keys, values, q_gain, k_gain, stale_cache, coords):
    videos, rows, width = queries.shape
    qn = prepare(queries, q_gain, coords)
    kn = prepare(keys, k_gain, coords)
    next_cache = jnp.concatenate([to_pairs(kn), to_pairs(values)], axis=-1)
    query_pairs = to_pairs(qn)
    patch_of = jnp.arange(rows) // TOK_DEV
    same = patch_of[:, None] == patch_of[None, :]
    scale = 1.0 / math.sqrt(DH)

    def one_pair(items):
        query_rows, fresh, stale = items
        fresh_scores = jnp.dot(query_rows, fresh[:, :DH].T, preferred_element_type=jnp.float32) * scale
        stale_scores = jnp.dot(query_rows, stale[:, :DH].T, preferred_element_type=jnp.float32) * scale
        scores = jnp.where(same, fresh_scores, stale_scores)
        top = lax.optimization_barrier(jnp.max(scores, axis=-1, keepdims=True))
        weights = jnp.exp(scores - top)
        total = lax.optimization_barrier(jnp.sum(weights, axis=-1, keepdims=True))
        probs = weights.astype(jnp.bfloat16)
        zero = jnp.zeros_like(probs)
        summed = jnp.dot(jnp.where(same, probs, zero), fresh[:, DH:], preferred_element_type=jnp.float32)
        summed = summed + jnp.dot(jnp.where(same, zero, probs), stale[:, DH:], preferred_element_type=jnp.float32)
        return (summed / total).astype(jnp.bfloat16)
    result = lax.map(one_pair, (query_pairs, next_cache, stale_cache))
    attended = result.reshape(videos, HEADS, rows, DH).transpose(0, 2, 1, 3).reshape(videos, rows, width)
    return (attended, next_cache)
```

```python
import functools
import math

import jax
import jax.numpy as jnp
from jax import lax
from jax.experimental import pallas as pl
from jax.experimental.pallas import tpu as pltpu
from jax.sharding import PartitionSpec as P

DH = 128
VMEM = pl.BlockSpec(memory_space=pltpu.VMEM)
SMEM = pl.BlockSpec(memory_space=pltpu.SMEM)


def rope_tables(coords_ref, tok_rows):
    half = DH // 2
    side = DH // 6
    first = half - 2 * side
    shape = (tok_rows, DH)
    row = lax.broadcasted_iota(jnp.int32, shape, 0)
    lane = lax.broadcasted_iota(jnp.int32, shape, 1)
    pair = lane // 2
    axis = (pair >= first).astype(jnp.int32) + (pair >= first + side).astype(jnp.int32)
    place = jnp.zeros(shape, jnp.int32)
    for which in range(3):
        for token in range(tok_rows):
            place = jnp.where((axis == which) & (row == token), coords_ref[which, token], place)
    step = jnp.where(axis == 0, pair, jnp.where(axis == 1, pair - first, pair - first - side))
    count = jnp.where(axis == 0, float(first), float(side))
    freq = jnp.exp(step.astype(jnp.float32) / count * (-math.log(10000.0)))
    angle = place.astype(jnp.float32) * freq
    sine = jnp.sin(angle)
    even = lane % 2 == 0
    return jnp.cos(angle), jnp.where(even, -sine, 0.0), jnp.where(even, 0.0, sine)


def prepare_kernel(heads_here, q_ref, k_ref, v_ref, q_gain_ref, k_gain_ref, coords_ref, out_ref):
    videos, tok_rows, width = q_ref.shape
    groups = width // (DH * heads_here)
    cosine, sine_even, sine_odd = rope_tables(coords_ref, tok_rows)
    for video in range(videos):
        for part, (ref, gain_ref) in enumerate(((q_ref, q_gain_ref), (k_ref, k_gain_ref))):
            wide = ref[video].astype(jnp.float32)
            meansq = jnp.sum(wide * wide, axis=-1, keepdims=True) * (1.0 / width)
            inverse = lax.rsqrt(meansq + 1e-06)
            for head in range(width // DH):
                here = slice(head * DH, (head + 1) * DH)
                y = ref[video, :, here].astype(jnp.float32) * inverse * gain_ref[:, here]
                turned = (
                    y * cosine
                    + pltpu.roll(y, DH - 1, 1) * sine_even
                    + pltpu.roll(y, 1, 1) * sine_odd
                )
                start = (head % heads_here * 3 + part) * DH
                out_ref[video * groups + head // heads_here, :, start : start + DH] = turned.astype(
                    jnp.bfloat16
                )
        for head in range(width // DH):
            start = (head % heads_here * 3 + 2) * DH
            out_ref[video * groups + head // heads_here, :, start : start + DH] = v_ref[
                video, :, head * DH : (head + 1) * DH
            ]


def attend_kernel(tok_rows, got_ref, stale_ref, attended_ref, cache_ref):
    pairs_here, total_rows, _ = stale_ref.shape
    scale = 1.0 / math.sqrt(DH)
    block = min(total_rows, 128)
    dims = (((1,), (1,)), ((), ()))
    for pair in range(pairs_here):
        fresh = got_ref[:, (pair * 3 + 1) * DH : (pair * 3 + 3) * DH]
        cache_ref[pair] = fresh
        stale = stale_ref[pair]
        for start in range(0, total_rows, block):
            query = got_ref[start : start + block, pair * 3 * DH : (pair * 3 + 1) * DH]
            shape = (block, total_rows)
            same = (start + lax.broadcasted_iota(jnp.int32, shape, 0)) // tok_rows == (
                lax.broadcasted_iota(jnp.int32, shape, 1) // tok_rows
            )
            fresh_scores = lax.dot_general(
                query, fresh[:, :DH], dims, preferred_element_type=jnp.float32
            )
            stale_scores = lax.dot_general(
                query, stale[:, :DH], dims, preferred_element_type=jnp.float32
            )
            scores = jnp.where(same, fresh_scores, stale_scores) * scale
            top = jnp.max(scores, axis=-1, keepdims=True)
            weights = jnp.exp(scores - top)
            total = jnp.sum(weights, axis=-1, keepdims=True)
            summed = jnp.dot(
                jnp.where(same, weights, 0.0).astype(jnp.bfloat16),
                fresh[:, DH:],
                preferred_element_type=jnp.float32,
            ) + jnp.dot(
                jnp.where(same, 0.0, weights).astype(jnp.bfloat16),
                stale[:, DH:],
                preferred_element_type=jnp.float32,
            )
            attended_ref[start : start + block, pair * DH : (pair + 1) * DH] = (
                summed / total
            ).astype(jnp.bfloat16)


def local(queries, keys, values, q_gain, k_gain, stale_cache, coords):
    videos, tok_rows, width = queries.shape
    pairs_here, total_rows, _ = stale_cache.shape
    patches = total_rows // tok_rows
    params = pltpu.CompilerParams(vmem_limit_bytes=40 * 1024 * 1024)
    sent = pl.pallas_call(
        functools.partial(prepare_kernel, pairs_here),
        out_shape=jax.ShapeDtypeStruct((patches, tok_rows, pairs_here * 3 * DH), jnp.bfloat16),
        in_specs=[VMEM] * 5 + [SMEM],
        out_specs=VMEM,
        compiler_params=params,
        name="prepare",
    )(queries, keys, values, q_gain.reshape(1, width), k_gain.reshape(1, width), coords)
    got = lax.all_to_all(sent, "patch", split_axis=0, concat_axis=0, tiled=True)
    attended, next_cache = pl.pallas_call(
        functools.partial(attend_kernel, tok_rows),
        out_shape=(
            jax.ShapeDtypeStruct((total_rows, pairs_here * DH), jnp.bfloat16),
            jax.ShapeDtypeStruct(stale_cache.shape, jnp.bfloat16),
        ),
        in_specs=[VMEM] * 2,
        out_specs=(VMEM, VMEM),
        compiler_params=params,
        name="attend",
    )(got.reshape(total_rows, pairs_here * 3 * DH), stale_cache)
    back = lax.all_to_all(
        attended.reshape(patches, tok_rows, pairs_here * DH), "patch", split_axis=0, concat_axis=0, tiled=True
    )
    attended = jnp.transpose(
        back.reshape(videos, patches // videos, tok_rows, pairs_here * DH), (0, 2, 1, 3)
    ).reshape(videos, tok_rows, width)
    return (attended, next_cache)


def solution(mesh):
    in_specs = (
        P("req", "patch", None),
        P("req", "patch", None),
        P("req", "patch", None),
        P(),
        P(),
        P(("req", "patch"), None, None),
        P(None, "patch"),
    )
    out_specs = (P("req", "patch", None), P(("req", "patch"), None, None))
    return jax.shard_map(local, mesh=mesh, in_specs=in_specs, out_specs=out_specs, check_vma=False)
```

```python
import functools
import math

import jax
import jax.numpy as jnp
from jax import lax
from jax.experimental import pallas as pl
from jax.experimental.pallas import tpu as pltpu
from jax.sharding import PartitionSpec as P

DH = 128
VMEM = pl.BlockSpec(memory_space=pltpu.VMEM)
HBM = pl.BlockSpec(memory_space=pltpu.HBM)
PARAMS = pltpu.CompilerParams(vmem_limit_bytes=48 * 1024 * 1024)


def rope_tables(coords_ref, tok_rows):
    half = DH // 2
    side = DH // 6
    first = half - 2 * side
    shape = (tok_rows, DH)
    row = lax.broadcasted_iota(jnp.int32, shape, 0)
    lane = lax.broadcasted_iota(jnp.int32, shape, 1)
    pair = lane // 2
    axis = (pair >= first).astype(jnp.int32) + (pair >= first + side).astype(jnp.int32)
    place = jnp.zeros(shape, jnp.int32)
    for which in range(3):
        for token in range(tok_rows):
            place = jnp.where((axis == which) & (row == token), coords_ref[which, token], place)
    step = jnp.where(axis == 0, pair, jnp.where(axis == 1, pair - first, pair - first - side))
    count = jnp.where(axis == 0, float(first), float(side))
    freq = jnp.exp(step.astype(jnp.float32) / count * (-math.log(10000.0)))
    angle = place.astype(jnp.float32) * freq
    sine = jnp.sin(angle)
    even = lane % 2 == 0
    return jnp.cos(angle), jnp.where(even, -sine, 0.0), jnp.where(even, 0.0, sine)


def prepare_kernel(pairs_here, patches, *refs):
    sources, outs, scratch = refs[:6], refs[6 : 6 + patches], refs[6 + patches :]
    held, inverse_ref, sems = scratch[:6], scratch[6], scratch[7]
    copies = [
        pltpu.make_async_copy(source, place, sems.at[i])
        for i, (source, place) in enumerate(zip(sources, held))
    ]
    for i in (5, 0, 3, 1, 4, 2):
        copies[i].start()
    q_ref, k_ref, v_ref, q_gain_ref, k_gain_ref, coords_ref = held
    videos, tok_rows, width = q_ref.shape
    groups = width // (DH * pairs_here)
    span = pairs_here * DH
    me = lax.axis_index("patch")
    copies[5].wait()
    cosine, sine_even, sine_odd = rope_tables(coords_ref, tok_rows)
    for part, ref in enumerate((q_ref, k_ref)):
        copies[part].wait()
        for video in range(videos):
            wide = ref[video].astype(jnp.float32)
            meansq = jnp.sum(wide * wide, axis=-1, keepdims=True) * (1.0 / width)
            inverse_ref[part, video] = jnp.broadcast_to(lax.rsqrt(meansq + 1e-06), (tok_rows, DH))
    for i in (3, 4, 2):
        copies[i].wait()
    for s in range(patches):
        target = me ^ s
        video = target // groups
        lanes = pl.ds(pl.multiple_of((target % groups) * span, DH), span)
        for part, (ref, gain_ref) in enumerate(((q_ref, q_gain_ref), (k_ref, k_gain_ref))):
            wide = ref[video, :, lanes].astype(jnp.float32)
            gain = gain_ref[:, lanes]
            inverse = inverse_ref[part, video]
            for pair in range(pairs_here):
                here = slice(pair * DH, (pair + 1) * DH)
                y = wide[:, here] * inverse * gain[:, here]
                turned = (
                    y * cosine
                    + pltpu.roll(y, DH - 1, 1) * sine_even
                    + pltpu.roll(y, 1, 1) * sine_odd
                )
                start = (pair * 3 + part) * DH
                outs[s][:, start : start + DH] = turned.astype(jnp.bfloat16)
        wide = v_ref[video, :, lanes]
        for pair in range(pairs_here):
            start = (pair * 3 + 2) * DH
            outs[s][:, start : start + DH] = wide[:, pair * DH : (pair + 1) * DH]


def rows_of(refs, start):
    rows = [ref[:, start : start + DH].astype(jnp.float32) for ref in refs]
    return jnp.concatenate(rows, axis=0).astype(jnp.bfloat16)


def attend_kernel(patches, *refs):
    got, stale_ref, outs = refs[:patches], refs[patches], refs[patches + 1 :]
    pairs_here, total_rows, _ = stale_ref.shape
    tok_rows = total_rows // patches
    scale = 1.0 / math.sqrt(DH)
    group = min(patches, max(1, 128 // tok_rows))
    block = group * tok_rows
    dims = (((1,), (1,)), ((), ()))
    me = lax.axis_index("patch")
    row = lax.broadcasted_iota(jnp.int32, (block, block), 0) // tok_rows
    same = row == lax.broadcasted_iota(jnp.int32, (block, block), 1) // tok_rows
    row = lax.broadcasted_iota(jnp.int32, (block, total_rows), 0) // tok_rows
    owner = lax.broadcasted_iota(jnp.int32, (block, total_rows), 1) // tok_rows
    for first in range(0, patches, group):
        here = got[first : first + group]
        own = ((row + first) ^ me) == owner
        for pair in range(pairs_here):
            query = rows_of(here, pair * 3 * DH)
            key = rows_of(here, (pair * 3 + 1) * DH)
            value = rows_of(here, (pair * 3 + 2) * DH)
            stale = stale_ref[pair]
            fresh_scores = lax.dot_general(query, key, dims, preferred_element_type=jnp.float32)
            stale_scores = lax.dot_general(
                query, stale[:, :DH], dims, preferred_element_type=jnp.float32
            )
            scores = jnp.concatenate(
                [
                    jnp.where(same, fresh_scores * scale, -jnp.inf),
                    jnp.where(own, -jnp.inf, stale_scores * scale),
                ],
                axis=1,
            )
            weights = jnp.exp(scores - jnp.max(scores, axis=-1, keepdims=True))
            total = jnp.sum(weights, axis=-1, keepdims=True)
            summed = jnp.dot(
                weights.astype(jnp.bfloat16),
                jnp.concatenate([value, stale[:, DH:]], axis=0),
                preferred_element_type=jnp.float32,
            )
            result = summed * (1.0 / total)
            for i in range(group):
                outs[first + i][:, pair * DH : (pair + 1) * DH] = result[
                    i * tok_rows : (i + 1) * tok_rows
                ].astype(jnp.bfloat16)


def cache_kernel(patches, *refs):
    got, out_ref = refs[:patches], refs[patches]
    me = lax.axis_index("patch")
    for s in range(patches):
        for pair in range(out_ref.shape[0]):
            start = (pair * 3 + 1) * DH
            out_ref[pair, me ^ s] = got[s][:, start : start + 2 * DH]


def gather_kernel(patches, *refs):
    back, out_ref, sem = refs[:patches], refs[patches], refs[patches + 1]
    span = back[0].shape[1]
    groups = out_ref.shape[2] // span
    me = lax.axis_index("patch")
    copies = []
    for s in range(patches):
        source = me ^ s
        lanes = pl.ds(pl.multiple_of((source % groups) * span, DH), span)
        copies.append(
            pltpu.make_async_copy(back[s], out_ref.at[source // groups, :, lanes], sem.at[s])
        )
    for copy in copies:
        copy.start()
    for copy in copies:
        copy.wait()


def exchange(arrays):
    patches = len(arrays)
    return [arrays[0]] + [
        lax.ppermute(arrays[s], "patch", [(i, i ^ s) for i in range(patches)])
        for s in range(1, patches)
    ]


def local(queries, keys, values, q_gain, k_gain, stale_cache, coords):
    videos, tok_rows, width = queries.shape
    pairs_here, total_rows, _ = stale_cache.shape
    patches = total_rows // tok_rows
    span = pairs_here * DH
    sent = pl.pallas_call(
        functools.partial(prepare_kernel, pairs_here, patches),
        out_shape=[jax.ShapeDtypeStruct((tok_rows, span * 3), jnp.bfloat16)] * patches,
        in_specs=[HBM] * 6,
        out_specs=[VMEM] * patches,
        scratch_shapes=[
            pltpu.VMEM(queries.shape, jnp.bfloat16),
            pltpu.VMEM(queries.shape, jnp.bfloat16),
            pltpu.VMEM(queries.shape, jnp.bfloat16),
            pltpu.VMEM((1, width), jnp.float32),
            pltpu.VMEM((1, width), jnp.float32),
            pltpu.SMEM(coords.shape, jnp.int32),
            pltpu.VMEM((2, videos, tok_rows, DH), jnp.float32),
            pltpu.SemaphoreType.DMA((6,)),
        ],
        compiler_params=PARAMS,
        name="prepare",
    )(queries, keys, values, q_gain.reshape(1, width), k_gain.reshape(1, width), coords)
    got = exchange(sent)
    result = pl.pallas_call(
        functools.partial(attend_kernel, patches),
        out_shape=[jax.ShapeDtypeStruct((tok_rows, span), jnp.bfloat16)] * patches,
        in_specs=[VMEM] * (patches + 1),
        out_specs=[VMEM] * patches,
        compiler_params=PARAMS,
        name="attend",
    )(*got, stale_cache)
    back = exchange(result)
    next_cache = pl.pallas_call(
        functools.partial(cache_kernel, patches),
        out_shape=jax.ShapeDtypeStruct((pairs_here, patches, tok_rows, 2 * DH), jnp.bfloat16),
        in_specs=[VMEM] * patches,
        out_specs=VMEM,
        compiler_params=PARAMS,
        cost_estimate=pl.CostEstimate(flops=0, bytes_accessed=stale_cache.size * 4, transcendentals=0),
        name="cache",
    )(*got)
    attended = pl.pallas_call(
        functools.partial(gather_kernel, patches),
        out_shape=jax.ShapeDtypeStruct(queries.shape, jnp.bfloat16),
        in_specs=[VMEM] * patches,
        out_specs=HBM,
        scratch_shapes=[pltpu.SemaphoreType.DMA((patches,))],
        compiler_params=PARAMS,
        name="gather",
    )(*back)
    return (attended, next_cache.reshape(stale_cache.shape))


def solution(mesh):
    in_specs = (
        P("req", "patch", None),
        P("req", "patch", None),
        P("req", "patch", None),
        P(),
        P(),
        P(("req", "patch"), None, None),
        P(None, "patch"),
    )
    out_specs = (P("req", "patch", None), P(("req", "patch"), None, None))
    return jax.shard_map(local, mesh=mesh, in_specs=in_specs, out_specs=out_specs, check_vma=False)
```

```python
import functools
import math

import jax
import jax.numpy as jnp
from jax import lax
from jax.experimental import pallas as pl
from jax.experimental.pallas import tpu as pltpu
from jax.sharding import PartitionSpec as P

DH = 128
VMEM = pl.BlockSpec(memory_space=pltpu.VMEM)
HBM = pl.BlockSpec(memory_space=pltpu.HBM)
MIB = 1024 * 1024


def rope_tables(coords_ref, tok_rows):
    half = DH // 2
    side = DH // 6
    first = half - 2 * side
    shape = (tok_rows, DH)
    row = lax.broadcasted_iota(jnp.int32, shape, 0)
    lane = lax.broadcasted_iota(jnp.int32, shape, 1)
    pair = lane // 2
    axis = (pair >= first).astype(jnp.int32) + (pair >= first + side).astype(jnp.int32)
    place = jnp.zeros(shape, jnp.int32)
    for which in range(3):
        for token in range(tok_rows):
            place = jnp.where((axis == which) & (row == token), coords_ref[which, token], place)
    step = jnp.where(axis == 0, pair, jnp.where(axis == 1, pair - first, pair - first - side))
    count = jnp.where(axis == 0, float(first), float(side))
    freq = jnp.exp(step.astype(jnp.float32) / count * (-math.log(10000.0)))
    angle = place.astype(jnp.float32) * freq
    sine = jnp.sin(angle)
    even = lane % 2 == 0
    return jnp.cos(angle), jnp.where(even, -sine, 0.0), jnp.where(even, 0.0, sine)


def prepare_kernel(groups, *refs):
    sources, refs = refs[:6], refs[6:]
    videos, tok_rows, width = sources[0].shape
    queries, fresh, refs = refs[:videos], refs[videos : 2 * videos], refs[2 * videos :]
    held, sems = refs[:6], refs[6]
    copies = [
        pltpu.make_async_copy(source, place, sems.at[i])
        for i, (source, place) in enumerate(zip(sources, held))
    ]
    for i in (5, 1, 4, 2, 0, 3):
        copies[i].start()
    q_ref, k_ref, v_ref, q_gain_ref, k_gain_ref, coords_ref = held
    own = lax.axis_index("patch") // groups
    copies[5].wait()
    cosine, sine_even, sine_odd = rope_tables(coords_ref, tok_rows)

    def turned(ref, gain_ref, video):
        wide = ref[video].astype(jnp.float32)
        meansq = jnp.sum(wide * wide, axis=-1, keepdims=True) * (1.0 / width)
        inverse = lax.rsqrt(meansq + 1e-06)
        for head in range(width // DH):
            here = slice(head * DH, (head + 1) * DH)
            y = wide[:, here] * inverse * gain_ref[:, here]
            y = (
                y * cosine
                + pltpu.roll(y, DH - 1, 1) * sine_even
                + pltpu.roll(y, 1, 1) * sine_odd
            )
            yield head, y.astype(jnp.bfloat16)

    for i in (1, 4, 2):
        copies[i].wait()
    for s in range(videos):
        for head, y in turned(k_ref, k_gain_ref, own ^ s):
            fresh[s][:, 2 * head * DH : (2 * head + 1) * DH] = y
            fresh[s][:, (2 * head + 1) * DH : (2 * head + 2) * DH] = v_ref[
                own ^ s, :, head * DH : (head + 1) * DH
            ]
    for i in (0, 3):
        copies[i].wait()
    for s in range(videos):
        for head, y in turned(q_ref, q_gain_ref, own ^ s):
            queries[s][:, head * DH : (head + 1) * DH] = y


def rows_of(refs, start):
    rows = [ref[:, start : start + DH].astype(jnp.float32) for ref in refs]
    return jnp.concatenate(rows, axis=0).astype(jnp.bfloat16)


def attend_kernel(groups, videos, *refs):
    queries, fresh, refs = refs[:videos], refs[videos : 2 * videos], refs[2 * videos :]
    stale_ref, outs = refs[0], refs[1:]
    heads, total_rows, _ = stale_ref.shape
    tok_rows = queries[0].shape[0]
    rows = videos * tok_rows
    scale = 1.0 / math.sqrt(DH)
    dims = (((1,), (1,)), ((), ()))
    me = lax.axis_index("patch")
    row = lax.broadcasted_iota(jnp.int32, (rows, rows), 0) // tok_rows
    same = row == lax.broadcasted_iota(jnp.int32, (rows, rows), 1) // tok_rows
    row = lax.broadcasted_iota(jnp.int32, (rows, total_rows), 0) // tok_rows
    owner = lax.broadcasted_iota(jnp.int32, (rows, total_rows), 1) // tok_rows
    own = (row * groups) ^ me == owner
    for head in range(heads):
        query = rows_of(queries, head * DH)
        key = rows_of(fresh, 2 * head * DH)
        value = rows_of(fresh, (2 * head + 1) * DH)
        stale = stale_ref[head]
        fresh_scores = lax.dot_general(query, key, dims, preferred_element_type=jnp.float32)
        stale_scores = lax.dot_general(
            query, stale[:, :DH], dims, preferred_element_type=jnp.float32
        )
        fresh_scores = jnp.where(same, fresh_scores * scale, -jnp.inf)
        stale_scores = jnp.where(own, -jnp.inf, stale_scores * scale)
        top = jnp.maximum(
            jnp.max(fresh_scores, axis=-1, keepdims=True),
            jnp.max(stale_scores, axis=-1, keepdims=True),
        )
        fresh_weights = jnp.exp(fresh_scores - top)
        stale_weights = jnp.exp(stale_scores - top)
        total = jnp.sum(fresh_weights, axis=-1, keepdims=True) + jnp.sum(
            stale_weights, axis=-1, keepdims=True
        )
        summed = jnp.dot(
            fresh_weights.astype(jnp.bfloat16), value, preferred_element_type=jnp.float32
        ) + jnp.dot(
            stale_weights.astype(jnp.bfloat16), stale[:, DH:], preferred_element_type=jnp.float32
        )
        result = (summed * (1.0 / total)).astype(jnp.bfloat16)
        for s in range(videos):
            outs[s][:, head * DH : (head + 1) * DH] = result[s * tok_rows : (s + 1) * tok_rows]


def pack_kernel(groups, videos, *refs):
    fresh, outs = refs[:videos], refs[videos:]
    span = outs[0].shape[2]
    mine = lax.axis_index("patch") % groups
    for t in range(groups):
        lanes = pl.ds(pl.multiple_of((mine ^ t) * span, DH), span)
        for s in range(videos):
            outs[t][s] = fresh[s][:, lanes]


def cache_kernel(groups, *refs):
    got, out_ref = refs[:groups], refs[groups]
    me = lax.axis_index("patch")
    for t in range(groups):
        for s in range(got[0].shape[0]):
            for pair in range(out_ref.shape[0]):
                out_ref[pair, me ^ (s * groups) ^ t] = got[t][s, :, 2 * pair * DH : 2 * (pair + 1) * DH]


def gather_kernel(groups, videos, *refs):
    back, out_ref, sem = refs[:videos], refs[videos], refs[videos + 1]
    own = lax.axis_index("patch") // groups
    copies = [
        pltpu.make_async_copy(back[s], out_ref.at[own ^ s], sem.at[s]) for s in range(videos)
    ]
    for copy in copies:
        copy.start()
    for copy in copies:
        copy.wait()


def exchange(arrays, stride, patches):
    return [arrays[0]] + [
        lax.ppermute(arrays[s], "patch", [(i, i ^ (s * stride)) for i in range(patches)])
        for s in range(1, len(arrays))
    ]


def local(queries, keys, values, q_gain, k_gain, stale_cache, coords):
    videos, tok_rows, width = queries.shape
    pairs_here, total_rows, _ = stale_cache.shape
    patches = total_rows // tok_rows
    groups = patches // videos
    heads = width // DH
    bf16 = jnp.bfloat16

    def kernel(body, name, limit, **kwargs):
        return pl.pallas_call(
            body, name=name, compiler_params=pltpu.CompilerParams(vmem_limit_bytes=limit * MIB), **kwargs
        )

    planes = [[v * groups + g for g in range(groups)] for v in range(videos)]
    stale_all = lax.all_gather(
        stale_cache, "patch", axis_index_groups=planes, axis=0, tiled=True
    )
    sent = kernel(
        functools.partial(prepare_kernel, groups),
        "prepare",
        61,
        out_shape=[jax.ShapeDtypeStruct((tok_rows, width), bf16)] * videos
        + [jax.ShapeDtypeStruct((tok_rows, 2 * width), bf16)] * videos,
        in_specs=[HBM] * 6,
        out_specs=[VMEM] * (2 * videos),
        scratch_shapes=[
            pltpu.VMEM(queries.shape, bf16),
            pltpu.VMEM(queries.shape, bf16),
            pltpu.VMEM(queries.shape, bf16),
            pltpu.VMEM((1, width), jnp.float32),
            pltpu.VMEM((1, width), jnp.float32),
            pltpu.SMEM(coords.shape, jnp.int32),
            pltpu.SemaphoreType.DMA((6,)),
        ],
    )(queries, keys, values, q_gain.reshape(1, width), k_gain.reshape(1, width), coords)
    fresh = exchange(sent[videos:], groups, patches)
    query = exchange(sent[:videos], groups, patches)
    result = kernel(
        functools.partial(attend_kernel, groups, videos),
        "attend",
        40,
        out_shape=[jax.ShapeDtypeStruct((tok_rows, width), bf16)] * videos,
        in_specs=[VMEM] * (2 * videos + 1),
        out_specs=[VMEM] * videos,
    )(*query, *fresh, stale_all)
    packed = kernel(
        functools.partial(pack_kernel, groups, videos),
        "pack",
        16,
        out_shape=[jax.ShapeDtypeStruct((videos, tok_rows, pairs_here * 2 * DH), bf16)] * groups,
        in_specs=[VMEM] * videos,
        out_specs=[VMEM] * groups,
    )(*fresh)
    spread = exchange(packed, 1, patches)
    back = exchange(result, groups, patches)
    next_cache = kernel(
        functools.partial(cache_kernel, groups),
        "cache",
        16,
        out_shape=jax.ShapeDtypeStruct((pairs_here, patches, tok_rows, 2 * DH), bf16),
        in_specs=[VMEM] * groups,
        out_specs=VMEM,
        cost_estimate=pl.CostEstimate(flops=0, bytes_accessed=stale_cache.size * 4, transcendentals=0),
    )(*spread)
    attended = kernel(
        functools.partial(gather_kernel, groups, videos),
        "gather",
        16,
        out_shape=jax.ShapeDtypeStruct(queries.shape, bf16),
        in_specs=[VMEM] * videos,
        out_specs=HBM,
        scratch_shapes=[pltpu.SemaphoreType.DMA((videos,))],
    )(*back)
    return (attended, next_cache.reshape(stale_cache.shape))


def solution(mesh):
    in_specs = (
        P("req", "patch", None),
        P("req", "patch", None),
        P("req", "patch", None),
        P(),
        P(),
        P(("req", "patch"), None, None),
        P(None, "patch"),
    )
    out_specs = (P("req", "patch", None), P(("req", "patch"), None, None))
    return jax.shard_map(local, mesh=mesh, in_specs=in_specs, out_specs=out_specs, check_vma=False)
```

```python
import functools
import math

import jax
import jax.numpy as jnp
from jax import lax
from jax.experimental import pallas as pl
from jax.experimental.pallas import tpu as pltpu
from jax.sharding import PartitionSpec as P

DH = 128
VMEM = pl.BlockSpec(memory_space=pltpu.VMEM)
HBM = pl.BlockSpec(memory_space=pltpu.HBM)
SMEM = pl.BlockSpec(memory_space=pltpu.SMEM)
MIB = 1024 * 1024
BF16 = jnp.bfloat16
F32 = jnp.float32
TRANSPOSED = (((1,), (1,)), ((), ()))


def rope_tables(coords_ref, tok_rows):
    half = DH // 2
    side = DH // 6
    first = half - 2 * side
    shape = (tok_rows, DH)
    row = lax.broadcasted_iota(jnp.int32, shape, 0)
    lane = lax.broadcasted_iota(jnp.int32, shape, 1)
    pair = lane // 2
    axis = (pair >= first).astype(jnp.int32) + (pair >= first + side).astype(jnp.int32)
    place = jnp.zeros(shape, jnp.int32)
    for which in range(3):
        for token in range(tok_rows):
            place = jnp.where((axis == which) & (row == token), coords_ref[which, token], place)
    step = jnp.where(axis == 0, pair, jnp.where(axis == 1, pair - first, pair - first - side))
    count = jnp.where(axis == 0, float(first), float(side))
    freq = jnp.exp(step.astype(F32) / count * (-math.log(10000.0)))
    angle = place.astype(F32) * freq
    sine = jnp.sin(angle)
    even = lane % 2 == 0
    return jnp.cos(angle), jnp.where(even, -sine, 0.0), jnp.where(even, 0.0, sine)


def normed_heads(wide, gain_ref, tables):
    cosine, sine_even, sine_odd = tables
    width = wide.shape[-1]
    meansq = jnp.sum(wide * wide, axis=-1, keepdims=True) * (1.0 / width)
    inverse = lax.rsqrt(meansq + 1e-06)
    for head in range(width // DH):
        here = slice(head * DH, (head + 1) * DH)
        y = wide[:, here] * inverse * gain_ref[:, here]
        y = y * cosine + pltpu.roll(y, DH - 1, 1) * sine_even + pltpu.roll(y, 1, 1) * sine_odd
        yield head, y.astype(BF16)


def query_kernel(groups, q_hbm, gain_hbm, coords_hbm, *refs):
    videos, tok_rows, width = q_hbm.shape
    outs, tables_ref, refs = refs[:videos], refs[videos], refs[videos + 1 :]
    q_ref, gain_ref, coords_ref, done_ref, sems, out_sems = refs
    own = lax.axis_index("patch") // groups
    copies = [
        pltpu.make_async_copy(source, place, sems.at[i])
        for i, (source, place) in enumerate(
            ((coords_hbm, coords_ref), (q_hbm, q_ref), (gain_hbm, gain_ref))
        )
    ]
    for copy in copies:
        copy.start()
    copies[0].wait()
    tables = rope_tables(coords_ref, tok_rows)
    for i in range(3):
        tables_ref[i] = tables[i]
    copies[1].wait()
    copies[2].wait()
    sends = []
    for s in range(videos):
        for head, y in normed_heads(q_ref[own ^ s].astype(F32), gain_ref, tables):
            done_ref[s, :, head * DH : (head + 1) * DH] = y
        sends.append(pltpu.make_async_copy(done_ref.at[s], outs[s], out_sems.at[s]))
        sends[-1].start()
    for send in sends:
        send.wait()


def key_kernel(k_ref, v_ref, gain_ref, tables_ref, out_ref):
    videos, tok_rows, width = k_ref.shape
    tables = [tables_ref[i] for i in range(3)]
    span = out_ref.shape[2]
    groups = out_ref.shape[0] // videos
    pairs = span // (2 * DH)
    for video in range(videos):
        for head, y in normed_heads(k_ref[video].astype(F32), gain_ref, tables):
            target, start = video * groups + head // pairs, head % pairs * 2 * DH
            out_ref[target, :, start : start + DH] = y
            out_ref[target, :, start + DH : start + 2 * DH] = v_ref[
                video, :, head * DH : (head + 1) * DH
            ]


def softmax_parts(scores):
    top = jnp.max(scores, axis=-1, keepdims=True)
    weights = jnp.exp(scores - top)
    total = jnp.sum(weights, axis=-1, keepdims=True)
    return weights.astype(BF16), 1.0 / total, top + jnp.log(total)


def stacked(refs, lanes):
    rows = [ref[:, lanes].astype(F32) for ref in refs]
    return jnp.concatenate(rows, axis=0).astype(BF16)


def fresh_kernel(groups, videos, *refs):
    queries, fresh_ref, out_ref, log_ref = refs[:videos], refs[videos], refs[videos + 1], refs[videos + 2]
    own = lax.axis_index("patch") // groups
    _, tok_rows, width = out_ref.shape
    span = width // groups
    pairs = span // DH
    rows = videos * tok_rows
    scale = 1.0 / math.sqrt(DH)
    shape = (pairs * rows, rows)
    same = lax.broadcasted_iota(jnp.int32, shape, 0) % rows // tok_rows == (
        lax.broadcasted_iota(jnp.int32, shape, 1) // tok_rows
    )
    lane = lax.broadcasted_iota(jnp.int32, (rows, DH), 1)
    logs = jnp.zeros((rows, DH), F32)
    for group in range(groups):
        query = stacked(queries, slice(group * span, (group + 1) * span))
        fresh = jnp.concatenate(
            [fresh_ref[(own ^ s) * groups + group].astype(F32) for s in range(videos)], axis=0
        ).astype(BF16)
        scores = jnp.concatenate(
            [
                lax.dot_general(
                    query[:, pair * DH : (pair + 1) * DH],
                    fresh[:, 2 * pair * DH : (2 * pair + 1) * DH],
                    TRANSPOSED,
                    preferred_element_type=F32,
                )
                for pair in range(pairs)
            ],
            axis=0,
        )
        weights, inverse, log = softmax_parts(jnp.where(same, scores * scale, -jnp.inf))
        for pair in range(pairs):
            here = slice(pair * rows, (pair + 1) * rows)
            head = group * pairs + pair
            result = inverse[here] * jnp.dot(
                weights[here],
                fresh[:, (2 * pair + 1) * DH : (2 * pair + 2) * DH],
                preferred_element_type=F32,
            )
            logs = jnp.where(lane == head, log[here], logs)
            for s in range(videos):
                out_ref[s, :, head * DH : (head + 1) * DH] = result[s * tok_rows : (s + 1) * tok_rows]
    for s in range(videos):
        log_ref[s] = logs[s * tok_rows : (s + 1) * tok_rows]


def stale_kernel(groups, videos, *refs):
    queries, pieces, outs = refs[:videos], refs[videos : videos + groups], refs[videos + groups :]
    me = lax.axis_index("patch")
    mine = me % groups
    pairs, total_rows, _ = pieces[0].shape
    tok_rows, width = queries[0].shape
    span = pairs * DH
    rows = videos * tok_rows
    scale = 1.0 / math.sqrt(DH)
    shape = (pairs * rows, total_rows)
    patch = (lax.broadcasted_iota(jnp.int32, shape, 0) % rows // tok_rows * groups) ^ me
    own = patch == lax.broadcasted_iota(jnp.int32, shape, 1) // tok_rows
    lane = lax.broadcasted_iota(jnp.int32, (rows, DH), 1)
    logs = jnp.zeros((rows, DH), F32)
    for t in range(groups):
        start = pl.multiple_of((mine ^ t) * span, DH)
        query = stacked(queries, pl.ds(start, span))
        scores = jnp.concatenate(
            [
                lax.dot_general(
                    query[:, pair * DH : (pair + 1) * DH],
                    pieces[t][pair, :, :DH],
                    TRANSPOSED,
                    preferred_element_type=F32,
                )
                for pair in range(pairs)
            ],
            axis=0,
        )
        weights, inverse, log = softmax_parts(jnp.where(own, -jnp.inf, scores * scale))
        results = []
        for pair in range(pairs):
            here = slice(pair * rows, (pair + 1) * rows)
            results.append(
                inverse[here]
                * jnp.dot(weights[here], pieces[t][pair, :, DH:], preferred_element_type=F32)
            )
            logs = jnp.where(lane == t * pairs + pair, log[here], logs)
        result = jnp.concatenate(results, axis=1).astype(BF16)
        for s in range(videos):
            outs[s][:, pl.ds(start, span)] = result[s * tok_rows : (s + 1) * tok_rows]
    high = logs.astype(BF16).astype(F32)
    middle = (logs - high).astype(BF16).astype(F32)
    low = (logs - high - middle).astype(BF16).astype(F32)
    heads = groups * pairs
    terms = (high + pltpu.roll(middle, heads, 1) + pltpu.roll(low, 2 * heads, 1)).astype(BF16)
    for s in range(videos):
        outs[s][:, width:] = terms[s * tok_rows : (s + 1) * tok_rows]


def join_kernel(groups, videos, *refs):
    back = refs[:videos]
    fresh_ref, log_ref, out_ref, done_ref, sems = refs[videos:]
    me = lax.axis_index("patch")
    own, mine = me // groups, me % groups
    _, tok_rows, width = fresh_ref.shape
    heads = width // DH
    pairs = heads // groups
    copies = []
    for s in range(videos):
        terms = back[s][:, width:].astype(F32)
        stale_log = terms + pltpu.roll(terms, DH - heads, 1) + pltpu.roll(terms, DH - 2 * heads, 1)
        fresh_log = log_ref[s]
        for t in range(groups):
            start = pl.multiple_of((mine ^ t) * pairs * DH, DH)
            stale = back[s][:, pl.ds(start, pairs * DH)].astype(F32)
            fresh = fresh_ref[s, :, pl.ds(start, pairs * DH)]
            shift = DH + t * pairs - (mine ^ t) * pairs
            gap = stale_log - pltpu.roll(fresh_log, shift % DH, 1)
            share = 1.0 / (1.0 + jnp.exp(gap))
            parts = []
            for pair in range(pairs):
                here = slice(pair * DH, (pair + 1) * DH)
                of = share[:, t * pairs + pair : t * pairs + pair + 1]
                parts.append(of * fresh[:, here] + (1.0 - of) * stale[:, here])
            done_ref[s, :, pl.ds(start, pairs * DH)] = jnp.concatenate(parts, axis=1).astype(BF16)
        copies.append(pltpu.make_async_copy(done_ref.at[s], out_ref.at[own ^ s], sems.at[s]))
        copies[-1].start()
    for copy in copies:
        copy.wait()


def cache_kernel(got_ref, out_ref, sems):
    copies = []
    for pair in range(out_ref.shape[0]):
        lanes = pl.ds(2 * pair * DH, 2 * DH)
        copies.append(
            pltpu.make_async_copy(got_ref.at[:, :, lanes], out_ref.at[pair], sems.at[pair])
        )
        copies[-1].start()
    for copy in copies:
        copy.wait()


def permuted(array, offset, patches):
    return lax.ppermute(array, "patch", [(i, i ^ offset) for i in range(patches)])


def exchange(arrays, stride, patches):
    return [arrays[0]] + [
        permuted(arrays[s], s * stride, patches) for s in range(1, len(arrays))
    ]


def local(queries, keys, values, q_gain, k_gain, stale_cache, coords):
    videos, tok_rows, width = queries.shape
    pairs_here, total_rows, _ = stale_cache.shape
    patches = total_rows // tok_rows
    groups = patches // videos
    rows = jax.ShapeDtypeStruct((tok_rows, width), BF16)

    def kernel(body, name, limit, cost=0, **kwargs):
        return pl.pallas_call(
            body,
            name=name,
            compiler_params=pltpu.CompilerParams(vmem_limit_bytes=limit * MIB),
            cost_estimate=pl.CostEstimate(flops=0, bytes_accessed=cost, transcendentals=0),
            **kwargs,
        )

    pieces = {0: stale_cache}
    bit = groups // 2
    pieces[bit] = permuted(stale_cache, bit, patches)
    *query, tables = kernel(
        functools.partial(query_kernel, groups),
        "query",
        56,
        out_shape=[rows] * videos + [jax.ShapeDtypeStruct((3, tok_rows, DH), F32)],
        in_specs=[HBM] * 3,
        out_specs=[HBM] * videos + [VMEM],
        scratch_shapes=[
            pltpu.VMEM(queries.shape, BF16),
            pltpu.VMEM((1, width), F32),
            pltpu.SMEM(coords.shape, jnp.int32),
            pltpu.VMEM(queries.shape, BF16),
            pltpu.SemaphoreType.DMA((3,)),
            pltpu.SemaphoreType.DMA((videos,)),
        ],
    )(queries, q_gain.reshape(1, width), coords)
    query_got = exchange(query, groups, patches)
    fresh = kernel(
        key_kernel,
        "key",
        16,
        out_shape=jax.ShapeDtypeStruct((patches, tok_rows, 2 * pairs_here * DH), BF16),
        in_specs=[VMEM] * 4,
        out_specs=VMEM,
    )(keys, values, k_gain.reshape(1, width), tables)
    cached = lax.all_to_all(fresh, "patch", split_axis=0, concat_axis=0, tiled=True)
    fresh_sum, fresh_log = kernel(
        functools.partial(fresh_kernel, groups, videos),
        "fresh",
        16,
        out_shape=(
            jax.ShapeDtypeStruct((videos, tok_rows, width), F32),
            jax.ShapeDtypeStruct((videos, tok_rows, DH), F32),
        ),
        in_specs=[VMEM] * (videos + 1),
        out_specs=(VMEM, VMEM),
    )(*query, fresh)
    pieces, query_got, fresh_log = lax.optimization_barrier((pieces, query_got, fresh_log))
    while bit > 1:
        bit //= 2
        pieces.update({t | bit: permuted(piece, bit, patches) for t, piece in list(pieces.items())})
    result = kernel(
        functools.partial(stale_kernel, groups, videos),
        "stale",
        32,
        out_shape=[jax.ShapeDtypeStruct((tok_rows, width + DH), BF16)] * videos,
        in_specs=[VMEM] * (videos + groups),
        out_specs=[VMEM] * videos,
    )(*query_got, *[pieces[t] for t in range(groups)])
    back = exchange(result, groups, patches)
    next_cache = kernel(
        cache_kernel,
        "cache",
        16,
        out_shape=jax.ShapeDtypeStruct((pairs_here, patches, tok_rows, 2 * DH), BF16),
        in_specs=[VMEM],
        out_specs=HBM,
        scratch_shapes=[pltpu.SemaphoreType.DMA((pairs_here,))],
    )(cached)
    attended = kernel(
        functools.partial(join_kernel, groups, videos),
        "join",
        16,
        out_shape=jax.ShapeDtypeStruct(queries.shape, BF16),
        in_specs=[VMEM] * (videos + 2),
        out_specs=HBM,
        scratch_shapes=[
            pltpu.VMEM(queries.shape, BF16),
            pltpu.SemaphoreType.DMA((videos,)),
        ],
    )(*back, fresh_sum, fresh_log)
    return (attended, next_cache.reshape(stale_cache.shape))


def solution(mesh):
    in_specs = (
        P("req", "patch", None),
        P("req", "patch", None),
        P("req", "patch", None),
        P(),
        P(),
        P(("req", "patch"), None, None),
        P(None, "patch"),
    )
    out_specs = (P("req", "patch", None), P(("req", "patch"), None, None))
    return jax.shard_map(local, mesh=mesh, in_specs=in_specs, out_specs=out_specs, check_vma=False)
```

```python
import functools
import math

import jax
import jax.numpy as jnp
from jax import lax
from jax.experimental import pallas as pl
from jax.experimental.pallas import tpu as pltpu
from jax.sharding import PartitionSpec as P

DH = 128
VMEM = pl.BlockSpec(memory_space=pltpu.VMEM)
HBM = pl.BlockSpec(memory_space=pltpu.HBM)
SMEM = pl.BlockSpec(memory_space=pltpu.SMEM)
MIB = 1024 * 1024
BF16 = jnp.bfloat16
F32 = jnp.float32
TRANSPOSED = (((1,), (1,)), ((), ()))


def rope_tables(coords_ref, tok_rows):
    half = DH // 2
    side = DH // 6
    first = half - 2 * side
    shape = (tok_rows, DH)
    row = lax.broadcasted_iota(jnp.int32, shape, 0)
    lane = lax.broadcasted_iota(jnp.int32, shape, 1)
    pair = lane // 2
    axis = (pair >= first).astype(jnp.int32) + (pair >= first + side).astype(jnp.int32)
    place = jnp.zeros(shape, jnp.int32)
    for which in range(3):
        for token in range(tok_rows):
            place = jnp.where((axis == which) & (row == token), coords_ref[which, token], place)
    step = jnp.where(axis == 0, pair, jnp.where(axis == 1, pair - first, pair - first - side))
    count = jnp.where(axis == 0, float(first), float(side))
    freq = jnp.exp(step.astype(F32) / count * (-math.log(10000.0)))
    angle = place.astype(F32) * freq
    sine = jnp.sin(angle)
    even = lane % 2 == 0
    return jnp.cos(angle), jnp.where(even, -sine, 0.0), jnp.where(even, 0.0, sine)


def normed_heads(wide, gain_ref, tables):
    cosine, sine_even, sine_odd = tables
    width = wide.shape[-1]
    meansq = jnp.sum(wide * wide, axis=-1, keepdims=True) * (1.0 / width)
    inverse = lax.rsqrt(meansq + 1e-06)
    for head in range(width // DH):
        here = slice(head * DH, (head + 1) * DH)
        y = wide[:, here] * inverse * gain_ref[:, here]
        y = y * cosine + pltpu.roll(y, DH - 1, 1) * sine_even + pltpu.roll(y, 1, 1) * sine_odd
        yield head, y.astype(BF16)


def query_kernel(groups, q_hbm, gain_hbm, coords_hbm, *refs):
    videos, tok_rows, width = q_hbm.shape
    outs, tables_ref, refs = refs[:videos], refs[videos], refs[videos + 1 :]
    q_ref, gain_ref, coords_ref, done_ref, sems, out_sems = refs
    own = lax.axis_index("patch") // groups
    copies = [
        pltpu.make_async_copy(source, place, sems.at[i])
        for i, (source, place) in enumerate(
            ((coords_hbm, coords_ref), (q_hbm, q_ref), (gain_hbm, gain_ref))
        )
    ]
    for copy in copies:
        copy.start()
    copies[0].wait()
    tables = rope_tables(coords_ref, tok_rows)
    for i in range(3):
        tables_ref[i] = tables[i]
    copies[1].wait()
    copies[2].wait()
    sends = []
    for s in range(videos):
        for head, y in normed_heads(q_ref[own ^ s].astype(F32), gain_ref, tables):
            done_ref[s, :, head * DH : (head + 1) * DH] = y
        sends.append(pltpu.make_async_copy(done_ref.at[s], outs[s], out_sems.at[s]))
        sends[-1].start()
    for send in sends:
        send.wait()


def key_kernel(k_ref, v_ref, gain_ref, tables_ref, out_ref):
    videos, tok_rows, width = k_ref.shape
    tables = [tables_ref[i] for i in range(3)]
    span = out_ref.shape[2]
    groups = out_ref.shape[0] // videos
    pairs = span // (2 * DH)
    for video in range(videos):
        for head, y in normed_heads(k_ref[video].astype(F32), gain_ref, tables):
            target, start = video * groups + head // pairs, head % pairs * 2 * DH
            out_ref[target, :, start : start + DH] = y
            out_ref[target, :, start + DH : start + 2 * DH] = v_ref[
                video, :, head * DH : (head + 1) * DH
            ]


def softmax_parts(scores):
    top = jnp.max(scores, axis=-1, keepdims=True)
    weights = jnp.exp(scores - top)
    total = jnp.sum(weights, axis=-1, keepdims=True)
    return weights.astype(BF16), 1.0 / total, top + jnp.log(total)


def stacked(refs, lanes):
    rows = [ref[:, lanes].astype(F32) for ref in refs]
    return jnp.concatenate(rows, axis=0).astype(BF16)


def fresh_kernel(groups, videos, *refs):
    queries, fresh_ref, out_ref, log_ref = refs[:videos], refs[videos], refs[videos + 1], refs[videos + 2]
    own = lax.axis_index("patch") // groups
    _, tok_rows, width = out_ref.shape
    span = width // groups
    pairs = span // DH
    rows = videos * tok_rows
    scale = 1.0 / math.sqrt(DH)
    shape = (pairs * rows, rows)
    same = lax.broadcasted_iota(jnp.int32, shape, 0) % rows // tok_rows == (
        lax.broadcasted_iota(jnp.int32, shape, 1) // tok_rows
    )
    lane = lax.broadcasted_iota(jnp.int32, (rows, DH), 1)
    logs = jnp.zeros((rows, DH), F32)
    for group in range(groups):
        query = stacked(queries, slice(group * span, (group + 1) * span))
        fresh = jnp.concatenate(
            [fresh_ref[(own ^ s) * groups + group].astype(F32) for s in range(videos)], axis=0
        ).astype(BF16)
        scores = jnp.concatenate(
            [
                lax.dot_general(
                    query[:, pair * DH : (pair + 1) * DH],
                    fresh[:, 2 * pair * DH : (2 * pair + 1) * DH],
                    TRANSPOSED,
                    preferred_element_type=F32,
                )
                for pair in range(pairs)
            ],
            axis=0,
        )
        weights, inverse, log = softmax_parts(jnp.where(same, scores * scale, -jnp.inf))
        for pair in range(pairs):
            here = slice(pair * rows, (pair + 1) * rows)
            head = group * pairs + pair
            result = inverse[here] * jnp.dot(
                weights[here],
                fresh[:, (2 * pair + 1) * DH : (2 * pair + 2) * DH],
                preferred_element_type=F32,
            )
            logs = jnp.where(lane == head, log[here], logs)
            for s in range(videos):
                out_ref[s, :, head * DH : (head + 1) * DH] = result[s * tok_rows : (s + 1) * tok_rows]
    for s in range(videos):
        log_ref[s] = logs[s * tok_rows : (s + 1) * tok_rows]


def stale_kernel(groups, videos, *refs):
    queries, pieces, outs = refs[:videos], refs[videos : videos + groups], refs[videos + groups :]
    me = lax.axis_index("patch")
    mine = me % groups
    pairs, total_rows, _ = pieces[0].shape
    tok_rows, width = queries[0].shape
    span = pairs * DH
    rows = videos * tok_rows
    scale = 1.0 / math.sqrt(DH)
    shape = (pairs * rows, total_rows)
    patch = (lax.broadcasted_iota(jnp.int32, shape, 0) % rows // tok_rows * groups) ^ me
    own = patch == lax.broadcasted_iota(jnp.int32, shape, 1) // tok_rows
    lane = lax.broadcasted_iota(jnp.int32, (rows, DH), 1)
    logs = jnp.zeros((rows, DH), F32)
    for t in range(groups):
        start = pl.multiple_of((mine ^ t) * span, DH)
        query = stacked(queries, pl.ds(start, span))
        scores = jnp.concatenate(
            [
                lax.dot_general(
                    query[:, pair * DH : (pair + 1) * DH],
                    pieces[t][pair, :, :DH],
                    TRANSPOSED,
                    preferred_element_type=F32,
                )
                for pair in range(pairs)
            ],
            axis=0,
        )
        weights, inverse, log = softmax_parts(jnp.where(own, -jnp.inf, scores * scale))
        results = []
        for pair in range(pairs):
            here = slice(pair * rows, (pair + 1) * rows)
            results.append(
                inverse[here]
                * jnp.dot(weights[here], pieces[t][pair, :, DH:], preferred_element_type=F32)
            )
            logs = jnp.where(lane == t * pairs + pair, log[here], logs)
        result = jnp.concatenate(results, axis=1).astype(BF16)
        for s in range(videos):
            outs[s][:, pl.ds(start, span)] = result[s * tok_rows : (s + 1) * tok_rows]
    high = logs.astype(BF16).astype(F32)
    middle = (logs - high).astype(BF16).astype(F32)
    low = (logs - high - middle).astype(BF16).astype(F32)
    heads = groups * pairs
    terms = (high + pltpu.roll(middle, heads, 1) + pltpu.roll(low, 2 * heads, 1)).astype(BF16)
    for s in range(videos):
        outs[s][:, width:] = terms[s * tok_rows : (s + 1) * tok_rows]


def join_kernel(groups, videos, *refs):
    back = refs[:videos]
    fresh_ref, log_ref, out_ref, done_ref, sems = refs[videos:]
    me = lax.axis_index("patch")
    own, mine = me // groups, me % groups
    _, tok_rows, width = fresh_ref.shape
    heads = width // DH
    pairs = heads // groups
    copies = []
    for s in range(videos):
        terms = back[s][:, width:].astype(F32)
        stale_log = terms + pltpu.roll(terms, DH - heads, 1) + pltpu.roll(terms, DH - 2 * heads, 1)
        fresh_log = log_ref[s]
        for t in range(groups):
            start = pl.multiple_of((mine ^ t) * pairs * DH, DH)
            stale = back[s][:, pl.ds(start, pairs * DH)].astype(F32)
            fresh = fresh_ref[s, :, pl.ds(start, pairs * DH)]
            shift = DH + t * pairs - (mine ^ t) * pairs
            gap = stale_log - pltpu.roll(fresh_log, shift % DH, 1)
            share = 1.0 / (1.0 + jnp.exp(gap))
            parts = []
            for pair in range(pairs):
                here = slice(pair * DH, (pair + 1) * DH)
                of = share[:, t * pairs + pair : t * pairs + pair + 1]
                parts.append(of * fresh[:, here] + (1.0 - of) * stale[:, here])
            done_ref[s, :, pl.ds(start, pairs * DH)] = jnp.concatenate(parts, axis=1).astype(BF16)
        copies.append(pltpu.make_async_copy(done_ref.at[s], out_ref.at[own ^ s], sems.at[s]))
        copies[-1].start()
    for copy in copies:
        copy.wait()


def cache_kernel(got_ref, out_ref, sems):
    copies = []
    for pair in range(out_ref.shape[0]):
        lanes = pl.ds(2 * pair * DH, 2 * DH)
        copies.append(
            pltpu.make_async_copy(got_ref.at[:, :, lanes], out_ref.at[pair], sems.at[pair])
        )
        copies[-1].start()
    for copy in copies:
        copy.wait()


def permuted(array, offset, patches):
    return lax.ppermute(array, "patch", [(i, i ^ offset) for i in range(patches)])


def exchange(arrays, stride, patches):
    return [arrays[0]] + [
        permuted(arrays[s], s * stride, patches) for s in range(1, len(arrays))
    ]


def local(queries, keys, values, q_gain, k_gain, stale_cache, coords):
    videos, tok_rows, width = queries.shape
    pairs_here, total_rows, _ = stale_cache.shape
    patches = total_rows // tok_rows
    groups = patches // videos
    rows = jax.ShapeDtypeStruct((tok_rows, width), BF16)

    def kernel(body, name, limit, cost=0, **kwargs):
        return pl.pallas_call(
            body,
            name=name,
            compiler_params=pltpu.CompilerParams(vmem_limit_bytes=limit * MIB),
            cost_estimate=pl.CostEstimate(flops=0, bytes_accessed=cost, transcendentals=0),
            **kwargs,
        )

    pieces = {0: stale_cache}
    bit = groups // 2
    pieces[bit] = permuted(stale_cache, bit, patches)
    *query, tables = kernel(
        functools.partial(query_kernel, groups),
        "query",
        56,
        out_shape=[rows] * videos + [jax.ShapeDtypeStruct((3, tok_rows, DH), F32)],
        in_specs=[HBM] * 3,
        out_specs=[HBM] * videos + [VMEM],
        scratch_shapes=[
            pltpu.VMEM(queries.shape, BF16),
            pltpu.VMEM((1, width), F32),
            pltpu.SMEM(coords.shape, jnp.int32),
            pltpu.VMEM(queries.shape, BF16),
            pltpu.SemaphoreType.DMA((3,)),
            pltpu.SemaphoreType.DMA((videos,)),
        ],
    )(queries, q_gain.reshape(1, width), coords)
    query_got = exchange(query, groups, patches)
    fresh = kernel(
        key_kernel,
        "key",
        16,
        out_shape=jax.ShapeDtypeStruct((patches, tok_rows, 2 * pairs_here * DH), BF16),
        in_specs=[VMEM] * 4,
        out_specs=VMEM,
    )(keys, values, k_gain.reshape(1, width), tables)
    cached = lax.all_to_all(fresh, "patch", split_axis=0, concat_axis=0, tiled=True)
    fresh_sum, fresh_log = kernel(
        functools.partial(fresh_kernel, groups, videos),
        "fresh",
        16,
        out_shape=(
            jax.ShapeDtypeStruct((videos, tok_rows, width), F32),
            jax.ShapeDtypeStruct((videos, tok_rows, DH), F32),
        ),
        in_specs=[VMEM] * (videos + 1),
        out_specs=(VMEM, VMEM),
    )(*query, fresh)
    pieces, query_got, fresh_log = lax.optimization_barrier((pieces, query_got, fresh_log))
    while bit > 1:
        bit //= 2
        pieces.update({t | bit: permuted(piece, bit, patches) for t, piece in list(pieces.items())})
    result = kernel(
        functools.partial(stale_kernel, groups, videos),
        "stale",
        32,
        cost=36 * MIB,
        out_shape=[jax.ShapeDtypeStruct((tok_rows, width + DH), BF16)] * videos,
        in_specs=[VMEM] * (videos + groups),
        out_specs=[VMEM] * videos,
    )(*query_got, *[pieces[t] for t in range(groups)])
    back = exchange(result, groups, patches)
    next_cache = kernel(
        cache_kernel,
        "cache",
        16,
        out_shape=jax.ShapeDtypeStruct((pairs_here, patches, tok_rows, 2 * DH), BF16),
        in_specs=[VMEM],
        out_specs=HBM,
        scratch_shapes=[pltpu.SemaphoreType.DMA((pairs_here,))],
    )(cached)
    attended = kernel(
        functools.partial(join_kernel, groups, videos),
        "join",
        16,
        out_shape=jax.ShapeDtypeStruct(queries.shape, BF16),
        in_specs=[VMEM] * (videos + 2),
        out_specs=HBM,
        scratch_shapes=[
            pltpu.VMEM(queries.shape, BF16),
            pltpu.SemaphoreType.DMA((videos,)),
        ],
    )(*back, fresh_sum, fresh_log)
    return (attended, next_cache.reshape(stale_cache.shape))


def solution(mesh):
    in_specs = (
        P("req", "patch", None),
        P("req", "patch", None),
        P("req", "patch", None),
        P(),
        P(),
        P(("req", "patch"), None, None),
        P(None, "patch"),
    )
    out_specs = (P("req", "patch", None), P(("req", "patch"), None, None))
    return jax.shard_map(local, mesh=mesh, in_specs=in_specs, out_specs=out_specs, check_vma=False)
```

```python
import functools
import math

import jax
import jax.numpy as jnp
from jax import lax
from jax.experimental import pallas as pl
from jax.experimental.pallas import tpu as pltpu
from jax.sharding import PartitionSpec as P

DH = 128
VMEM = pl.BlockSpec(memory_space=pltpu.VMEM)
HBM = pl.BlockSpec(memory_space=pltpu.HBM)
SMEM = pl.BlockSpec(memory_space=pltpu.SMEM)
MIB = 1024 * 1024
BF16 = jnp.bfloat16
F32 = jnp.float32
TRANSPOSED = (((1,), (1,)), ((), ()))


def rope_tables(coords_ref, tok_rows):
    half = DH // 2
    side = DH // 6
    first = half - 2 * side
    shape = (tok_rows, DH)
    row = lax.broadcasted_iota(jnp.int32, shape, 0)
    lane = lax.broadcasted_iota(jnp.int32, shape, 1)
    pair = lane // 2
    axis = (pair >= first).astype(jnp.int32) + (pair >= first + side).astype(jnp.int32)
    place = jnp.zeros(shape, jnp.int32)
    for which in range(3):
        for token in range(tok_rows):
            place = jnp.where((axis == which) & (row == token), coords_ref[which, token], place)
    step = jnp.where(axis == 0, pair, jnp.where(axis == 1, pair - first, pair - first - side))
    count = jnp.where(axis == 0, float(first), float(side))
    freq = jnp.exp(step.astype(F32) / count * (-math.log(10000.0)))
    angle = place.astype(F32) * freq
    sine = jnp.sin(angle)
    even = lane % 2 == 0
    return jnp.cos(angle), jnp.where(even, -sine, 0.0), jnp.where(even, 0.0, sine)


def normed_heads(wide, gain_ref, tables):
    cosine, sine_even, sine_odd = tables
    width = wide.shape[-1]
    meansq = jnp.sum(wide * wide, axis=-1, keepdims=True) * (1.0 / width)
    inverse = lax.rsqrt(meansq + 1e-06)
    for head in range(width // DH):
        here = slice(head * DH, (head + 1) * DH)
        y = wide[:, here] * inverse * gain_ref[:, here]
        y = y * cosine + pltpu.roll(y, DH - 1, 1) * sine_even + pltpu.roll(y, 1, 1) * sine_odd
        yield head, y.astype(BF16)


def query_kernel(groups, q_hbm, gain_hbm, coords_hbm, *refs):
    videos, tok_rows, width = q_hbm.shape
    outs, tables_ref, refs = refs[:videos], refs[videos], refs[videos + 1 :]
    q_ref, gain_ref, coords_ref, done_ref, sems, out_sems = refs
    own = lax.axis_index("patch") // groups
    copies = [
        pltpu.make_async_copy(source, place, sems.at[i])
        for i, (source, place) in enumerate(
            ((coords_hbm, coords_ref), (q_hbm, q_ref), (gain_hbm, gain_ref))
        )
    ]
    for copy in copies:
        copy.start()
    copies[0].wait()
    tables = rope_tables(coords_ref, tok_rows)
    for i in range(3):
        tables_ref[i] = tables[i]
    copies[1].wait()
    copies[2].wait()
    sends = []
    for s in range(videos):
        for head, y in normed_heads(q_ref[own ^ s].astype(F32), gain_ref, tables):
            done_ref[s, :, head * DH : (head + 1) * DH] = y
        sends.append(pltpu.make_async_copy(done_ref.at[s], outs[s], out_sems.at[s]))
        sends[-1].start()
    for send in sends:
        send.wait()


def key_kernel(k_ref, gain_ref, tables_ref, out_ref):
    videos = k_ref.shape[0]
    tables = [tables_ref[i] for i in range(3)]
    groups = out_ref.shape[0] // videos
    pairs = out_ref.shape[2] // DH
    for video in range(videos):
        for head, y in normed_heads(k_ref[video].astype(F32), gain_ref, tables):
            start = head % pairs * DH
            out_ref[video * groups + head // pairs, :, start : start + DH] = y


def softmax_parts(scores):
    top = jnp.max(scores, axis=-1, keepdims=True)
    weights = jnp.exp(scores - top)
    total = jnp.sum(weights, axis=-1, keepdims=True)
    return weights.astype(BF16), 1.0 / total, top + jnp.log(total)


def stacked(refs, lanes):
    rows = [ref[:, lanes].astype(F32) for ref in refs]
    return jnp.concatenate(rows, axis=0).astype(BF16)


def fresh_kernel(groups, videos, *refs):
    queries = refs[:videos]
    key_ref, value_ref, out_ref, log_ref = refs[videos:]
    own = lax.axis_index("patch") // groups
    _, tok_rows, width = out_ref.shape
    span = width // groups
    pairs = span // DH
    rows = videos * tok_rows
    scale = 1.0 / math.sqrt(DH)
    shape = (pairs * rows, rows)
    same = lax.broadcasted_iota(jnp.int32, shape, 0) % rows // tok_rows == (
        lax.broadcasted_iota(jnp.int32, shape, 1) // tok_rows
    )
    lane = lax.broadcasted_iota(jnp.int32, (rows, DH), 1)
    logs = jnp.zeros((rows, DH), F32)
    for group in range(groups):
        query = stacked(queries, slice(group * span, (group + 1) * span))
        lanes = slice(group * span, (group + 1) * span)
        key = stacked([key_ref.at[(own ^ s) * groups + group] for s in range(videos)], slice(None))
        value = stacked([value_ref.at[own ^ s] for s in range(videos)], lanes)
        scores = jnp.concatenate(
            [
                lax.dot_general(
                    query[:, pair * DH : (pair + 1) * DH],
                    key[:, pair * DH : (pair + 1) * DH],
                    TRANSPOSED,
                    preferred_element_type=F32,
                )
                for pair in range(pairs)
            ],
            axis=0,
        )
        weights, inverse, log = softmax_parts(jnp.where(same, scores * scale, -jnp.inf))
        for pair in range(pairs):
            here = slice(pair * rows, (pair + 1) * rows)
            head = group * pairs + pair
            result = inverse[here] * jnp.dot(
                weights[here],
                value[:, pair * DH : (pair + 1) * DH],
                preferred_element_type=F32,
            )
            logs = jnp.where(lane == head, log[here], logs)
            for s in range(videos):
                out_ref[s, :, head * DH : (head + 1) * DH] = result[s * tok_rows : (s + 1) * tok_rows]
    for s in range(videos):
        log_ref[s] = logs[s * tok_rows : (s + 1) * tok_rows]


def stale_kernel(groups, videos, *refs):
    queries, pieces, outs = refs[:videos], refs[videos : videos + groups], refs[videos + groups :]
    me = lax.axis_index("patch")
    mine = me % groups
    pairs, total_rows, _ = pieces[0].shape
    tok_rows, width = queries[0].shape
    span = pairs * DH
    rows = videos * tok_rows
    scale = 1.0 / math.sqrt(DH)
    shape = (pairs * rows, total_rows)
    patch = (lax.broadcasted_iota(jnp.int32, shape, 0) % rows // tok_rows * groups) ^ me
    own = patch == lax.broadcasted_iota(jnp.int32, shape, 1) // tok_rows
    lane = lax.broadcasted_iota(jnp.int32, (rows, DH), 1)
    logs = jnp.zeros((rows, DH), F32)
    for t in range(groups):
        start = pl.multiple_of((mine ^ t) * span, DH)
        query = stacked(queries, pl.ds(start, span))
        scores = jnp.concatenate(
            [
                lax.dot_general(
                    query[:, pair * DH : (pair + 1) * DH],
                    pieces[t][pair, :, :DH],
                    TRANSPOSED,
                    preferred_element_type=F32,
                )
                for pair in range(pairs)
            ],
            axis=0,
        )
        weights, inverse, log = softmax_parts(jnp.where(own, -jnp.inf, scores * scale))
        results = []
        for pair in range(pairs):
            here = slice(pair * rows, (pair + 1) * rows)
            results.append(
                inverse[here]
                * jnp.dot(weights[here], pieces[t][pair, :, DH:], preferred_element_type=F32)
            )
            logs = jnp.where(lane == t * pairs + pair, log[here], logs)
        result = jnp.concatenate(results, axis=1).astype(BF16)
        for s in range(videos):
            outs[s][:, pl.ds(start, span)] = result[s * tok_rows : (s + 1) * tok_rows]
    high = logs.astype(BF16).astype(F32)
    middle = (logs - high).astype(BF16).astype(F32)
    low = (logs - high - middle).astype(BF16).astype(F32)
    heads = groups * pairs
    terms = (high + pltpu.roll(middle, heads, 1) + pltpu.roll(low, 2 * heads, 1)).astype(BF16)
    for s in range(videos):
        outs[s][:, width:] = terms[s * tok_rows : (s + 1) * tok_rows]


def join_kernel(groups, videos, *refs):
    back = refs[:videos]
    fresh_ref, log_ref, out_ref, done_ref, sems = refs[videos:]
    me = lax.axis_index("patch")
    own, mine = me // groups, me % groups
    _, tok_rows, width = fresh_ref.shape
    heads = width // DH
    pairs = heads // groups
    copies = []
    for s in range(videos):
        terms = back[s][:, width:].astype(F32)
        stale_log = terms + pltpu.roll(terms, DH - heads, 1) + pltpu.roll(terms, DH - 2 * heads, 1)
        fresh_log = log_ref[s]
        for t in range(groups):
            start = pl.multiple_of((mine ^ t) * pairs * DH, DH)
            stale = back[s][:, pl.ds(start, pairs * DH)].astype(F32)
            fresh = fresh_ref[s, :, pl.ds(start, pairs * DH)]
            shift = DH + t * pairs - (mine ^ t) * pairs
            gap = stale_log - pltpu.roll(fresh_log, shift % DH, 1)
            share = 1.0 / (1.0 + jnp.exp(gap))
            parts = []
            for pair in range(pairs):
                here = slice(pair * DH, (pair + 1) * DH)
                of = share[:, t * pairs + pair : t * pairs + pair + 1]
                parts.append(of * fresh[:, here] + (1.0 - of) * stale[:, here])
            done_ref[s, :, pl.ds(start, pairs * DH)] = jnp.concatenate(parts, axis=1).astype(BF16)
        copies.append(pltpu.make_async_copy(done_ref.at[s], out_ref.at[own ^ s], sems.at[s]))
        copies[-1].start()
    for copy in copies:
        copy.wait()


def cache_kernel(key_ref, value_ref, out_ref, sems):
    copies = []
    for pair in range(out_ref.shape[0]):
        for part, ref in enumerate((key_ref, value_ref)):
            copies.append(
                pltpu.make_async_copy(
                    ref.at[:, :, pl.ds(pair * DH, DH)],
                    out_ref.at[pair, :, :, pl.ds(part * DH, DH)],
                    sems.at[part, pair],
                )
            )
            copies[-1].start()
    for copy in copies:
        copy.wait()


def permuted(array, offset, patches):
    return lax.ppermute(array, "patch", [(i, i ^ offset) for i in range(patches)])


def exchange(arrays, stride, patches):
    return [arrays[0]] + [
        permuted(arrays[s], s * stride, patches) for s in range(1, len(arrays))
    ]


def local(queries, keys, values, q_gain, k_gain, stale_cache, coords):
    videos, tok_rows, width = queries.shape
    pairs_here, total_rows, _ = stale_cache.shape
    patches = total_rows // tok_rows
    groups = patches // videos
    rows = jax.ShapeDtypeStruct((tok_rows, width), BF16)

    def kernel(body, name, limit, cost=0, **kwargs):
        return pl.pallas_call(
            body,
            name=name,
            compiler_params=pltpu.CompilerParams(vmem_limit_bytes=limit * MIB),
            cost_estimate=pl.CostEstimate(flops=0, bytes_accessed=cost, transcendentals=0),
            **kwargs,
        )

    value_sent = jnp.transpose(
        values.reshape(videos, tok_rows, groups, pairs_here * DH), (0, 2, 1, 3)
    ).reshape(patches, tok_rows, pairs_here * DH)
    value_got = lax.all_to_all(value_sent, "patch", split_axis=0, concat_axis=0, tiled=True)
    pieces = {0: stale_cache}
    bit = groups // 2
    pieces[bit] = permuted(stale_cache, bit, patches)
    *query, tables = kernel(
        functools.partial(query_kernel, groups),
        "query",
        56,
        out_shape=[rows] * videos + [jax.ShapeDtypeStruct((3, tok_rows, DH), F32)],
        in_specs=[HBM] * 3,
        out_specs=[HBM] * videos + [VMEM],
        scratch_shapes=[
            pltpu.VMEM(queries.shape, BF16),
            pltpu.VMEM((1, width), F32),
            pltpu.SMEM(coords.shape, jnp.int32),
            pltpu.VMEM(queries.shape, BF16),
            pltpu.SemaphoreType.DMA((3,)),
            pltpu.SemaphoreType.DMA((videos,)),
        ],
    )(queries, q_gain.reshape(1, width), coords)
    query_got = exchange(query, groups, patches)
    key = kernel(
        key_kernel,
        "key",
        16,
        out_shape=jax.ShapeDtypeStruct((patches, tok_rows, pairs_here * DH), BF16),
        in_specs=[VMEM] * 3,
        out_specs=VMEM,
    )(keys, k_gain.reshape(1, width), tables)
    key_sent, query_got = lax.optimization_barrier((key, query_got))
    key_got = lax.all_to_all(key_sent, "patch", split_axis=0, concat_axis=0, tiled=True)
    fresh_sum, fresh_log = kernel(
        functools.partial(fresh_kernel, groups, videos),
        "fresh",
        16,
        out_shape=(
            jax.ShapeDtypeStruct((videos, tok_rows, width), F32),
            jax.ShapeDtypeStruct((videos, tok_rows, DH), F32),
        ),
        in_specs=[VMEM] * (videos + 2),
        out_specs=(VMEM, VMEM),
    )(*query, key, values)
    pieces, query_got, fresh_log = lax.optimization_barrier((pieces, query_got, fresh_log))
    while bit > 1:
        bit //= 2
        pieces.update({t | bit: permuted(piece, bit, patches) for t, piece in list(pieces.items())})
    result = kernel(
        functools.partial(stale_kernel, groups, videos),
        "stale",
        32,
        out_shape=[jax.ShapeDtypeStruct((tok_rows, width + DH), BF16)] * videos,
        in_specs=[VMEM] * (videos + groups),
        out_specs=[VMEM] * videos,
    )(*query_got, *[pieces[t] for t in range(groups)])
    back = exchange(result, groups, patches)
    next_cache = kernel(
        cache_kernel,
        "cache",
        16,
        out_shape=jax.ShapeDtypeStruct((pairs_here, patches, tok_rows, 2 * DH), BF16),
        in_specs=[VMEM, VMEM],
        out_specs=HBM,
        scratch_shapes=[pltpu.SemaphoreType.DMA((2, pairs_here))],
    )(key_got, value_got)
    attended = kernel(
        functools.partial(join_kernel, groups, videos),
        "join",
        16,
        out_shape=jax.ShapeDtypeStruct(queries.shape, BF16),
        in_specs=[VMEM] * (videos + 2),
        out_specs=HBM,
        scratch_shapes=[
            pltpu.VMEM(queries.shape, BF16),
            pltpu.SemaphoreType.DMA((videos,)),
        ],
    )(*back, fresh_sum, fresh_log)
    return (attended, next_cache.reshape(stale_cache.shape))


def solution(mesh):
    in_specs = (
        P("req", "patch", None),
        P("req", "patch", None),
        P("req", "patch", None),
        P(),
        P(),
        P(("req", "patch"), None, None),
        P(None, "patch"),
    )
    out_specs = (P("req", "patch", None), P(("req", "patch"), None, None))
    return jax.shard_map(local, mesh=mesh, in_specs=in_specs, out_specs=out_specs, check_vma=False)
```

```python
import functools
import math

import jax
import jax.numpy as jnp
from jax import lax
from jax.experimental import pallas as pl
from jax.experimental.pallas import tpu as pltpu
from jax.sharding import PartitionSpec as P

DH = 128
VMEM = pl.BlockSpec(memory_space=pltpu.VMEM)
HBM = pl.BlockSpec(memory_space=pltpu.HBM)
SMEM = pl.BlockSpec(memory_space=pltpu.SMEM)
MIB = 1024 * 1024
BF16 = jnp.bfloat16
F32 = jnp.float32
TRANSPOSED = (((1,), (1,)), ((), ()))


def rope_tables(coords_ref, tok_rows):
    half = DH // 2
    side = DH // 6
    first = half - 2 * side
    shape = (tok_rows, DH)
    row = lax.broadcasted_iota(jnp.int32, shape, 0)
    lane = lax.broadcasted_iota(jnp.int32, shape, 1)
    pair = lane // 2
    axis = (pair >= first).astype(jnp.int32) + (pair >= first + side).astype(jnp.int32)
    place = jnp.zeros(shape, jnp.int32)
    for which in range(3):
        for token in range(tok_rows):
            place = jnp.where((axis == which) & (row == token), coords_ref[which, token], place)
    step = jnp.where(axis == 0, pair, jnp.where(axis == 1, pair - first, pair - first - side))
    count = jnp.where(axis == 0, float(first), float(side))
    freq = jnp.exp(step.astype(F32) / count * (-math.log(10000.0)))
    angle = place.astype(F32) * freq
    sine = jnp.sin(angle)
    even = lane % 2 == 0
    return jnp.cos(angle), jnp.where(even, -sine, 0.0), jnp.where(even, 0.0, sine)


def normed_heads(wide, gain_ref, tables):
    cosine, sine_even, sine_odd = tables
    width = wide.shape[-1]
    meansq = jnp.sum(wide * wide, axis=-1, keepdims=True) * (1.0 / width)
    inverse = lax.rsqrt(meansq + 1e-06)
    for head in range(width // DH):
        here = slice(head * DH, (head + 1) * DH)
        y = wide[:, here] * inverse * gain_ref[:, here]
        y = y * cosine + pltpu.roll(y, DH - 1, 1) * sine_even + pltpu.roll(y, 1, 1) * sine_odd
        yield head, y.astype(BF16)


def query_kernel(groups, q_hbm, gain_hbm, coords_hbm, value_hbm, *refs):
    videos, tok_rows, width = q_hbm.shape
    outs, tables_ref, value_out, refs = refs[:videos], refs[videos], refs[videos + 1], refs[videos + 2 :]
    q_ref, gain_ref, coords_ref, done_ref, sems, out_sems, value_sems = refs
    own = lax.axis_index("patch") // groups
    copies = [
        pltpu.make_async_copy(source, place, sems.at[i])
        for i, (source, place) in enumerate(
            ((coords_hbm, coords_ref), (q_hbm, q_ref), (gain_hbm, gain_ref))
        )
    ]
    for copy in copies:
        copy.start()
    span = width // groups
    spreads = [
        pltpu.make_async_copy(
            value_hbm.at[:, :, pl.ds(group * span, span)], value_out.at[:, group], value_sems.at[group]
        )
        for group in range(groups)
    ]
    for spread in spreads:
        spread.start()
    copies[0].wait()
    tables = rope_tables(coords_ref, tok_rows)
    for i in range(3):
        tables_ref[i] = tables[i]
    copies[1].wait()
    copies[2].wait()
    sends = []
    for s in range(videos):
        for head, y in normed_heads(q_ref[own ^ s].astype(F32), gain_ref, tables):
            done_ref[s, :, head * DH : (head + 1) * DH] = y
        sends.append(pltpu.make_async_copy(done_ref.at[s], outs[s], out_sems.at[s]))
        sends[-1].start()
    for copy in sends + spreads:
        copy.wait()


def key_kernel(k_ref, gain_ref, tables_ref, out_ref):
    videos = k_ref.shape[0]
    tables = [tables_ref[i] for i in range(3)]
    groups = out_ref.shape[0] // videos
    pairs = out_ref.shape[2] // DH
    for video in range(videos):
        for head, y in normed_heads(k_ref[video].astype(F32), gain_ref, tables):
            start = head % pairs * DH
            out_ref[video * groups + head // pairs, :, start : start + DH] = y


def softmax_parts(scores):
    top = jnp.max(scores, axis=-1, keepdims=True)
    weights = jnp.exp(scores - top)
    total = jnp.sum(weights, axis=-1, keepdims=True)
    return weights.astype(BF16), 1.0 / total, top + jnp.log(total)


def stacked(refs, lanes):
    rows = [ref[:, lanes].astype(F32) for ref in refs]
    return jnp.concatenate(rows, axis=0).astype(BF16)


def fresh_kernel(groups, videos, *refs):
    queries = refs[:videos]
    key_ref, value_ref, out_ref, log_ref = refs[videos:]
    me = lax.axis_index("patch")
    own, mine = me // groups, me % groups
    _, tok_rows, width = out_ref.shape
    span = width // groups
    pairs = span // DH
    rows = videos * tok_rows
    scale = 1.0 / math.sqrt(DH)
    shape = (pairs * rows, rows)
    same = lax.broadcasted_iota(jnp.int32, shape, 0) % rows // tok_rows == (
        lax.broadcasted_iota(jnp.int32, shape, 1) // tok_rows
    )
    lane = lax.broadcasted_iota(jnp.int32, (rows, DH), 1)
    logs = jnp.zeros((rows, DH), F32)
    for t in range(groups):
        lanes = pl.ds(pl.multiple_of((mine ^ t) * span, DH), span)
        query = stacked(queries, lanes)
        key = stacked([key_ref.at[me ^ (s * groups) ^ t] for s in range(videos)], slice(None))
        value = stacked([value_ref.at[own ^ s] for s in range(videos)], lanes)
        scores = jnp.concatenate(
            [
                lax.dot_general(
                    query[:, pair * DH : (pair + 1) * DH],
                    key[:, pair * DH : (pair + 1) * DH],
                    TRANSPOSED,
                    preferred_element_type=F32,
                )
                for pair in range(pairs)
            ],
            axis=0,
        )
        weights, inverse, log = softmax_parts(jnp.where(same, scores * scale, -jnp.inf))
        for pair in range(pairs):
            here = slice(pair * rows, (pair + 1) * rows)
            head = t * pairs + pair
            result = inverse[here] * jnp.dot(
                weights[here],
                value[:, pair * DH : (pair + 1) * DH],
                preferred_element_type=F32,
            )
            logs = jnp.where(lane == head, log[here], logs)
            for s in range(videos):
                out_ref[s, :, head * DH : (head + 1) * DH] = result[s * tok_rows : (s + 1) * tok_rows]
    for s in range(videos):
        log_ref[s] = logs[s * tok_rows : (s + 1) * tok_rows]


def stale_kernel(groups, videos, *refs):
    queries, pieces, outs = refs[:videos], refs[videos : videos + groups], refs[videos + groups :]
    me = lax.axis_index("patch")
    mine = me % groups
    pairs, total_rows, _ = pieces[0].shape
    tok_rows, width = queries[0].shape
    span = pairs * DH
    rows = videos * tok_rows
    scale = 1.0 / math.sqrt(DH)
    shape = (pairs * rows, total_rows)
    patch = (lax.broadcasted_iota(jnp.int32, shape, 0) % rows // tok_rows * groups) ^ me
    own = patch == lax.broadcasted_iota(jnp.int32, shape, 1) // tok_rows
    lane = lax.broadcasted_iota(jnp.int32, (rows, DH), 1)
    logs = jnp.zeros((rows, DH), F32)
    for t in range(groups):
        start = pl.multiple_of((mine ^ t) * span, DH)
        query = stacked(queries, pl.ds(start, span))
        scores = jnp.concatenate(
            [
                lax.dot_general(
                    query[:, pair * DH : (pair + 1) * DH],
                    pieces[t][pair, :, :DH],
                    TRANSPOSED,
                    preferred_element_type=F32,
                )
                for pair in range(pairs)
            ],
            axis=0,
        )
        weights, inverse, log = softmax_parts(jnp.where(own, -jnp.inf, scores * scale))
        results = []
        for pair in range(pairs):
            here = slice(pair * rows, (pair + 1) * rows)
            results.append(
                inverse[here]
                * jnp.dot(weights[here], pieces[t][pair, :, DH:], preferred_element_type=F32)
            )
            logs = jnp.where(lane == t * pairs + pair, log[here], logs)
        result = jnp.concatenate(results, axis=1).astype(BF16)
        for s in range(videos):
            outs[s][:, t * span : (t + 1) * span] = result[s * tok_rows : (s + 1) * tok_rows]
    high = logs.astype(BF16).astype(F32)
    middle = (logs - high).astype(BF16).astype(F32)
    low = (logs - high - middle).astype(BF16).astype(F32)
    heads = groups * pairs
    terms = (high + pltpu.roll(middle, heads, 1) + pltpu.roll(low, 2 * heads, 1)).astype(BF16)
    for s in range(videos):
        outs[s][:, width:] = terms[s * tok_rows : (s + 1) * tok_rows]


def join_kernel(groups, videos, *refs):
    back = refs[:videos]
    fresh_ref, log_ref, out_ref, done_ref, sems = refs[videos:]
    me = lax.axis_index("patch")
    own, mine = me // groups, me % groups
    _, tok_rows, width = fresh_ref.shape
    heads = width // DH
    pairs = heads // groups
    span = pairs * DH
    copies = []
    for s in range(videos):
        terms = back[s][:, width:].astype(F32)
        stale_log = terms + pltpu.roll(terms, DH - heads, 1) + pltpu.roll(terms, DH - 2 * heads, 1)
        share = 1.0 / (1.0 + jnp.exp(stale_log - log_ref[s]))
        for t in range(groups):
            parts = []
            for pair in range(pairs):
                head = t * pairs + pair
                here = slice(head * DH, (head + 1) * DH)
                stale = back[s][:, here].astype(F32)
                parts.append(stale + share[:, head : head + 1] * (fresh_ref[s, :, here] - stale))
            lanes = pl.ds(pl.multiple_of((mine ^ t) * span, DH), span)
            done_ref[s, :, lanes] = jnp.concatenate(parts, axis=1).astype(BF16)
        copies.append(pltpu.make_async_copy(done_ref.at[s], out_ref.at[own ^ s], sems.at[s]))
        copies[-1].start()
    for copy in copies:
        copy.wait()


def cache_kernel(key_ref, value_ref, out_ref, sems):
    copies = []
    for pair in range(out_ref.shape[0]):
        for part, ref in enumerate((key_ref, value_ref)):
            copies.append(
                pltpu.make_async_copy(
                    ref.at[:, :, pl.ds(pair * DH, DH)],
                    out_ref.at[pair, :, :, pl.ds(part * DH, DH)],
                    sems.at[part, pair],
                )
            )
            copies[-1].start()
    for copy in copies:
        copy.wait()


def permuted(array, offset, patches):
    return lax.ppermute(array, "patch", [(i, i ^ offset) for i in range(patches)])


def exchange(arrays, stride, patches):
    return [arrays[0]] + [
        permuted(arrays[s], s * stride, patches) for s in range(1, len(arrays))
    ]


def local(queries, keys, values, q_gain, k_gain, stale_cache, coords):
    videos, tok_rows, width = queries.shape
    pairs_here, total_rows, _ = stale_cache.shape
    patches = total_rows // tok_rows
    groups = patches // videos
    rows = jax.ShapeDtypeStruct((tok_rows, width), BF16)

    def kernel(body, name, limit, cost=0, **kwargs):
        return pl.pallas_call(
            body,
            name=name,
            compiler_params=pltpu.CompilerParams(vmem_limit_bytes=limit * MIB),
            cost_estimate=pl.CostEstimate(flops=0, bytes_accessed=cost, transcendentals=0),
            **kwargs,
        )

    pieces = {0: stale_cache}
    bit = groups // 2
    pieces[bit] = permuted(stale_cache, bit, patches)
    *query, tables, value_sent = kernel(
        functools.partial(query_kernel, groups),
        "query",
        56,
        out_shape=[rows] * videos
        + [
            jax.ShapeDtypeStruct((3, tok_rows, DH), F32),
            jax.ShapeDtypeStruct((videos, groups, tok_rows, pairs_here * DH), BF16),
        ],
        in_specs=[HBM] * 4,
        out_specs=[HBM] * videos + [VMEM, HBM],
        scratch_shapes=[
            pltpu.VMEM(queries.shape, BF16),
            pltpu.VMEM((1, width), F32),
            pltpu.SMEM(coords.shape, jnp.int32),
            pltpu.VMEM(queries.shape, BF16),
            pltpu.SemaphoreType.DMA((3,)),
            pltpu.SemaphoreType.DMA((videos,)),
            pltpu.SemaphoreType.DMA((groups,)),
        ],
    )(queries, q_gain.reshape(1, width), coords, values)
    value_got = lax.all_to_all(
        value_sent.reshape(patches, tok_rows, pairs_here * DH), "patch", split_axis=0, concat_axis=0, tiled=True
    )
    query_got = exchange(query, groups, patches)
    key = kernel(
        key_kernel,
        "key",
        16,
        out_shape=jax.ShapeDtypeStruct((patches, tok_rows, pairs_here * DH), BF16),
        in_specs=[VMEM] * 3,
        out_specs=VMEM,
    )(keys, k_gain.reshape(1, width), tables)
    key_sent, query_got = lax.optimization_barrier((key, query_got))
    key_got = lax.all_to_all(key_sent, "patch", split_axis=0, concat_axis=0, tiled=True)
    fresh_sum, fresh_log = kernel(
        functools.partial(fresh_kernel, groups, videos),
        "fresh",
        16,
        out_shape=(
            jax.ShapeDtypeStruct((videos, tok_rows, width), F32),
            jax.ShapeDtypeStruct((videos, tok_rows, DH), F32),
        ),
        in_specs=[VMEM] * (videos + 2),
        out_specs=(VMEM, VMEM),
    )(*query, key, values)
    pieces, query_got, fresh_log = lax.optimization_barrier((pieces, query_got, fresh_log))
    while bit > 1:
        bit //= 2
        pieces.update({t | bit: permuted(piece, bit, patches) for t, piece in list(pieces.items())})
    result = kernel(
        functools.partial(stale_kernel, groups, videos),
        "stale",
        32,
        out_shape=[jax.ShapeDtypeStruct((tok_rows, width + DH), BF16)] * videos,
        in_specs=[VMEM] * (videos + groups),
        out_specs=[VMEM] * videos,
    )(*query_got, *[pieces[t] for t in range(groups)])
    back = exchange(result, groups, patches)
    next_cache = kernel(
        cache_kernel,
        "cache",
        16,
        out_shape=jax.ShapeDtypeStruct((pairs_here, patches, tok_rows, 2 * DH), BF16),
        in_specs=[VMEM, VMEM],
        out_specs=HBM,
        scratch_shapes=[pltpu.SemaphoreType.DMA((2, pairs_here))],
    )(key_got, value_got)
    attended = kernel(
        functools.partial(join_kernel, groups, videos),
        "join",
        16,
        out_shape=jax.ShapeDtypeStruct(queries.shape, BF16),
        in_specs=[VMEM] * (videos + 2),
        out_specs=HBM,
        scratch_shapes=[
            pltpu.VMEM(queries.shape, BF16),
            pltpu.SemaphoreType.DMA((videos,)),
        ],
    )(*back, fresh_sum, fresh_log)
    return (attended, next_cache.reshape(stale_cache.shape))


def solution(mesh):
    in_specs = (
        P("req", "patch", None),
        P("req", "patch", None),
        P("req", "patch", None),
        P(),
        P(),
        P(("req", "patch"), None, None),
        P(None, "patch"),
    )
    out_specs = (P("req", "patch", None), P(("req", "patch"), None, None))
    return jax.shard_map(local, mesh=mesh, in_specs=in_specs, out_specs=out_specs, check_vma=False)
```

```python
import functools
import math

import jax
import jax.numpy as jnp
from jax import lax
from jax.experimental import pallas as pl
from jax.experimental.pallas import tpu as pltpu
from jax.sharding import PartitionSpec as P

DH = 128
VMEM = pl.BlockSpec(memory_space=pltpu.VMEM)
HBM = pl.BlockSpec(memory_space=pltpu.HBM)
SMEM = pl.BlockSpec(memory_space=pltpu.SMEM)
MIB = 1024 * 1024
BF16 = jnp.bfloat16
F32 = jnp.float32
TRANSPOSED = (((1,), (1,)), ((), ()))


def rope_tables(coords_ref, tok_rows):
    half = DH // 2
    side = DH // 6
    first = half - 2 * side
    shape = (tok_rows, DH)
    row = lax.broadcasted_iota(jnp.int32, shape, 0)
    lane = lax.broadcasted_iota(jnp.int32, shape, 1)
    pair = lane // 2
    axis = (pair >= first).astype(jnp.int32) + (pair >= first + side).astype(jnp.int32)
    place = jnp.zeros(shape, jnp.int32)
    for which in range(3):
        for token in range(tok_rows):
            place = jnp.where((axis == which) & (row == token), coords_ref[which, token], place)
    step = jnp.where(axis == 0, pair, jnp.where(axis == 1, pair - first, pair - first - side))
    count = jnp.where(axis == 0, float(first), float(side))
    freq = jnp.exp(step.astype(F32) / count * (-math.log(10000.0)))
    angle = place.astype(F32) * freq
    sine = jnp.sin(angle)
    even = lane % 2 == 0
    return jnp.cos(angle), jnp.where(even, -sine, 0.0), jnp.where(even, 0.0, sine)


def normed_heads(wide, gain_ref, tables):
    cosine, sine_even, sine_odd = tables
    width = wide.shape[-1]
    meansq = jnp.sum(wide * wide, axis=-1, keepdims=True) * (1.0 / width)
    inverse = lax.rsqrt(meansq + 1e-06)
    for head in range(width // DH):
        here = slice(head * DH, (head + 1) * DH)
        y = wide[:, here] * inverse * gain_ref[:, here]
        y = y * cosine + pltpu.roll(y, DH - 1, 1) * sine_even + pltpu.roll(y, 1, 1) * sine_odd
        yield head, y.astype(BF16)


def query_kernel(groups, q_hbm, gain_hbm, coords_hbm, *refs):
    videos, tok_rows, width = q_hbm.shape
    outs, tables_ref, refs = refs[:videos], refs[videos], refs[videos + 1 :]
    q_ref, gain_ref, coords_ref, done_ref, sems, out_sems = refs
    own = lax.axis_index("patch") // groups
    copies = [
        pltpu.make_async_copy(source, place, sems.at[i])
        for i, (source, place) in enumerate(
            ((coords_hbm, coords_ref), (q_hbm, q_ref), (gain_hbm, gain_ref))
        )
    ]
    for copy in copies:
        copy.start()
    copies[0].wait()
    tables = rope_tables(coords_ref, tok_rows)
    for i in range(3):
        tables_ref[i] = tables[i]
    copies[1].wait()
    copies[2].wait()
    sends = []
    for s in range(videos):
        for head, y in normed_heads(q_ref[own ^ s].astype(F32), gain_ref, tables):
            done_ref[s, :, head * DH : (head + 1) * DH] = y
        sends.append(pltpu.make_async_copy(done_ref.at[s], outs[s], out_sems.at[s]))
        sends[-1].start()
    for send in sends:
        send.wait()


def key_kernel(k_ref, gain_ref, tables_ref, out_ref):
    videos = k_ref.shape[0]
    tables = [tables_ref[i] for i in range(3)]
    groups = out_ref.shape[0] // videos
    pairs = out_ref.shape[2] // DH
    for video in range(videos):
        for head, y in normed_heads(k_ref[video].astype(F32), gain_ref, tables):
            start = head % pairs * DH
            out_ref[video * groups + head // pairs, :, start : start + DH] = y


def softmax_parts(scores):
    top = jnp.max(scores, axis=-1, keepdims=True)
    weights = jnp.exp(scores - top)
    total = jnp.sum(weights, axis=-1, keepdims=True)
    return weights.astype(BF16), 1.0 / total, top + jnp.log(total)


def stacked(refs, lanes):
    rows = [ref[:, lanes].astype(F32) for ref in refs]
    return jnp.concatenate(rows, axis=0).astype(BF16)


def fresh_kernel(groups, videos, *refs):
    queries = refs[:videos]
    key_ref, value_ref, out_ref, log_ref = refs[videos:]
    me = lax.axis_index("patch")
    own, mine = me // groups, me % groups
    _, tok_rows, width = out_ref.shape
    span = width // groups
    pairs = span // DH
    rows = videos * tok_rows
    scale = 1.0 / math.sqrt(DH)
    shape = (pairs * rows, rows)
    same = lax.broadcasted_iota(jnp.int32, shape, 0) % rows // tok_rows == (
        lax.broadcasted_iota(jnp.int32, shape, 1) // tok_rows
    )
    lane = lax.broadcasted_iota(jnp.int32, (rows, DH), 1)
    logs = jnp.zeros((rows, DH), F32)
    for t in range(groups):
        lanes = pl.ds(pl.multiple_of((mine ^ t) * span, DH), span)
        query = stacked(queries, lanes)
        key = stacked([key_ref.at[me ^ (s * groups) ^ t] for s in range(videos)], slice(None))
        value = stacked([value_ref.at[own ^ s] for s in range(videos)], lanes)
        scores = jnp.concatenate(
            [
                lax.dot_general(
                    query[:, pair * DH : (pair + 1) * DH],
                    key[:, pair * DH : (pair + 1) * DH],
                    TRANSPOSED,
                    preferred_element_type=F32,
                )
                for pair in range(pairs)
            ],
            axis=0,
        )
        weights, inverse, log = softmax_parts(jnp.where(same, scores * scale, -jnp.inf))
        for pair in range(pairs):
            here = slice(pair * rows, (pair + 1) * rows)
            head = t * pairs + pair
            result = inverse[here] * jnp.dot(
                weights[here],
                value[:, pair * DH : (pair + 1) * DH],
                preferred_element_type=F32,
            )
            logs = jnp.where(lane == head, log[here], logs)
            for s in range(videos):
                out_ref[s, :, head * DH : (head + 1) * DH] = result[s * tok_rows : (s + 1) * tok_rows]
    for s in range(videos):
        log_ref[s] = logs[s * tok_rows : (s + 1) * tok_rows]


def stale_kernel(groups, videos, *refs):
    queries, pieces, outs = refs[:videos], refs[videos : videos + groups], refs[videos + groups :]
    me = lax.axis_index("patch")
    mine = me % groups
    pairs, total_rows, _ = pieces[0].shape
    tok_rows, width = queries[0].shape
    span = pairs * DH
    rows = videos * tok_rows
    scale = 1.0 / math.sqrt(DH)
    shape = (pairs * rows, total_rows)
    patch = (lax.broadcasted_iota(jnp.int32, shape, 0) % rows // tok_rows * groups) ^ me
    own = patch == lax.broadcasted_iota(jnp.int32, shape, 1) // tok_rows
    lane = lax.broadcasted_iota(jnp.int32, (rows, DH), 1)
    logs = jnp.zeros((rows, DH), F32)
    for t in range(groups):
        start = pl.multiple_of((mine ^ t) * span, DH)
        query = stacked(queries, pl.ds(start, span))
        scores = jnp.concatenate(
            [
                lax.dot_general(
                    query[:, pair * DH : (pair + 1) * DH],
                    pieces[t][pair, :, :DH],
                    TRANSPOSED,
                    preferred_element_type=F32,
                )
                for pair in range(pairs)
            ],
            axis=0,
        )
        weights, inverse, log = softmax_parts(jnp.where(own, -jnp.inf, scores * scale))
        results = []
        for pair in range(pairs):
            here = slice(pair * rows, (pair + 1) * rows)
            results.append(
                inverse[here]
                * jnp.dot(weights[here], pieces[t][pair, :, DH:], preferred_element_type=F32)
            )
            logs = jnp.where(lane == t * pairs + pair, log[here], logs)
        result = jnp.concatenate(results, axis=1).astype(BF16)
        for s in range(videos):
            outs[s][:, t * span : (t + 1) * span] = result[s * tok_rows : (s + 1) * tok_rows]
    high = logs.astype(BF16).astype(F32)
    middle = (logs - high).astype(BF16).astype(F32)
    low = (logs - high - middle).astype(BF16).astype(F32)
    heads = groups * pairs
    terms = (high + pltpu.roll(middle, heads, 1) + pltpu.roll(low, 2 * heads, 1)).astype(BF16)
    for s in range(videos):
        outs[s][:, width:] = terms[s * tok_rows : (s + 1) * tok_rows]


def join_kernel(groups, videos, *refs):
    back = refs[:videos]
    fresh_ref, log_ref, out_ref, done_ref, sems = refs[videos:]
    me = lax.axis_index("patch")
    own, mine = me // groups, me % groups
    _, tok_rows, width = fresh_ref.shape
    heads = width // DH
    pairs = heads // groups
    span = pairs * DH
    copies = []
    for s in range(videos):
        terms = back[s][:, width:].astype(F32)
        stale_log = terms + pltpu.roll(terms, DH - heads, 1) + pltpu.roll(terms, DH - 2 * heads, 1)
        share = 1.0 / (1.0 + jnp.exp(stale_log - log_ref[s]))
        for t in range(groups):
            parts = []
            for pair in range(pairs):
                head = t * pairs + pair
                here = slice(head * DH, (head + 1) * DH)
                stale = back[s][:, here].astype(F32)
                parts.append(stale + share[:, head : head + 1] * (fresh_ref[s, :, here] - stale))
            lanes = pl.ds(pl.multiple_of((mine ^ t) * span, DH), span)
            done_ref[s, :, lanes] = jnp.concatenate(parts, axis=1).astype(BF16)
        copies.append(pltpu.make_async_copy(done_ref.at[s], out_ref.at[own ^ s], sems.at[s]))
        copies[-1].start()
    for copy in copies:
        copy.wait()


def cache_kernel(key_ref, value_ref, out_ref, sems):
    copies = []
    for pair in range(out_ref.shape[0]):
        for part, source in enumerate((key_ref.at[:, :, pl.ds(pair * DH, DH)], value_ref.at[:, pair])):
            target = out_ref.at[pair, :, :, pl.ds(part * DH, DH)]
            copies.append(pltpu.make_async_copy(source, target, sems.at[part, pair]))
            copies[-1].start()
    for copy in copies:
        copy.wait()


def permuted(array, offset, patches):
    return lax.ppermute(array, "patch", [(i, i ^ offset) for i in range(patches)])


def exchange(arrays, stride, patches):
    return [arrays[0]] + [
        permuted(arrays[s], s * stride, patches) for s in range(1, len(arrays))
    ]


def local(queries, keys, values, q_gain, k_gain, stale_cache, coords):
    videos, tok_rows, width = queries.shape
    pairs_here, total_rows, _ = stale_cache.shape
    patches = total_rows // tok_rows
    groups = patches // videos
    rows = jax.ShapeDtypeStruct((tok_rows, width), BF16)

    def kernel(body, name, limit, cost=0, **kwargs):
        return pl.pallas_call(
            body,
            name=name,
            compiler_params=pltpu.CompilerParams(vmem_limit_bytes=limit * MIB),
            cost_estimate=pl.CostEstimate(flops=0, bytes_accessed=cost, transcendentals=0),
            **kwargs,
        )

    pieces = {0: stale_cache}
    bit = groups // 2
    pieces[bit] = permuted(stale_cache, bit, patches)
    value_sent = jnp.transpose(values.reshape(videos, tok_rows, width // DH, DH), (0, 2, 1, 3))
    value_got = lax.all_to_all(
        value_sent.reshape(patches, pairs_here, tok_rows, DH), "patch", split_axis=0, concat_axis=0, tiled=True
    )
    *query, tables = kernel(
        functools.partial(query_kernel, groups),
        "query",
        56,
        out_shape=[rows] * videos + [jax.ShapeDtypeStruct((3, tok_rows, DH), F32)],
        in_specs=[HBM] * 3,
        out_specs=[HBM] * videos + [VMEM],
        scratch_shapes=[
            pltpu.VMEM(queries.shape, BF16),
            pltpu.VMEM((1, width), F32),
            pltpu.SMEM(coords.shape, jnp.int32),
            pltpu.VMEM(queries.shape, BF16),
            pltpu.SemaphoreType.DMA((3,)),
            pltpu.SemaphoreType.DMA((videos,)),
        ],
    )(queries, q_gain.reshape(1, width), coords)
    query_got = exchange(query, groups, patches)
    key = kernel(
        key_kernel,
        "key",
        16,
        out_shape=jax.ShapeDtypeStruct((patches, tok_rows, pairs_here * DH), BF16),
        in_specs=[VMEM] * 3,
        out_specs=VMEM,
    )(keys, k_gain.reshape(1, width), tables)
    key_sent, query_got = lax.optimization_barrier((key, query_got))
    key_got = lax.all_to_all(key_sent, "patch", split_axis=0, concat_axis=0, tiled=True)
    fresh_sum, fresh_log = kernel(
        functools.partial(fresh_kernel, groups, videos),
        "fresh",
        16,
        out_shape=(
            jax.ShapeDtypeStruct((videos, tok_rows, width), F32),
            jax.ShapeDtypeStruct((videos, tok_rows, DH), F32),
        ),
        in_specs=[VMEM] * (videos + 2),
        out_specs=(VMEM, VMEM),
    )(*query, key, values)
    pieces, query_got, fresh_log = lax.optimization_barrier((pieces, query_got, fresh_log))
    while bit > 1:
        bit //= 2
        pieces.update({t | bit: permuted(piece, bit, patches) for t, piece in list(pieces.items())})
    result = kernel(
        functools.partial(stale_kernel, groups, videos),
        "stale",
        32,
        out_shape=[jax.ShapeDtypeStruct((tok_rows, width + DH), BF16)] * videos,
        in_specs=[VMEM] * (videos + groups),
        out_specs=[VMEM] * videos,
    )(*query_got, *[pieces[t] for t in range(groups)])
    back = exchange(result, groups, patches)
    next_cache = kernel(
        cache_kernel,
        "cache",
        16,
        out_shape=jax.ShapeDtypeStruct((pairs_here, patches, tok_rows, 2 * DH), BF16),
        in_specs=[VMEM, VMEM],
        out_specs=HBM,
        scratch_shapes=[pltpu.SemaphoreType.DMA((2, pairs_here))],
    )(key_got, value_got)
    attended = kernel(
        functools.partial(join_kernel, groups, videos),
        "join",
        16,
        out_shape=jax.ShapeDtypeStruct(queries.shape, BF16),
        in_specs=[VMEM] * (videos + 2),
        out_specs=HBM,
        scratch_shapes=[
            pltpu.VMEM(queries.shape, BF16),
            pltpu.SemaphoreType.DMA((videos,)),
        ],
    )(*back, fresh_sum, fresh_log)
    return (attended, next_cache.reshape(stale_cache.shape))


def solution(mesh):
    in_specs = (
        P("req", "patch", None),
        P("req", "patch", None),
        P("req", "patch", None),
        P(),
        P(),
        P(("req", "patch"), None, None),
        P(None, "patch"),
    )
    out_specs = (P("req", "patch", None), P(("req", "patch"), None, None))
    return jax.shard_map(local, mesh=mesh, in_specs=in_specs, out_specs=out_specs, check_vma=False)
```

```python
import functools
import math

import jax
import jax.numpy as jnp
from jax import lax
from jax.experimental import pallas as pl
from jax.experimental.pallas import tpu as pltpu
from jax.sharding import PartitionSpec as P

DH = 128
VMEM = pl.BlockSpec(memory_space=pltpu.VMEM)
HBM = pl.BlockSpec(memory_space=pltpu.HBM)
SMEM = pl.BlockSpec(memory_space=pltpu.SMEM)
MIB = 1024 * 1024
BF16 = jnp.bfloat16
F32 = jnp.float32
TRANSPOSED = (((1,), (1,)), ((), ()))


def rope_tables(coords_ref, tok_rows):
    half = DH // 2
    side = DH // 6
    first = half - 2 * side
    shape = (tok_rows, DH)
    row = lax.broadcasted_iota(jnp.int32, shape, 0)
    lane = lax.broadcasted_iota(jnp.int32, shape, 1)
    pair = lane // 2
    axis = (pair >= first).astype(jnp.int32) + (pair >= first + side).astype(jnp.int32)
    place = jnp.zeros(shape, jnp.int32)
    for which in range(3):
        for token in range(tok_rows):
            place = jnp.where((axis == which) & (row == token), coords_ref[which, token], place)
    step = jnp.where(axis == 0, pair, jnp.where(axis == 1, pair - first, pair - first - side))
    count = jnp.where(axis == 0, float(first), float(side))
    freq = jnp.exp(step.astype(F32) / count * (-math.log(10000.0)))
    angle = place.astype(F32) * freq
    sine = jnp.sin(angle)
    even = lane % 2 == 0
    return jnp.cos(angle), jnp.where(even, -sine, 0.0), jnp.where(even, 0.0, sine)


def normed_heads(wide, gain_ref, tables):
    cosine, sine_even, sine_odd = tables
    width = wide.shape[-1]
    meansq = jnp.sum(wide * wide, axis=-1, keepdims=True) * (1.0 / width)
    inverse = lax.rsqrt(meansq + 1e-06)
    for head in range(width // DH):
        here = slice(head * DH, (head + 1) * DH)
        y = wide[:, here] * inverse * gain_ref[:, here]
        y = y * cosine + pltpu.roll(y, DH - 1, 1) * sine_even + pltpu.roll(y, 1, 1) * sine_odd
        yield head, y.astype(BF16)


def query_kernel(groups, q_hbm, gain_hbm, coords_hbm, *refs):
    videos, tok_rows, width = q_hbm.shape
    outs, tables_ref, refs = refs[:videos], refs[videos], refs[videos + 1 :]
    q_ref, gain_ref, coords_ref, done_ref, sems, out_sems = refs
    own = lax.axis_index("patch") // groups
    copies = [
        pltpu.make_async_copy(source, place, sems.at[i])
        for i, (source, place) in enumerate(
            ((coords_hbm, coords_ref), (q_hbm, q_ref), (gain_hbm, gain_ref))
        )
    ]
    for copy in copies:
        copy.start()
    copies[0].wait()
    tables = rope_tables(coords_ref, tok_rows)
    for i in range(3):
        tables_ref[i] = tables[i]
    copies[1].wait()
    copies[2].wait()
    sends = []
    for s in range(videos):
        for head, y in normed_heads(q_ref[own ^ s].astype(F32), gain_ref, tables):
            done_ref[s, :, head * DH : (head + 1) * DH] = y
        sends.append(pltpu.make_async_copy(done_ref.at[s], outs[s], out_sems.at[s]))
        sends[-1].start()
    for send in sends:
        send.wait()


def key_kernel(k_ref, gain_ref, tables_ref, out_ref):
    videos = k_ref.shape[0]
    tables = [tables_ref[i] for i in range(3)]
    groups = out_ref.shape[0] // videos
    pairs = out_ref.shape[2] // DH
    for video in range(videos):
        for head, y in normed_heads(k_ref[video].astype(F32), gain_ref, tables):
            start = head % pairs * DH
            out_ref[video * groups + head // pairs, :, start : start + DH] = y


def softmax_parts(scores):
    top = jnp.max(scores, axis=-1, keepdims=True)
    weights = jnp.exp(scores - top)
    total = jnp.sum(weights, axis=-1, keepdims=True)
    return weights.astype(BF16), 1.0 / total, top + jnp.log(total)


def stacked(refs, lanes):
    rows = [ref[:, lanes].astype(F32) for ref in refs]
    return jnp.concatenate(rows, axis=0).astype(BF16)


def fresh_kernel(groups, videos, *refs):
    queries = refs[:videos]
    key_ref, value_ref, out_ref, log_ref = refs[videos:]
    me = lax.axis_index("patch")
    own, mine = me // groups, me % groups
    _, tok_rows, width = out_ref.shape
    span = width // groups
    pairs = span // DH
    rows = videos * tok_rows
    scale = 1.0 / math.sqrt(DH)
    shape = (pairs * rows, rows)
    same = lax.broadcasted_iota(jnp.int32, shape, 0) % rows // tok_rows == (
        lax.broadcasted_iota(jnp.int32, shape, 1) // tok_rows
    )
    lane = lax.broadcasted_iota(jnp.int32, (rows, DH), 1)
    logs = jnp.zeros((rows, DH), F32)
    for t in range(groups):
        lanes = pl.ds(pl.multiple_of((mine ^ t) * span, DH), span)
        query = stacked(queries, lanes)
        key = stacked([key_ref.at[me ^ (s * groups) ^ t] for s in range(videos)], slice(None))
        value = stacked([value_ref.at[own ^ s] for s in range(videos)], lanes)
        scores = jnp.concatenate(
            [
                lax.dot_general(
                    query[:, pair * DH : (pair + 1) * DH],
                    key[:, pair * DH : (pair + 1) * DH],
                    TRANSPOSED,
                    preferred_element_type=F32,
                )
                for pair in range(pairs)
            ],
            axis=0,
        )
        weights, inverse, log = softmax_parts(jnp.where(same, scores * scale, -jnp.inf))
        for pair in range(pairs):
            here = slice(pair * rows, (pair + 1) * rows)
            head = t * pairs + pair
            result = inverse[here] * jnp.dot(
                weights[here],
                value[:, pair * DH : (pair + 1) * DH],
                preferred_element_type=F32,
            )
            logs = jnp.where(lane == head, log[here], logs)
            for s in range(videos):
                out_ref[s, :, head * DH : (head + 1) * DH] = result[s * tok_rows : (s + 1) * tok_rows]
    for s in range(videos):
        log_ref[s] = logs[s * tok_rows : (s + 1) * tok_rows]


def stale_kernel(groups, videos, *refs):
    queries, pieces, outs = refs[:videos], refs[videos : videos + groups], refs[videos + groups :]
    me = lax.axis_index("patch")
    mine = me % groups
    pairs, total_rows, _ = pieces[0].shape
    tok_rows, width = queries[0].shape
    span = pairs * DH
    rows = videos * tok_rows
    scale = 1.0 / math.sqrt(DH)
    shape = (pairs * rows, total_rows)
    patch = (lax.broadcasted_iota(jnp.int32, shape, 0) % rows // tok_rows * groups) ^ me
    own = patch == lax.broadcasted_iota(jnp.int32, shape, 1) // tok_rows
    lane = lax.broadcasted_iota(jnp.int32, (rows, DH), 1)
    logs = jnp.zeros((rows, DH), F32)
    for t in range(groups):
        start = pl.multiple_of((mine ^ t) * span, DH)
        query = stacked(queries, pl.ds(start, span))
        scores = jnp.concatenate(
            [
                lax.dot_general(
                    query[:, pair * DH : (pair + 1) * DH],
                    pieces[t][pair, :, :DH],
                    TRANSPOSED,
                    preferred_element_type=F32,
                )
                for pair in range(pairs)
            ],
            axis=0,
        )
        weights, inverse, log = softmax_parts(jnp.where(own, -jnp.inf, scores * scale))
        results = []
        for pair in range(pairs):
            here = slice(pair * rows, (pair + 1) * rows)
            results.append(
                inverse[here]
                * jnp.dot(weights[here], pieces[t][pair, :, DH:], preferred_element_type=F32)
            )
            logs = jnp.where(lane == t * pairs + pair, log[here], logs)
        result = jnp.concatenate(results, axis=1).astype(BF16)
        for s in range(videos):
            outs[s][:, t * span : (t + 1) * span] = result[s * tok_rows : (s + 1) * tok_rows]
    high = logs.astype(BF16).astype(F32)
    middle = (logs - high).astype(BF16).astype(F32)
    low = (logs - high - middle).astype(BF16).astype(F32)
    heads = groups * pairs
    terms = (high + pltpu.roll(middle, heads, 1) + pltpu.roll(low, 2 * heads, 1)).astype(BF16)
    for s in range(videos):
        outs[s][:, width:] = terms[s * tok_rows : (s + 1) * tok_rows]


def join_kernel(groups, videos, *refs):
    back = refs[:videos]
    fresh_ref, log_ref, out_ref, done_ref, sems = refs[videos:]
    me = lax.axis_index("patch")
    own, mine = me // groups, me % groups
    _, tok_rows, width = fresh_ref.shape
    heads = width // DH
    pairs = heads // groups
    span = pairs * DH
    copies = []
    for s in range(videos):
        terms = back[s][:, width:].astype(F32)
        stale_log = terms + pltpu.roll(terms, DH - heads, 1) + pltpu.roll(terms, DH - 2 * heads, 1)
        share = 1.0 / (1.0 + jnp.exp(stale_log - log_ref[s]))
        for t in range(groups):
            parts = []
            for pair in range(pairs):
                head = t * pairs + pair
                here = slice(head * DH, (head + 1) * DH)
                stale = back[s][:, here].astype(F32)
                parts.append(stale + share[:, head : head + 1] * (fresh_ref[s, :, here] - stale))
            lanes = pl.ds(pl.multiple_of((mine ^ t) * span, DH), span)
            done_ref[s, :, lanes] = jnp.concatenate(parts, axis=1).astype(BF16)
        copies.append(pltpu.make_async_copy(done_ref.at[s], out_ref.at[own ^ s], sems.at[s]))
        copies[-1].start()
    for copy in copies:
        copy.wait()


def cache_kernel(key_ref, value_ref, out_ref, sems):
    copies = []
    for pair in range(out_ref.shape[0]):
        for part, source in enumerate((key_ref.at[:, :, pl.ds(pair * DH, DH)], value_ref.at[:, pair])):
            target = out_ref.at[pair, :, :, pl.ds(part * DH, DH)]
            copies.append(pltpu.make_async_copy(source, target, sems.at[part, pair]))
            copies[-1].start()
    for copy in copies:
        copy.wait()


def permuted(array, offset, patches):
    return lax.ppermute(array, "patch", [(i, i ^ offset) for i in range(patches)])


def exchange(arrays, stride, patches):
    return [arrays[0]] + [
        permuted(arrays[s], s * stride, patches) for s in range(1, len(arrays))
    ]


def local(queries, keys, values, q_gain, k_gain, stale_cache, coords):
    videos, tok_rows, width = queries.shape
    pairs_here, total_rows, _ = stale_cache.shape
    patches = total_rows // tok_rows
    groups = patches // videos
    rows = jax.ShapeDtypeStruct((tok_rows, width), BF16)

    def kernel(body, name, limit, cost=0, **kwargs):
        return pl.pallas_call(
            body,
            name=name,
            compiler_params=pltpu.CompilerParams(vmem_limit_bytes=limit * MIB),
            cost_estimate=pl.CostEstimate(flops=0, bytes_accessed=cost, transcendentals=0),
            **kwargs,
        )

    pieces = {0: stale_cache}
    bit = groups // 2
    pieces[bit] = permuted(stale_cache, bit, patches)
    value_sent = jnp.transpose(values.reshape(videos, tok_rows, width // DH, DH), (0, 2, 1, 3))
    value_got = lax.all_to_all(
        value_sent.reshape(patches, pairs_here, tok_rows, DH), "patch", split_axis=0, concat_axis=0, tiled=True
    )
    *query, tables = kernel(
        functools.partial(query_kernel, groups),
        "query",
        56,
        out_shape=[rows] * videos + [jax.ShapeDtypeStruct((3, tok_rows, DH), F32)],
        in_specs=[HBM] * 3,
        out_specs=[HBM] * videos + [VMEM],
        scratch_shapes=[
            pltpu.VMEM(queries.shape, BF16),
            pltpu.VMEM((1, width), F32),
            pltpu.SMEM(coords.shape, jnp.int32),
            pltpu.VMEM(queries.shape, BF16),
            pltpu.SemaphoreType.DMA((3,)),
            pltpu.SemaphoreType.DMA((videos,)),
        ],
    )(queries, q_gain.reshape(1, width), coords)
    query_got = exchange(query, groups, patches)
    key = kernel(
        key_kernel,
        "key",
        16,
        out_shape=jax.ShapeDtypeStruct((patches, tok_rows, pairs_here * DH), BF16),
        in_specs=[VMEM] * 3,
        out_specs=VMEM,
    )(keys, k_gain.reshape(1, width), tables)
    key_got = lax.all_to_all(key, "patch", split_axis=0, concat_axis=0, tiled=True)
    pieces, query_got = lax.optimization_barrier((pieces, query_got))
    while bit > 1:
        bit //= 2
        pieces.update({t | bit: permuted(piece, bit, patches) for t, piece in list(pieces.items())})
    result = kernel(
        functools.partial(stale_kernel, groups, videos),
        "stale",
        32,
        out_shape=[jax.ShapeDtypeStruct((tok_rows, width + DH), BF16)] * videos,
        in_specs=[VMEM] * (videos + groups),
        out_specs=[VMEM] * videos,
    )(*query_got, *[pieces[t] for t in range(groups)])
    result, key_late = lax.optimization_barrier((result, key))
    back = exchange(result, groups, patches)
    fresh_sum, fresh_log = kernel(
        functools.partial(fresh_kernel, groups, videos),
        "fresh",
        16,
        out_shape=(
            jax.ShapeDtypeStruct((videos, tok_rows, width), F32),
            jax.ShapeDtypeStruct((videos, tok_rows, DH), F32),
        ),
        in_specs=[VMEM] * (videos + 2),
        out_specs=(VMEM, VMEM),
    )(*query, key_late, values)
    attended = kernel(
        functools.partial(join_kernel, groups, videos),
        "join",
        16,
        out_shape=jax.ShapeDtypeStruct(queries.shape, BF16),
        in_specs=[VMEM] * (videos + 2),
        out_specs=HBM,
        scratch_shapes=[
            pltpu.VMEM(queries.shape, BF16),
            pltpu.SemaphoreType.DMA((videos,)),
        ],
    )(*back, fresh_sum, fresh_log)
    attended, key_got, value_got = lax.optimization_barrier((attended, key_got, value_got))
    next_cache = kernel(
        cache_kernel,
        "cache",
        16,
        out_shape=jax.ShapeDtypeStruct((pairs_here, patches, tok_rows, 2 * DH), BF16),
        in_specs=[VMEM, VMEM],
        out_specs=HBM,
        scratch_shapes=[pltpu.SemaphoreType.DMA((2, pairs_here))],
    )(key_got, value_got)
    return (attended, next_cache.reshape(stale_cache.shape))


def solution(mesh):
    in_specs = (
        P("req", "patch", None),
        P("req", "patch", None),
        P("req", "patch", None),
        P(),
        P(),
        P(("req", "patch"), None, None),
        P(None, "patch"),
    )
    out_specs = (P("req", "patch", None), P(("req", "patch"), None, None))
    return jax.shard_map(local, mesh=mesh, in_specs=in_specs, out_specs=out_specs, check_vma=False)
```

```python
import functools
import math

import jax
import jax.numpy as jnp
from jax import lax
from jax.experimental import pallas as pl
from jax.experimental.pallas import tpu as pltpu
from jax.sharding import PartitionSpec as P

DH = 128
VMEM = pl.BlockSpec(memory_space=pltpu.VMEM)
HBM = pl.BlockSpec(memory_space=pltpu.HBM)
SMEM = pl.BlockSpec(memory_space=pltpu.SMEM)
MIB = 1024 * 1024
BF16 = jnp.bfloat16
F32 = jnp.float32
TRANSPOSED = (((1,), (1,)), ((), ()))


def rope_tables(coords_ref, tok_rows):
    half = DH // 2
    side = DH // 6
    first = half - 2 * side
    shape = (tok_rows, DH)
    row = lax.broadcasted_iota(jnp.int32, shape, 0)
    lane = lax.broadcasted_iota(jnp.int32, shape, 1)
    pair = lane // 2
    axis = (pair >= first).astype(jnp.int32) + (pair >= first + side).astype(jnp.int32)
    place = jnp.zeros(shape, jnp.int32)
    for which in range(3):
        for token in range(tok_rows):
            place = jnp.where((axis == which) & (row == token), coords_ref[which, token], place)
    step = jnp.where(axis == 0, pair, jnp.where(axis == 1, pair - first, pair - first - side))
    count = jnp.where(axis == 0, float(first), float(side))
    freq = jnp.exp(step.astype(F32) / count * (-math.log(10000.0)))
    angle = place.astype(F32) * freq
    sine = jnp.sin(angle)
    even = lane % 2 == 0
    return jnp.cos(angle), jnp.where(even, -sine, 0.0), jnp.where(even, 0.0, sine)


def normed_heads(wide, gain_ref, tables):
    cosine, sine_even, sine_odd = tables
    width = wide.shape[-1]
    meansq = jnp.sum(wide * wide, axis=-1, keepdims=True) * (1.0 / width)
    inverse = lax.rsqrt(meansq + 1e-06)
    for head in range(width // DH):
        here = slice(head * DH, (head + 1) * DH)
        y = wide[:, here] * inverse * gain_ref[:, here]
        y = y * cosine + pltpu.roll(y, DH - 1, 1) * sine_even + pltpu.roll(y, 1, 1) * sine_odd
        yield head, y.astype(BF16)


def query_kernel(groups, q_hbm, gain_hbm, coords_hbm, *refs):
    videos, tok_rows, width = q_hbm.shape
    outs, tables_ref, refs = refs[:videos], refs[videos], refs[videos + 1 :]
    q_ref, gain_ref, coords_ref, done_ref, sems, out_sems = refs
    own = lax.axis_index("patch") // groups
    copies = [
        pltpu.make_async_copy(source, place, sems.at[i])
        for i, (source, place) in enumerate(
            ((coords_hbm, coords_ref), (q_hbm, q_ref), (gain_hbm, gain_ref))
        )
    ]
    for copy in copies:
        copy.start()
    copies[0].wait()
    tables = rope_tables(coords_ref, tok_rows)
    for i in range(3):
        tables_ref[i] = tables[i]
    copies[1].wait()
    copies[2].wait()
    sends = []
    for s in range(videos):
        for head, y in normed_heads(q_ref[own ^ s].astype(F32), gain_ref, tables):
            done_ref[s, :, head * DH : (head + 1) * DH] = y
        sends.append(pltpu.make_async_copy(done_ref.at[s], outs[s], out_sems.at[s]))
        sends[-1].start()
    for send in sends:
        send.wait()


def key_kernel(k_ref, gain_ref, tables_ref, out_ref):
    videos = k_ref.shape[0]
    tables = [tables_ref[i] for i in range(3)]
    groups = out_ref.shape[0] // videos
    pairs = out_ref.shape[2] // DH
    for video in range(videos):
        for head, y in normed_heads(k_ref[video].astype(F32), gain_ref, tables):
            start = head % pairs * DH
            out_ref[video * groups + head // pairs, :, start : start + DH] = y


def softmax_parts(scores):
    top = jnp.max(scores, axis=-1, keepdims=True)
    weights = jnp.exp(scores - top)
    total = jnp.sum(weights, axis=-1, keepdims=True)
    return weights.astype(BF16), 1.0 / total, top + jnp.log(total)


def stacked(refs, lanes):
    rows = [ref[:, lanes].astype(F32) for ref in refs]
    return jnp.concatenate(rows, axis=0).astype(BF16)


def fresh_kernel(groups, videos, *refs):
    queries = refs[:videos]
    key_ref, value_ref, out_ref, log_ref = refs[videos:]
    me = lax.axis_index("patch")
    own, mine = me // groups, me % groups
    _, tok_rows, width = out_ref.shape
    span = width // groups
    pairs = span // DH
    rows = videos * tok_rows
    scale = 1.0 / math.sqrt(DH)
    shape = (pairs * rows, rows)
    same = lax.broadcasted_iota(jnp.int32, shape, 0) % rows // tok_rows == (
        lax.broadcasted_iota(jnp.int32, shape, 1) // tok_rows
    )
    lane = lax.broadcasted_iota(jnp.int32, (rows, DH), 1)
    logs = jnp.zeros((rows, DH), F32)
    for t in range(groups):
        lanes = pl.ds(pl.multiple_of((mine ^ t) * span, DH), span)
        query = stacked(queries, lanes)
        key = stacked([key_ref.at[me ^ (s * groups) ^ t] for s in range(videos)], slice(None))
        value = stacked([value_ref.at[own ^ s] for s in range(videos)], lanes)
        scores = jnp.concatenate(
            [
                lax.dot_general(
                    query[:, pair * DH : (pair + 1) * DH],
                    key[:, pair * DH : (pair + 1) * DH],
                    TRANSPOSED,
                    preferred_element_type=F32,
                )
                for pair in range(pairs)
            ],
            axis=0,
        )
        weights, inverse, log = softmax_parts(jnp.where(same, scores * scale, -jnp.inf))
        for pair in range(pairs):
            here = slice(pair * rows, (pair + 1) * rows)
            head = t * pairs + pair
            result = inverse[here] * jnp.dot(
                weights[here],
                value[:, pair * DH : (pair + 1) * DH],
                preferred_element_type=F32,
            )
            logs = jnp.where(lane == head, log[here], logs)
            for s in range(videos):
                out_ref[s, :, head * DH : (head + 1) * DH] = result[s * tok_rows : (s + 1) * tok_rows]
    for s in range(videos):
        log_ref[s] = logs[s * tok_rows : (s + 1) * tok_rows]


def stale_kernel(groups, videos, *refs):
    queries, pieces, outs = refs[:videos], refs[videos : videos + groups], refs[videos + groups :]
    me = lax.axis_index("patch")
    mine = me % groups
    pairs, total_rows, _ = pieces[0].shape
    tok_rows, width = queries[0].shape
    span = pairs * DH
    rows = videos * tok_rows
    scale = 1.0 / math.sqrt(DH)
    shape = (pairs * rows, total_rows)
    patch = (lax.broadcasted_iota(jnp.int32, shape, 0) % rows // tok_rows * groups) ^ me
    own = patch == lax.broadcasted_iota(jnp.int32, shape, 1) // tok_rows
    lane = lax.broadcasted_iota(jnp.int32, (rows, DH), 1)
    logs = jnp.zeros((rows, DH), F32)
    for t in range(groups):
        start = pl.multiple_of((mine ^ t) * span, DH)
        query = stacked(queries, pl.ds(start, span))
        scores = jnp.concatenate(
            [
                lax.dot_general(
                    query[:, pair * DH : (pair + 1) * DH],
                    pieces[t][pair, :, :DH],
                    TRANSPOSED,
                    preferred_element_type=F32,
                )
                for pair in range(pairs)
            ],
            axis=0,
        )
        weights, inverse, log = softmax_parts(jnp.where(own, -jnp.inf, scores * scale))
        results = []
        for pair in range(pairs):
            here = slice(pair * rows, (pair + 1) * rows)
            results.append(
                inverse[here]
                * jnp.dot(weights[here], pieces[t][pair, :, DH:], preferred_element_type=F32)
            )
            logs = jnp.where(lane == t * pairs + pair, log[here], logs)
        result = jnp.concatenate(results, axis=1).astype(BF16)
        for s in range(videos):
            outs[s][:, t * span : (t + 1) * span] = result[s * tok_rows : (s + 1) * tok_rows]
    high = logs.astype(BF16).astype(F32)
    middle = (logs - high).astype(BF16).astype(F32)
    low = (logs - high - middle).astype(BF16).astype(F32)
    heads = groups * pairs
    terms = (high + pltpu.roll(middle, heads, 1) + pltpu.roll(low, 2 * heads, 1)).astype(BF16)
    for s in range(videos):
        outs[s][:, width:] = terms[s * tok_rows : (s + 1) * tok_rows]


def join_kernel(groups, videos, *refs):
    back = refs[:videos]
    fresh_ref, log_ref, out_ref, done_ref, sems = refs[videos:]
    me = lax.axis_index("patch")
    own, mine = me // groups, me % groups
    _, tok_rows, width = fresh_ref.shape
    heads = width // DH
    pairs = heads // groups
    span = pairs * DH
    copies = []
    for s in range(videos):
        terms = back[s][:, width:].astype(F32)
        stale_log = terms + pltpu.roll(terms, DH - heads, 1) + pltpu.roll(terms, DH - 2 * heads, 1)
        share = 1.0 / (1.0 + jnp.exp(stale_log - log_ref[s]))
        for t in range(groups):
            parts = []
            for pair in range(pairs):
                head = t * pairs + pair
                here = slice(head * DH, (head + 1) * DH)
                stale = back[s][:, here].astype(F32)
                parts.append(stale + share[:, head : head + 1] * (fresh_ref[s, :, here] - stale))
            lanes = pl.ds(pl.multiple_of((mine ^ t) * span, DH), span)
            done_ref[s, :, lanes] = jnp.concatenate(parts, axis=1).astype(BF16)
        copies.append(pltpu.make_async_copy(done_ref.at[s], out_ref.at[own ^ s], sems.at[s]))
        copies[-1].start()
    for copy in copies:
        copy.wait()


def cache_kernel(key_ref, value_ref, out_ref, sems):
    copies = []
    for pair in range(out_ref.shape[0]):
        for part, source in enumerate((key_ref.at[:, :, pl.ds(pair * DH, DH)], value_ref.at[:, pair])):
            target = out_ref.at[pair, :, :, pl.ds(part * DH, DH)]
            copies.append(pltpu.make_async_copy(source, target, sems.at[part, pair]))
            copies[-1].start()
    for copy in copies:
        copy.wait()


def permuted(array, offset, patches):
    return lax.ppermute(array, "patch", [(i, i ^ offset) for i in range(patches)])


def exchange(arrays, stride, patches):
    return [arrays[0]] + [
        permuted(arrays[s], s * stride, patches) for s in range(1, len(arrays))
    ]


def local(queries, keys, values, q_gain, k_gain, stale_cache, coords):
    videos, tok_rows, width = queries.shape
    pairs_here, total_rows, _ = stale_cache.shape
    patches = total_rows // tok_rows
    groups = patches // videos
    rows = jax.ShapeDtypeStruct((tok_rows, width), BF16)

    def kernel(body, name, limit, cost=0, **kwargs):
        return pl.pallas_call(
            body,
            name=name,
            compiler_params=pltpu.CompilerParams(vmem_limit_bytes=limit * MIB),
            cost_estimate=pl.CostEstimate(flops=0, bytes_accessed=cost, transcendentals=0),
            **kwargs,
        )

    pieces = {0: stale_cache}
    bit = groups // 2
    pieces[bit] = permuted(stale_cache, bit, patches)
    value_sent = jnp.transpose(values.reshape(videos, tok_rows, width // DH, DH), (0, 2, 1, 3))
    value_got = lax.all_to_all(
        value_sent.reshape(patches, pairs_here, tok_rows, DH), "patch", split_axis=0, concat_axis=0, tiled=True
    )
    *query, tables = kernel(
        functools.partial(query_kernel, groups),
        "query",
        56,
        out_shape=[rows] * videos + [jax.ShapeDtypeStruct((3, tok_rows, DH), F32)],
        in_specs=[HBM] * 3,
        out_specs=[HBM] * videos + [VMEM],
        scratch_shapes=[
            pltpu.VMEM(queries.shape, BF16),
            pltpu.VMEM((1, width), F32),
            pltpu.SMEM(coords.shape, jnp.int32),
            pltpu.VMEM(queries.shape, BF16),
            pltpu.SemaphoreType.DMA((3,)),
            pltpu.SemaphoreType.DMA((videos,)),
        ],
    )(queries, q_gain.reshape(1, width), coords)
    query_got = exchange(query, groups, patches)
    key = kernel(
        key_kernel,
        "key",
        16,
        out_shape=jax.ShapeDtypeStruct((patches, tok_rows, pairs_here * DH), BF16),
        in_specs=[VMEM] * 3,
        out_specs=VMEM,
    )(keys, k_gain.reshape(1, width), tables)
    key_sent, value_got = lax.optimization_barrier((key, value_got))
    key_got = lax.all_to_all(key_sent, "patch", split_axis=0, concat_axis=0, tiled=True)
    pieces, query_got = lax.optimization_barrier((pieces, query_got))
    while bit > 1:
        bit //= 2
        pieces.update({t | bit: permuted(piece, bit, patches) for t, piece in list(pieces.items())})
    result = kernel(
        functools.partial(stale_kernel, groups, videos),
        "stale",
        32,
        out_shape=[jax.ShapeDtypeStruct((tok_rows, width + DH), BF16)] * videos,
        in_specs=[VMEM] * (videos + groups),
        out_specs=[VMEM] * videos,
    )(*query_got, *[pieces[t] for t in range(groups)])
    result, key_late = lax.optimization_barrier((result, key))
    back = exchange(result, groups, patches)
    fresh_sum, fresh_log = kernel(
        functools.partial(fresh_kernel, groups, videos),
        "fresh",
        16,
        out_shape=(
            jax.ShapeDtypeStruct((videos, tok_rows, width), F32),
            jax.ShapeDtypeStruct((videos, tok_rows, DH), F32),
        ),
        in_specs=[VMEM] * (videos + 2),
        out_specs=(VMEM, VMEM),
    )(*query, key_late, values)
    next_cache = kernel(
        cache_kernel,
        "cache",
        16,
        out_shape=jax.ShapeDtypeStruct((pairs_here, patches, tok_rows, 2 * DH), BF16),
        in_specs=[VMEM, VMEM],
        out_specs=HBM,
        scratch_shapes=[pltpu.SemaphoreType.DMA((2, pairs_here))],
    )(key_got, value_got)
    attended = kernel(
        functools.partial(join_kernel, groups, videos),
        "join",
        16,
        out_shape=jax.ShapeDtypeStruct(queries.shape, BF16),
        in_specs=[VMEM] * (videos + 2),
        out_specs=HBM,
        scratch_shapes=[
            pltpu.VMEM(queries.shape, BF16),
            pltpu.SemaphoreType.DMA((videos,)),
        ],
    )(*back, fresh_sum, fresh_log)
    return (attended, next_cache.reshape(stale_cache.shape))


def solution(mesh):
    in_specs = (
        P("req", "patch", None),
        P("req", "patch", None),
        P("req", "patch", None),
        P(),
        P(),
        P(("req", "patch"), None, None),
        P(None, "patch"),
    )
    out_specs = (P("req", "patch", None), P(("req", "patch"), None, None))
    return jax.shard_map(local, mesh=mesh, in_specs=in_specs, out_specs=out_specs, check_vma=False)
```

```python
import functools
import math

import jax
import jax.numpy as jnp
from jax import lax
from jax.experimental import pallas as pl
from jax.experimental.pallas import tpu as pltpu
from jax.sharding import PartitionSpec as P

DH = 128
VMEM = pl.BlockSpec(memory_space=pltpu.VMEM)
HBM = pl.BlockSpec(memory_space=pltpu.HBM)
SMEM = pl.BlockSpec(memory_space=pltpu.SMEM)
MIB = 1024 * 1024
BF16 = jnp.bfloat16
F32 = jnp.float32
TRANSPOSED = (((1,), (1,)), ((), ()))


def rope_tables(coords_ref, tok_rows):
    half = DH // 2
    side = DH // 6
    first = half - 2 * side
    shape = (tok_rows, DH)
    row = lax.broadcasted_iota(jnp.int32, shape, 0)
    lane = lax.broadcasted_iota(jnp.int32, shape, 1)
    pair = lane // 2
    axis = (pair >= first).astype(jnp.int32) + (pair >= first + side).astype(jnp.int32)
    place = jnp.zeros(shape, jnp.int32)
    for which in range(3):
        for token in range(tok_rows):
            place = jnp.where((axis == which) & (row == token), coords_ref[which, token], place)
    step = jnp.where(axis == 0, pair, jnp.where(axis == 1, pair - first, pair - first - side))
    count = jnp.where(axis == 0, float(first), float(side))
    freq = jnp.exp(step.astype(F32) / count * (-math.log(10000.0)))
    angle = place.astype(F32) * freq
    sine = jnp.sin(angle)
    even = lane % 2 == 0
    return jnp.cos(angle), jnp.where(even, -sine, 0.0), jnp.where(even, 0.0, sine)


def normed_heads(wide, gain_ref, tables):
    cosine, sine_even, sine_odd = tables
    width = wide.shape[-1]
    meansq = jnp.sum(wide * wide, axis=-1, keepdims=True) * (1.0 / width)
    inverse = lax.rsqrt(meansq + 1e-06)
    for head in range(width // DH):
        here = slice(head * DH, (head + 1) * DH)
        y = wide[:, here] * inverse * gain_ref[:, here]
        y = y * cosine + pltpu.roll(y, DH - 1, 1) * sine_even + pltpu.roll(y, 1, 1) * sine_odd
        yield head, y.astype(BF16)


def query_kernel(groups, q_hbm, gain_hbm, coords_hbm, *refs):
    videos, tok_rows, width = q_hbm.shape
    outs, tables_ref, refs = refs[:videos], refs[videos], refs[videos + 1 :]
    q_ref, gain_ref, coords_ref, done_ref, sems, out_sems = refs
    own = lax.axis_index("patch") // groups
    copies = [
        pltpu.make_async_copy(source, place, sems.at[i])
        for i, (source, place) in enumerate(
            ((coords_hbm, coords_ref), (q_hbm, q_ref), (gain_hbm, gain_ref))
        )
    ]
    for copy in copies:
        copy.start()
    copies[0].wait()
    tables = rope_tables(coords_ref, tok_rows)
    for i in range(3):
        tables_ref[i] = tables[i]
    copies[1].wait()
    copies[2].wait()
    sends = []
    for s in range(videos):
        for head, y in normed_heads(q_ref[own ^ s].astype(F32), gain_ref, tables):
            done_ref[s, :, head * DH : (head + 1) * DH] = y
        sends.append(pltpu.make_async_copy(done_ref.at[s], outs[s], out_sems.at[s]))
        sends[-1].start()
    for send in sends:
        send.wait()


def key_kernel(k_ref, v_ref, gain_ref, tables_ref, out_ref):
    videos, tok_rows, width = k_ref.shape
    tables = [tables_ref[i] for i in range(3)]
    span = out_ref.shape[2]
    groups = out_ref.shape[0] // videos
    pairs = span // (2 * DH)
    for video in range(videos):
        for head, y in normed_heads(k_ref[video].astype(F32), gain_ref, tables):
            target, start = video * groups + head // pairs, head % pairs * 2 * DH
            out_ref[target, :, start : start + DH] = y
            out_ref[target, :, start + DH : start + 2 * DH] = v_ref[
                video, :, head * DH : (head + 1) * DH
            ]


def softmax_parts(scores):
    top = jnp.max(scores, axis=-1, keepdims=True)
    weights = jnp.exp(scores - top)
    total = jnp.sum(weights, axis=-1, keepdims=True)
    return weights.astype(BF16), 1.0 / total, top + jnp.log(total)


def stacked(refs, lanes):
    rows = [ref[:, lanes].astype(F32) for ref in refs]
    return jnp.concatenate(rows, axis=0).astype(BF16)


def fresh_kernel(groups, videos, *refs):
    queries = refs[:videos]
    fresh_ref, out_ref, log_ref = refs[videos:]
    me = lax.axis_index("patch")
    mine = me % groups
    _, tok_rows, width = out_ref.shape
    span = width // groups
    pairs = span // DH
    rows = videos * tok_rows
    scale = 1.0 / math.sqrt(DH)
    shape = (pairs * rows, rows)
    same = lax.broadcasted_iota(jnp.int32, shape, 0) % rows // tok_rows == (
        lax.broadcasted_iota(jnp.int32, shape, 1) // tok_rows
    )
    lane = lax.broadcasted_iota(jnp.int32, (rows, DH), 1)
    logs = jnp.zeros((rows, DH), F32)
    for t in range(groups):
        lanes = pl.ds(pl.multiple_of((mine ^ t) * span, DH), span)
        query = stacked(queries, lanes)
        fresh = stacked([fresh_ref.at[me ^ (s * groups) ^ t] for s in range(videos)], slice(None))
        scores = jnp.concatenate(
            [
                lax.dot_general(
                    query[:, pair * DH : (pair + 1) * DH],
                    fresh[:, 2 * pair * DH : (2 * pair + 1) * DH],
                    TRANSPOSED,
                    preferred_element_type=F32,
                )
                for pair in range(pairs)
            ],
            axis=0,
        )
        weights, inverse, log = softmax_parts(jnp.where(same, scores * scale, -jnp.inf))
        for pair in range(pairs):
            here = slice(pair * rows, (pair + 1) * rows)
            head = t * pairs + pair
            result = inverse[here] * jnp.dot(
                weights[here],
                fresh[:, (2 * pair + 1) * DH : (2 * pair + 2) * DH],
                preferred_element_type=F32,
            )
            logs = jnp.where(lane == head, log[here], logs)
            for s in range(videos):
                out_ref[s, :, head * DH : (head + 1) * DH] = result[s * tok_rows : (s + 1) * tok_rows]
    for s in range(videos):
        log_ref[s] = logs[s * tok_rows : (s + 1) * tok_rows]


def stale_kernel(groups, videos, *refs):
    queries, pieces, outs = refs[:videos], refs[videos : videos + groups], refs[videos + groups :]
    me = lax.axis_index("patch")
    mine = me % groups
    pairs, total_rows, _ = pieces[0].shape
    tok_rows, width = queries[0].shape
    span = pairs * DH
    rows = videos * tok_rows
    scale = 1.0 / math.sqrt(DH)
    shape = (pairs * rows, total_rows)
    patch = (lax.broadcasted_iota(jnp.int32, shape, 0) % rows // tok_rows * groups) ^ me
    own = patch == lax.broadcasted_iota(jnp.int32, shape, 1) // tok_rows
    lane = lax.broadcasted_iota(jnp.int32, (rows, DH), 1)
    logs = jnp.zeros((rows, DH), F32)
    for t in range(groups):
        start = pl.multiple_of((mine ^ t) * span, DH)
        query = stacked(queries, pl.ds(start, span))
        scores = jnp.concatenate(
            [
                lax.dot_general(
                    query[:, pair * DH : (pair + 1) * DH],
                    pieces[t][pair, :, :DH],
                    TRANSPOSED,
                    preferred_element_type=F32,
                )
                for pair in range(pairs)
            ],
            axis=0,
        )
        weights, inverse, log = softmax_parts(jnp.where(own, -jnp.inf, scores * scale))
        results = []
        for pair in range(pairs):
            here = slice(pair * rows, (pair + 1) * rows)
            results.append(
                inverse[here]
                * jnp.dot(weights[here], pieces[t][pair, :, DH:], preferred_element_type=F32)
            )
            logs = jnp.where(lane == t * pairs + pair, log[here], logs)
        result = jnp.concatenate(results, axis=1).astype(BF16)
        for s in range(videos):
            outs[s][:, t * span : (t + 1) * span] = result[s * tok_rows : (s + 1) * tok_rows]
    high = logs.astype(BF16).astype(F32)
    middle = (logs - high).astype(BF16).astype(F32)
    low = (logs - high - middle).astype(BF16).astype(F32)
    heads = groups * pairs
    terms = (high + pltpu.roll(middle, heads, 1) + pltpu.roll(low, 2 * heads, 1)).astype(BF16)
    for s in range(videos):
        outs[s][:, width:] = terms[s * tok_rows : (s + 1) * tok_rows]


def join_kernel(groups, videos, *refs):
    back = refs[:videos]
    fresh_ref, log_ref, out_ref, done_ref, sems = refs[videos:]
    me = lax.axis_index("patch")
    own, mine = me // groups, me % groups
    _, tok_rows, width = fresh_ref.shape
    heads = width // DH
    pairs = heads // groups
    span = pairs * DH
    copies = []
    for s in range(videos):
        terms = back[s][:, width:].astype(F32)
        stale_log = terms + pltpu.roll(terms, DH - heads, 1) + pltpu.roll(terms, DH - 2 * heads, 1)
        share = 1.0 / (1.0 + jnp.exp(stale_log - log_ref[s]))
        for t in range(groups):
            parts = []
            for pair in range(pairs):
                head = t * pairs + pair
                here = slice(head * DH, (head + 1) * DH)
                stale = back[s][:, here].astype(F32)
                parts.append(stale + share[:, head : head + 1] * (fresh_ref[s, :, here] - stale))
            lanes = pl.ds(pl.multiple_of((mine ^ t) * span, DH), span)
            done_ref[s, :, lanes] = jnp.concatenate(parts, axis=1).astype(BF16)
        copies.append(pltpu.make_async_copy(done_ref.at[s], out_ref.at[own ^ s], sems.at[s]))
        copies[-1].start()
    for copy in copies:
        copy.wait()


def cache_kernel(got_ref, out_ref, sems):
    copies = []
    for pair in range(out_ref.shape[0]):
        lanes = pl.ds(2 * pair * DH, 2 * DH)
        copies.append(
            pltpu.make_async_copy(got_ref.at[:, :, lanes], out_ref.at[pair], sems.at[pair])
        )
        copies[-1].start()
    for copy in copies:
        copy.wait()


def permuted(array, offset, patches):
    return lax.ppermute(array, "patch", [(i, i ^ offset) for i in range(patches)])


def exchange(arrays, stride, patches):
    return [arrays[0]] + [
        permuted(arrays[s], s * stride, patches) for s in range(1, len(arrays))
    ]


def local(queries, keys, values, q_gain, k_gain, stale_cache, coords):
    videos, tok_rows, width = queries.shape
    pairs_here, total_rows, _ = stale_cache.shape
    patches = total_rows // tok_rows
    groups = patches // videos
    rows = jax.ShapeDtypeStruct((tok_rows, width), BF16)

    def kernel(body, name, limit, cost=0, **kwargs):
        return pl.pallas_call(
            body,
            name=name,
            compiler_params=pltpu.CompilerParams(vmem_limit_bytes=limit * MIB),
            cost_estimate=pl.CostEstimate(flops=0, bytes_accessed=cost, transcendentals=0),
            **kwargs,
        )

    pieces = {0: stale_cache}
    bit = groups // 2
    pieces[bit] = permuted(stale_cache, bit, patches)
    *query, tables = kernel(
        functools.partial(query_kernel, groups),
        "query",
        56,
        out_shape=[rows] * videos + [jax.ShapeDtypeStruct((3, tok_rows, DH), F32)],
        in_specs=[HBM] * 3,
        out_specs=[HBM] * videos + [VMEM],
        scratch_shapes=[
            pltpu.VMEM(queries.shape, BF16),
            pltpu.VMEM((1, width), F32),
            pltpu.SMEM(coords.shape, jnp.int32),
            pltpu.VMEM(queries.shape, BF16),
            pltpu.SemaphoreType.DMA((3,)),
            pltpu.SemaphoreType.DMA((videos,)),
        ],
    )(queries, q_gain.reshape(1, width), coords)
    query_got = exchange(query, groups, patches)
    fresh = kernel(
        key_kernel,
        "key",
        16,
        out_shape=jax.ShapeDtypeStruct((patches, tok_rows, 2 * pairs_here * DH), BF16),
        in_specs=[VMEM] * 4,
        out_specs=VMEM,
    )(keys, values, k_gain.reshape(1, width), tables)
    cached = lax.all_to_all(fresh, "patch", split_axis=0, concat_axis=0, tiled=True)
    pieces, query_got = lax.optimization_barrier((pieces, query_got))
    while bit > 1:
        bit //= 2
        pieces.update({t | bit: permuted(piece, bit, patches) for t, piece in list(pieces.items())})
    result = kernel(
        functools.partial(stale_kernel, groups, videos),
        "stale",
        32,
        out_shape=[jax.ShapeDtypeStruct((tok_rows, width + DH), BF16)] * videos,
        in_specs=[VMEM] * (videos + groups),
        out_specs=[VMEM] * videos,
    )(*query_got, *[pieces[t] for t in range(groups)])
    result, fresh_late = lax.optimization_barrier((result, fresh))
    back = exchange(result, groups, patches)
    fresh_sum, fresh_log = kernel(
        functools.partial(fresh_kernel, groups, videos),
        "fresh",
        16,
        out_shape=(
            jax.ShapeDtypeStruct((videos, tok_rows, width), F32),
            jax.ShapeDtypeStruct((videos, tok_rows, DH), F32),
        ),
        in_specs=[VMEM] * (videos + 1),
        out_specs=(VMEM, VMEM),
    )(*query, fresh_late)
    attended = kernel(
        functools.partial(join_kernel, groups, videos),
        "join",
        16,
        out_shape=jax.ShapeDtypeStruct(queries.shape, BF16),
        in_specs=[VMEM] * (videos + 2),
        out_specs=HBM,
        scratch_shapes=[
            pltpu.VMEM(queries.shape, BF16),
            pltpu.SemaphoreType.DMA((videos,)),
        ],
    )(*back, fresh_sum, fresh_log)
    attended, cached = lax.optimization_barrier((attended, cached))
    next_cache = kernel(
        cache_kernel,
        "cache",
        16,
        out_shape=jax.ShapeDtypeStruct((pairs_here, patches, tok_rows, 2 * DH), BF16),
        in_specs=[VMEM],
        out_specs=HBM,
        scratch_shapes=[pltpu.SemaphoreType.DMA((pairs_here,))],
    )(cached)
    return (attended, next_cache.reshape(stale_cache.shape))


def solution(mesh):
    in_specs = (
        P("req", "patch", None),
        P("req", "patch", None),
        P("req", "patch", None),
        P(),
        P(),
        P(("req", "patch"), None, None),
        P(None, "patch"),
    )
    out_specs = (P("req", "patch", None), P(("req", "patch"), None, None))
    return jax.shard_map(local, mesh=mesh, in_specs=in_specs, out_specs=out_specs, check_vma=False)
```

```python
import functools
import math

import jax
import jax.numpy as jnp
from jax import lax
from jax.experimental import pallas as pl
from jax.experimental.pallas import tpu as pltpu
from jax.sharding import PartitionSpec as P

DH = 128
VMEM = pl.BlockSpec(memory_space=pltpu.VMEM)
HBM = pl.BlockSpec(memory_space=pltpu.HBM)
SMEM = pl.BlockSpec(memory_space=pltpu.SMEM)
MIB = 1024 * 1024
BF16 = jnp.bfloat16
F32 = jnp.float32
TRANSPOSED = (((1,), (1,)), ((), ()))


def rope_tables(coords_ref, tok_rows):
    half = DH // 2
    side = DH // 6
    first = half - 2 * side
    shape = (tok_rows, DH)
    row = lax.broadcasted_iota(jnp.int32, shape, 0)
    lane = lax.broadcasted_iota(jnp.int32, shape, 1)
    pair = lane // 2
    axis = (pair >= first).astype(jnp.int32) + (pair >= first + side).astype(jnp.int32)
    place = jnp.zeros(shape, jnp.int32)
    for which in range(3):
        for token in range(tok_rows):
            place = jnp.where((axis == which) & (row == token), coords_ref[which, token], place)
    step = jnp.where(axis == 0, pair, jnp.where(axis == 1, pair - first, pair - first - side))
    count = jnp.where(axis == 0, float(first), float(side))
    freq = jnp.exp(step.astype(F32) / count * (-math.log(10000.0)))
    angle = place.astype(F32) * freq
    sine = jnp.sin(angle)
    even = lane % 2 == 0
    return jnp.cos(angle), jnp.where(even, -sine, 0.0), jnp.where(even, 0.0, sine)


def normed_heads(wide, gain_ref, tables):
    cosine, sine_even, sine_odd = tables
    width = wide.shape[-1]
    meansq = jnp.sum(wide * wide, axis=-1, keepdims=True) * (1.0 / width)
    inverse = lax.rsqrt(meansq + 1e-06)
    for head in range(width // DH):
        here = slice(head * DH, (head + 1) * DH)
        y = wide[:, here] * inverse * gain_ref[:, here]
        y = y * cosine + pltpu.roll(y, DH - 1, 1) * sine_even + pltpu.roll(y, 1, 1) * sine_odd
        yield head, y.astype(BF16)


def query_kernel(groups, q_hbm, gain_hbm, coords_hbm, *refs):
    videos, tok_rows, width = q_hbm.shape
    outs, tables_ref, refs = refs[:videos], refs[videos], refs[videos + 1 :]
    q_ref, gain_ref, coords_ref, done_ref, sems, out_sems = refs
    own = lax.axis_index("patch") // groups
    copies = [
        pltpu.make_async_copy(source, place, sems.at[i])
        for i, (source, place) in enumerate(
            ((coords_hbm, coords_ref), (q_hbm, q_ref), (gain_hbm, gain_ref))
        )
    ]
    for copy in copies:
        copy.start()
    copies[0].wait()
    tables = rope_tables(coords_ref, tok_rows)
    for i in range(3):
        tables_ref[i] = tables[i]
    copies[1].wait()
    copies[2].wait()
    sends = []
    for s in range(videos):
        for head, y in normed_heads(q_ref[own ^ s].astype(F32), gain_ref, tables):
            done_ref[s, :, head * DH : (head + 1) * DH] = y
        sends.append(pltpu.make_async_copy(done_ref.at[s], outs[s], out_sems.at[s]))
        sends[-1].start()
    for send in sends:
        send.wait()


def key_kernel(k_ref, v_ref, gain_ref, tables_ref, out_ref):
    videos, tok_rows, width = k_ref.shape
    tables = [tables_ref[i] for i in range(3)]
    span = out_ref.shape[2]
    groups = out_ref.shape[0] // videos
    pairs = span // (2 * DH)
    for video in range(videos):
        for head, y in normed_heads(k_ref[video].astype(F32), gain_ref, tables):
            target, start = video * groups + head // pairs, head % pairs * 2 * DH
            out_ref[target, :, start : start + DH] = y
            out_ref[target, :, start + DH : start + 2 * DH] = v_ref[
                video, :, head * DH : (head + 1) * DH
            ]


def softmax_parts(scores):
    top = jnp.max(scores, axis=-1, keepdims=True)
    weights = jnp.exp(scores - top)
    total = jnp.sum(weights, axis=-1, keepdims=True)
    return weights.astype(BF16), 1.0 / total, top + jnp.log(total)


def stacked(refs, lanes):
    rows = [ref[:, lanes].astype(F32) for ref in refs]
    return jnp.concatenate(rows, axis=0).astype(BF16)


def fresh_kernel(groups, videos, *refs):
    queries = refs[:videos]
    fresh_ref, out_ref, log_ref = refs[videos:]
    me = lax.axis_index("patch")
    mine = me % groups
    _, tok_rows, width = out_ref.shape
    span = width // groups
    pairs = span // DH
    rows = videos * tok_rows
    scale = 1.0 / math.sqrt(DH)
    shape = (pairs * rows, rows)
    same = lax.broadcasted_iota(jnp.int32, shape, 0) % rows // tok_rows == (
        lax.broadcasted_iota(jnp.int32, shape, 1) // tok_rows
    )
    lane = lax.broadcasted_iota(jnp.int32, (rows, DH), 1)
    logs = jnp.zeros((rows, DH), F32)
    for t in range(groups):
        lanes = pl.ds(pl.multiple_of((mine ^ t) * span, DH), span)
        query = stacked(queries, lanes)
        fresh = stacked([fresh_ref.at[me ^ (s * groups) ^ t] for s in range(videos)], slice(None))
        scores = jnp.concatenate(
            [
                lax.dot_general(
                    query[:, pair * DH : (pair + 1) * DH],
                    fresh[:, 2 * pair * DH : (2 * pair + 1) * DH],
                    TRANSPOSED,
                    preferred_element_type=F32,
                )
                for pair in range(pairs)
            ],
            axis=0,
        )
        weights, inverse, log = softmax_parts(jnp.where(same, scores * scale, -jnp.inf))
        for pair in range(pairs):
            here = slice(pair * rows, (pair + 1) * rows)
            head = t * pairs + pair
            result = inverse[here] * jnp.dot(
                weights[here],
                fresh[:, (2 * pair + 1) * DH : (2 * pair + 2) * DH],
                preferred_element_type=F32,
            )
            logs = jnp.where(lane == head, log[here], logs)
            for s in range(videos):
                out_ref[s, :, head * DH : (head + 1) * DH] = result[s * tok_rows : (s + 1) * tok_rows]
    for s in range(videos):
        log_ref[s] = logs[s * tok_rows : (s + 1) * tok_rows]


def stale_kernel(groups, videos, *refs):
    queries, pieces, outs = refs[:videos], refs[videos : videos + groups], refs[videos + groups :]
    me = lax.axis_index("patch")
    mine = me % groups
    pairs, total_rows, _ = pieces[0].shape
    tok_rows, width = queries[0].shape
    span = pairs * DH
    rows = videos * tok_rows
    scale = 1.0 / math.sqrt(DH)
    shape = (pairs * rows, total_rows)
    patch = (lax.broadcasted_iota(jnp.int32, shape, 0) % rows // tok_rows * groups) ^ me
    own = patch == lax.broadcasted_iota(jnp.int32, shape, 1) // tok_rows
    lane = lax.broadcasted_iota(jnp.int32, (rows, DH), 1)
    logs = jnp.zeros((rows, DH), F32)
    for t in range(groups):
        start = pl.multiple_of((mine ^ t) * span, DH)
        query = stacked(queries, pl.ds(start, span))
        scores = jnp.concatenate(
            [
                lax.dot_general(
                    query[:, pair * DH : (pair + 1) * DH],
                    pieces[t][pair, :, :DH],
                    TRANSPOSED,
                    preferred_element_type=F32,
                )
                for pair in range(pairs)
            ],
            axis=0,
        )
        weights, inverse, log = softmax_parts(jnp.where(own, -jnp.inf, scores * scale))
        results = []
        for pair in range(pairs):
            here = slice(pair * rows, (pair + 1) * rows)
            results.append(
                inverse[here]
                * jnp.dot(weights[here], pieces[t][pair, :, DH:], preferred_element_type=F32)
            )
            logs = jnp.where(lane == t * pairs + pair, log[here], logs)
        result = jnp.concatenate(results, axis=1).astype(BF16)
        for s in range(videos):
            outs[s][:, t * span : (t + 1) * span] = result[s * tok_rows : (s + 1) * tok_rows]
    high = logs.astype(BF16).astype(F32)
    middle = (logs - high).astype(BF16).astype(F32)
    low = (logs - high - middle).astype(BF16).astype(F32)
    heads = groups * pairs
    terms = (high + pltpu.roll(middle, heads, 1) + pltpu.roll(low, 2 * heads, 1)).astype(BF16)
    for s in range(videos):
        outs[s][:, width:] = terms[s * tok_rows : (s + 1) * tok_rows]


def join_kernel(groups, videos, *refs):
    back = refs[:videos]
    fresh_ref, log_ref, out_ref, done_ref, sems = refs[videos:]
    me = lax.axis_index("patch")
    own, mine = me // groups, me % groups
    _, tok_rows, width = fresh_ref.shape
    heads = width // DH
    pairs = heads // groups
    span = pairs * DH
    copies = []
    for s in range(videos):
        terms = back[s][:, width:].astype(F32)
        stale_log = terms + pltpu.roll(terms, DH - heads, 1) + pltpu.roll(terms, DH - 2 * heads, 1)
        share = 1.0 / (1.0 + jnp.exp(stale_log - log_ref[s]))
        for t in range(groups):
            parts = []
            for pair in range(pairs):
                head = t * pairs + pair
                here = slice(head * DH, (head + 1) * DH)
                stale = back[s][:, here].astype(F32)
                parts.append(stale + share[:, head : head + 1] * (fresh_ref[s, :, here] - stale))
            lanes = pl.ds(pl.multiple_of((mine ^ t) * span, DH), span)
            done_ref[s, :, lanes] = jnp.concatenate(parts, axis=1).astype(BF16)
        copies.append(pltpu.make_async_copy(done_ref.at[s], out_ref.at[own ^ s], sems.at[s]))
        copies[-1].start()
    for copy in copies:
        copy.wait()


def cache_kernel(got_ref, out_ref, sems):
    copies = []
    for pair in range(out_ref.shape[0]):
        lanes = pl.ds(2 * pair * DH, 2 * DH)
        copies.append(
            pltpu.make_async_copy(got_ref.at[:, :, lanes], out_ref.at[pair], sems.at[pair])
        )
        copies[-1].start()
    for copy in copies:
        copy.wait()


def permuted(array, offset, patches):
    return lax.ppermute(array, "patch", [(i, i ^ offset) for i in range(patches)])


def exchange(arrays, stride, patches):
    return [arrays[0]] + [
        permuted(arrays[s], s * stride, patches) for s in range(1, len(arrays))
    ]


def local(queries, keys, values, q_gain, k_gain, stale_cache, coords):
    videos, tok_rows, width = queries.shape
    pairs_here, total_rows, _ = stale_cache.shape
    patches = total_rows // tok_rows
    groups = patches // videos
    rows = jax.ShapeDtypeStruct((tok_rows, width), BF16)

    def kernel(body, name, limit, cost=0, **kwargs):
        return pl.pallas_call(
            body,
            name=name,
            compiler_params=pltpu.CompilerParams(vmem_limit_bytes=limit * MIB),
            cost_estimate=pl.CostEstimate(flops=0, bytes_accessed=cost, transcendentals=0),
            **kwargs,
        )

    *query, tables = kernel(
        functools.partial(query_kernel, groups),
        "query",
        56,
        out_shape=[rows] * videos + [jax.ShapeDtypeStruct((3, tok_rows, DH), F32)],
        in_specs=[HBM] * 3,
        out_specs=[HBM] * videos + [VMEM],
        scratch_shapes=[
            pltpu.VMEM(queries.shape, BF16),
            pltpu.VMEM((1, width), F32),
            pltpu.SMEM(coords.shape, jnp.int32),
            pltpu.VMEM(queries.shape, BF16),
            pltpu.SemaphoreType.DMA((3,)),
            pltpu.SemaphoreType.DMA((videos,)),
        ],
    )(queries, q_gain.reshape(1, width), coords)
    query_got = exchange(query, groups, patches)
    stale_sent, tables = lax.optimization_barrier((stale_cache, tables))
    pieces = {0: stale_cache}
    bit = groups // 2
    pieces[bit] = permuted(stale_sent, bit, patches)
    fresh = kernel(
        key_kernel,
        "key",
        16,
        out_shape=jax.ShapeDtypeStruct((patches, tok_rows, 2 * pairs_here * DH), BF16),
        in_specs=[VMEM] * 4,
        out_specs=VMEM,
    )(keys, values, k_gain.reshape(1, width), tables)
    fresh_sent, query_got = lax.optimization_barrier((fresh, query_got))
    cached = lax.all_to_all(fresh_sent, "patch", split_axis=0, concat_axis=0, tiled=True)
    pieces, query_got = lax.optimization_barrier((pieces, query_got))
    while bit > 1:
        bit //= 2
        pieces.update({t | bit: permuted(piece, bit, patches) for t, piece in list(pieces.items())})
    result = kernel(
        functools.partial(stale_kernel, groups, videos),
        "stale",
        32,
        out_shape=[jax.ShapeDtypeStruct((tok_rows, width + DH), BF16)] * videos,
        in_specs=[VMEM] * (videos + groups),
        out_specs=[VMEM] * videos,
    )(*query_got, *[pieces[t] for t in range(groups)])
    result, fresh_late = lax.optimization_barrier((result, fresh))
    back = exchange(result, groups, patches)
    fresh_sum, fresh_log = kernel(
        functools.partial(fresh_kernel, groups, videos),
        "fresh",
        16,
        out_shape=(
            jax.ShapeDtypeStruct((videos, tok_rows, width), F32),
            jax.ShapeDtypeStruct((videos, tok_rows, DH), F32),
        ),
        in_specs=[VMEM] * (videos + 1),
        out_specs=(VMEM, VMEM),
    )(*query, fresh_late)
    next_cache = kernel(
        cache_kernel,
        "cache",
        16,
        out_shape=jax.ShapeDtypeStruct((pairs_here, patches, tok_rows, 2 * DH), BF16),
        in_specs=[VMEM],
        out_specs=HBM,
        scratch_shapes=[pltpu.SemaphoreType.DMA((pairs_here,))],
    )(cached)
    attended = kernel(
        functools.partial(join_kernel, groups, videos),
        "join",
        16,
        out_shape=jax.ShapeDtypeStruct(queries.shape, BF16),
        in_specs=[VMEM] * (videos + 2),
        out_specs=HBM,
        scratch_shapes=[
            pltpu.VMEM(queries.shape, BF16),
            pltpu.SemaphoreType.DMA((videos,)),
        ],
    )(*back, fresh_sum, fresh_log)
    return (attended, next_cache.reshape(stale_cache.shape))


def solution(mesh):
    in_specs = (
        P("req", "patch", None),
        P("req", "patch", None),
        P("req", "patch", None),
        P(),
        P(),
        P(("req", "patch"), None, None),
        P(None, "patch"),
    )
    out_specs = (P("req", "patch", None), P(("req", "patch"), None, None))
    return jax.shard_map(local, mesh=mesh, in_specs=in_specs, out_specs=out_specs, check_vma=False)
```

```python
import functools
import math

import jax
import jax.numpy as jnp
from jax import lax
from jax.experimental import pallas as pl
from jax.experimental.pallas import tpu as pltpu
from jax.sharding import PartitionSpec as P

DH = 128
VMEM = pl.BlockSpec(memory_space=pltpu.VMEM)
HBM = pl.BlockSpec(memory_space=pltpu.HBM)
SMEM = pl.BlockSpec(memory_space=pltpu.SMEM)
MIB = 1024 * 1024
BF16 = jnp.bfloat16
F32 = jnp.float32
TRANSPOSED = (((1,), (1,)), ((), ()))


def rope_tables(coords_ref, tok_rows):
    half = DH // 2
    side = DH // 6
    first = half - 2 * side
    shape = (tok_rows, DH)
    row = lax.broadcasted_iota(jnp.int32, shape, 0)
    lane = lax.broadcasted_iota(jnp.int32, shape, 1)
    pair = lane // 2
    axis = (pair >= first).astype(jnp.int32) + (pair >= first + side).astype(jnp.int32)
    place = jnp.zeros(shape, jnp.int32)
    for which in range(3):
        for token in range(tok_rows):
            place = jnp.where((axis == which) & (row == token), coords_ref[which, token], place)
    step = jnp.where(axis == 0, pair, jnp.where(axis == 1, pair - first, pair - first - side))
    count = jnp.where(axis == 0, float(first), float(side))
    freq = jnp.exp(step.astype(F32) / count * (-math.log(10000.0)))
    angle = place.astype(F32) * freq
    sine = jnp.sin(angle)
    even = lane % 2 == 0
    return jnp.cos(angle), jnp.where(even, -sine, 0.0), jnp.where(even, 0.0, sine)


def normed_heads(wide, gain_ref, tables):
    cosine, sine_even, sine_odd = tables
    width = wide.shape[-1]
    meansq = jnp.sum(wide * wide, axis=-1, keepdims=True) * (1.0 / width)
    inverse = lax.rsqrt(meansq + 1e-06)
    for head in range(width // DH):
        here = slice(head * DH, (head + 1) * DH)
        y = wide[:, here] * inverse * gain_ref[:, here]
        y = y * cosine + pltpu.roll(y, DH - 1, 1) * sine_even + pltpu.roll(y, 1, 1) * sine_odd
        yield head, y.astype(BF16)


def query_kernel(groups, q_hbm, gain_hbm, coords_hbm, *refs):
    videos, tok_rows, width = q_hbm.shape
    near_hbm, far_hbm, tables_ref, q_ref, gain_ref, coords_ref, done_ref, sems, out_sems = refs
    half = videos // 2
    own = lax.axis_index("patch") // groups
    copies = [
        pltpu.make_async_copy(source, place, sems.at[i])
        for i, (source, place) in enumerate(
            ((coords_hbm, coords_ref), (q_hbm, q_ref), (gain_hbm, gain_ref))
        )
    ]
    for copy in copies:
        copy.start()
    copies[0].wait()
    tables = rope_tables(coords_ref, tok_rows)
    for i in range(3):
        tables_ref[i] = tables[i]
    copies[1].wait()
    copies[2].wait()
    sends = []
    for s in (*range(half, videos), *range(half)):
        for head, y in normed_heads(q_ref[own ^ s].astype(F32), gain_ref, tables):
            done_ref[s, :, head * DH : (head + 1) * DH] = y
        out = far_hbm.at[s - half] if s >= half else near_hbm.at[s]
        sends.append(pltpu.make_async_copy(done_ref.at[s], out, out_sems.at[s]))
        sends[-1].start()
    for send in sends:
        send.wait()


def key_kernel(k_ref, v_ref, gain_ref, tables_ref, out_ref):
    videos, tok_rows, width = k_ref.shape
    tables = [tables_ref[i] for i in range(3)]
    span = out_ref.shape[2]
    groups = out_ref.shape[0] // videos
    pairs = span // (2 * DH)
    for video in range(videos):
        for head, y in normed_heads(k_ref[video].astype(F32), gain_ref, tables):
            target, start = video * groups + head // pairs, head % pairs * 2 * DH
            out_ref[target, :, start : start + DH] = y
            out_ref[target, :, start + DH : start + 2 * DH] = v_ref[
                video, :, head * DH : (head + 1) * DH
            ]


def softmax_parts(scores):
    top = jnp.max(scores, axis=-1, keepdims=True)
    weights = jnp.exp(scores - top)
    total = jnp.sum(weights, axis=-1, keepdims=True)
    return weights.astype(BF16), 1.0 / total, top + jnp.log(total)


def stacked(refs, lanes):
    rows = [ref[:, lanes].astype(F32) for ref in refs]
    return jnp.concatenate(rows, axis=0).astype(BF16)


def fresh_kernel(groups, videos, near_ref, far_ref, fresh_ref, out_ref, log_ref):
    queries = [ref.at[i] for ref in (near_ref, far_ref) for i in range(videos // 2)]
    me = lax.axis_index("patch")
    mine = me % groups
    _, tok_rows, width = out_ref.shape
    span = width // groups
    pairs = span // DH
    rows = videos * tok_rows
    scale = 1.0 / math.sqrt(DH)
    shape = (pairs * rows, rows)
    same = lax.broadcasted_iota(jnp.int32, shape, 0) % rows // tok_rows == (
        lax.broadcasted_iota(jnp.int32, shape, 1) // tok_rows
    )
    lane = lax.broadcasted_iota(jnp.int32, (rows, DH), 1)
    logs = jnp.zeros((rows, DH), F32)
    for t in range(groups):
        lanes = pl.ds(pl.multiple_of((mine ^ t) * span, DH), span)
        query = stacked(queries, lanes)
        fresh = stacked([fresh_ref.at[me ^ (s * groups) ^ t] for s in range(videos)], slice(None))
        scores = jnp.concatenate(
            [
                lax.dot_general(
                    query[:, pair * DH : (pair + 1) * DH],
                    fresh[:, 2 * pair * DH : (2 * pair + 1) * DH],
                    TRANSPOSED,
                    preferred_element_type=F32,
                )
                for pair in range(pairs)
            ],
            axis=0,
        )
        weights, inverse, log = softmax_parts(jnp.where(same, scores * scale, -jnp.inf))
        for pair in range(pairs):
            here = slice(pair * rows, (pair + 1) * rows)
            head = t * pairs + pair
            result = inverse[here] * jnp.dot(
                weights[here],
                fresh[:, (2 * pair + 1) * DH : (2 * pair + 2) * DH],
                preferred_element_type=F32,
            )
            logs = jnp.where(lane == head, log[here], logs)
            for s in range(videos):
                out_ref[s, :, head * DH : (head + 1) * DH] = result[s * tok_rows : (s + 1) * tok_rows]
    for s in range(videos):
        log_ref[s] = logs[s * tok_rows : (s + 1) * tok_rows]


def forward_kernel(near_ref, far_ref, out_ref):
    out_ref[0] = near_ref[1]
    out_ref[1] = far_ref[1]


def stale_kernel(groups, videos, near_ref, far_ref, forward_ref, *refs):
    queries = [near_ref.at[0], forward_ref.at[0], far_ref.at[0], forward_ref.at[1]]
    pieces, outs = refs[:groups], refs[groups:]
    me = lax.axis_index("patch")
    mine = me % groups
    pairs, total_rows, _ = pieces[0].shape
    tok_rows, width = queries[0].shape
    span = pairs * DH
    rows = videos * tok_rows
    scale = 1.0 / math.sqrt(DH)
    shape = (pairs * rows, total_rows)
    patch = (lax.broadcasted_iota(jnp.int32, shape, 0) % rows // tok_rows * groups) ^ me
    own = patch == lax.broadcasted_iota(jnp.int32, shape, 1) // tok_rows
    lane = lax.broadcasted_iota(jnp.int32, (rows, DH), 1)
    logs = jnp.zeros((rows, DH), F32)
    for t in range(groups):
        start = pl.multiple_of((mine ^ t) * span, DH)
        query = stacked(queries, pl.ds(start, span))
        scores = jnp.concatenate(
            [
                lax.dot_general(
                    query[:, pair * DH : (pair + 1) * DH],
                    pieces[t][pair, :, :DH],
                    TRANSPOSED,
                    preferred_element_type=F32,
                )
                for pair in range(pairs)
            ],
            axis=0,
        )
        weights, inverse, log = softmax_parts(jnp.where(own, -jnp.inf, scores * scale))
        results = []
        for pair in range(pairs):
            here = slice(pair * rows, (pair + 1) * rows)
            results.append(
                inverse[here]
                * jnp.dot(weights[here], pieces[t][pair, :, DH:], preferred_element_type=F32)
            )
            logs = jnp.where(lane == t * pairs + pair, log[here], logs)
        result = jnp.concatenate(results, axis=1).astype(BF16)
        for s in range(videos):
            outs[s][:, t * span : (t + 1) * span] = result[s * tok_rows : (s + 1) * tok_rows]
    high = logs.astype(BF16).astype(F32)
    middle = (logs - high).astype(BF16).astype(F32)
    low = (logs - high - middle).astype(BF16).astype(F32)
    heads = groups * pairs
    terms = (high + pltpu.roll(middle, heads, 1) + pltpu.roll(low, 2 * heads, 1)).astype(BF16)
    for s in range(videos):
        outs[s][:, width:] = terms[s * tok_rows : (s + 1) * tok_rows]


def join_kernel(groups, videos, *refs):
    back = refs[:videos]
    fresh_ref, log_ref, out_ref, done_ref, sems = refs[videos:]
    me = lax.axis_index("patch")
    own, mine = me // groups, me % groups
    _, tok_rows, width = fresh_ref.shape
    heads = width // DH
    pairs = heads // groups
    span = pairs * DH
    copies = []
    for s in range(videos):
        terms = back[s][:, width:].astype(F32)
        stale_log = terms + pltpu.roll(terms, DH - heads, 1) + pltpu.roll(terms, DH - 2 * heads, 1)
        share = 1.0 / (1.0 + jnp.exp(stale_log - log_ref[s]))
        for t in range(groups):
            parts = []
            for pair in range(pairs):
                head = t * pairs + pair
                here = slice(head * DH, (head + 1) * DH)
                stale = back[s][:, here].astype(F32)
                parts.append(stale + share[:, head : head + 1] * (fresh_ref[s, :, here] - stale))
            lanes = pl.ds(pl.multiple_of((mine ^ t) * span, DH), span)
            done_ref[s, :, lanes] = jnp.concatenate(parts, axis=1).astype(BF16)
        copies.append(pltpu.make_async_copy(done_ref.at[s], out_ref.at[own ^ s], sems.at[s]))
        copies[-1].start()
    for copy in copies:
        copy.wait()


def cache_kernel(got_ref, out_ref, sems):
    copies = []
    for pair in range(out_ref.shape[0]):
        lanes = pl.ds(2 * pair * DH, 2 * DH)
        copies.append(
            pltpu.make_async_copy(got_ref.at[:, :, lanes], out_ref.at[pair], sems.at[pair])
        )
        copies[-1].start()
    for copy in copies:
        copy.wait()


def permuted(array, offset, patches):
    return lax.ppermute(array, "patch", [(i, i ^ offset) for i in range(patches)])


def exchange(arrays, stride, patches):
    return [arrays[0]] + [
        permuted(arrays[s], s * stride, patches) for s in range(1, len(arrays))
    ]


def local(queries, keys, values, q_gain, k_gain, stale_cache, coords):
    videos, tok_rows, width = queries.shape
    pairs_here, total_rows, _ = stale_cache.shape
    patches = total_rows // tok_rows
    groups = patches // videos

    def kernel(body, name, limit, cost=0, **kwargs):
        return pl.pallas_call(
            body,
            name=name,
            compiler_params=pltpu.CompilerParams(vmem_limit_bytes=limit * MIB),
            cost_estimate=pl.CostEstimate(flops=0, bytes_accessed=cost, transcendentals=0),
            **kwargs,
        )

    half = videos // 2
    block = jax.ShapeDtypeStruct((half, tok_rows, width), BF16)
    near, far, tables = kernel(
        functools.partial(query_kernel, groups),
        "query",
        56,
        out_shape=(block, block, jax.ShapeDtypeStruct((3, tok_rows, DH), F32)),
        in_specs=[HBM] * 3,
        out_specs=(HBM, HBM, VMEM),
        scratch_shapes=[
            pltpu.VMEM(queries.shape, BF16),
            pltpu.VMEM((1, width), F32),
            pltpu.SMEM(coords.shape, jnp.int32),
            pltpu.VMEM(queries.shape, BF16),
            pltpu.SemaphoreType.DMA((3,)),
            pltpu.SemaphoreType.DMA((videos,)),
        ],
    )(queries, q_gain.reshape(1, width), coords)
    far_got = permuted(far, half * groups, patches)
    stale_sent, tables = lax.optimization_barrier((stale_cache, tables))
    pieces = {0: stale_cache}
    bit = groups // 2
    pieces[bit] = permuted(stale_sent, bit, patches)
    fresh = kernel(
        key_kernel,
        "key",
        16,
        out_shape=jax.ShapeDtypeStruct((patches, tok_rows, 2 * pairs_here * DH), BF16),
        in_specs=[VMEM] * 4,
        out_specs=VMEM,
    )(keys, values, k_gain.reshape(1, width), tables)
    fresh_sent, far_got = lax.optimization_barrier((fresh, far_got))
    cached = lax.all_to_all(fresh_sent, "patch", split_axis=0, concat_axis=0, tiled=True)
    forward = kernel(
        forward_kernel,
        "forward",
        16,
        out_shape=jax.ShapeDtypeStruct((2, tok_rows, width), BF16),
        in_specs=[VMEM] * 2,
        out_specs=VMEM,
    )(near, far_got)
    forward_got = permuted(forward, groups, patches)
    pieces, forward_got = lax.optimization_barrier((pieces, forward_got))
    while bit > 1:
        bit //= 2
        pieces.update({t | bit: permuted(piece, bit, patches) for t, piece in list(pieces.items())})
    result = kernel(
        functools.partial(stale_kernel, groups, videos),
        "stale",
        32,
        out_shape=[jax.ShapeDtypeStruct((tok_rows, width + DH), BF16)] * videos,
        in_specs=[VMEM] * (3 + groups),
        out_specs=[VMEM] * videos,
    )(near, far_got, forward_got, *[pieces[t] for t in range(groups)])
    result, fresh_late = lax.optimization_barrier((result, fresh))
    back = exchange(result, groups, patches)
    fresh_sum, fresh_log = kernel(
        functools.partial(fresh_kernel, groups, videos),
        "fresh",
        16,
        out_shape=(
            jax.ShapeDtypeStruct((videos, tok_rows, width), F32),
            jax.ShapeDtypeStruct((videos, tok_rows, DH), F32),
        ),
        in_specs=[VMEM] * 3,
        out_specs=(VMEM, VMEM),
    )(near, far, fresh_late)
    next_cache = kernel(
        cache_kernel,
        "cache",
        16,
        out_shape=jax.ShapeDtypeStruct((pairs_here, patches, tok_rows, 2 * DH), BF16),
        in_specs=[VMEM],
        out_specs=HBM,
        scratch_shapes=[pltpu.SemaphoreType.DMA((pairs_here,))],
    )(cached)
    attended = kernel(
        functools.partial(join_kernel, groups, videos),
        "join",
        16,
        out_shape=jax.ShapeDtypeStruct(queries.shape, BF16),
        in_specs=[VMEM] * (videos + 2),
        out_specs=HBM,
        scratch_shapes=[
            pltpu.VMEM(queries.shape, BF16),
            pltpu.SemaphoreType.DMA((videos,)),
        ],
    )(*back, fresh_sum, fresh_log)
    return (attended, next_cache.reshape(stale_cache.shape))


def solution(mesh):
    in_specs = (
        P("req", "patch", None),
        P("req", "patch", None),
        P("req", "patch", None),
        P(),
        P(),
        P(("req", "patch"), None, None),
        P(None, "patch"),
    )
    out_specs = (P("req", "patch", None), P(("req", "patch"), None, None))
    return jax.shard_map(local, mesh=mesh, in_specs=in_specs, out_specs=out_specs, check_vma=False)
```

```python
import functools
import math

import jax
import jax.numpy as jnp
from jax import lax
from jax.experimental import pallas as pl
from jax.experimental.pallas import tpu as pltpu
from jax.sharding import PartitionSpec as P

DH = 128
VMEM = pl.BlockSpec(memory_space=pltpu.VMEM)
HBM = pl.BlockSpec(memory_space=pltpu.HBM)
SMEM = pl.BlockSpec(memory_space=pltpu.SMEM)
MIB = 1024 * 1024
BF16 = jnp.bfloat16
F32 = jnp.float32
TRANSPOSED = (((1,), (1,)), ((), ()))


def rope_tables(coords_ref, tok_rows):
    half = DH // 2
    side = DH // 6
    first = half - 2 * side
    shape = (tok_rows, DH)
    row = lax.broadcasted_iota(jnp.int32, shape, 0)
    lane = lax.broadcasted_iota(jnp.int32, shape, 1)
    pair = lane // 2
    axis = (pair >= first).astype(jnp.int32) + (pair >= first + side).astype(jnp.int32)
    place = jnp.zeros(shape, jnp.int32)
    for which in range(3):
        for token in range(tok_rows):
            place = jnp.where((axis == which) & (row == token), coords_ref[which, token], place)
    step = jnp.where(axis == 0, pair, jnp.where(axis == 1, pair - first, pair - first - side))
    count = jnp.where(axis == 0, float(first), float(side))
    freq = jnp.exp(step.astype(F32) / count * (-math.log(10000.0)))
    angle = place.astype(F32) * freq
    sine = jnp.sin(angle)
    even = lane % 2 == 0
    return jnp.cos(angle), jnp.where(even, -sine, 0.0), jnp.where(even, 0.0, sine)


def normed_heads(wide, gain_ref, tables):
    cosine, sine_even, sine_odd = tables
    width = wide.shape[-1]
    meansq = jnp.sum(wide * wide, axis=-1, keepdims=True) * (1.0 / width)
    inverse = lax.rsqrt(meansq + 1e-06)
    for head in range(width // DH):
        here = slice(head * DH, (head + 1) * DH)
        y = wide[:, here] * inverse * gain_ref[:, here]
        y = y * cosine + pltpu.roll(y, DH - 1, 1) * sine_even + pltpu.roll(y, 1, 1) * sine_odd
        yield head, y.astype(BF16)


def query_kernel(groups, q_hbm, gain_hbm, coords_hbm, *refs):
    videos, tok_rows, width = q_hbm.shape
    outs, tables_ref, refs = refs[:videos], refs[videos], refs[videos + 1 :]
    q_ref, gain_ref, coords_ref, done_ref, sems, out_sems = refs
    own = lax.axis_index("patch") // groups
    copies = [
        pltpu.make_async_copy(source, place, sems.at[i])
        for i, (source, place) in enumerate(
            ((coords_hbm, coords_ref), (q_hbm, q_ref), (gain_hbm, gain_ref))
        )
    ]
    for copy in copies:
        copy.start()
    copies[0].wait()
    tables = rope_tables(coords_ref, tok_rows)
    for i in range(3):
        tables_ref[i] = tables[i]
    copies[1].wait()
    copies[2].wait()
    sends = []
    for s in range(videos):
        for head, y in normed_heads(q_ref[own ^ s].astype(F32), gain_ref, tables):
            done_ref[s, :, head * DH : (head + 1) * DH] = y
        sends.append(pltpu.make_async_copy(done_ref.at[s], outs[s], out_sems.at[s]))
        sends[-1].start()
    for send in sends:
        send.wait()


def key_kernel(k_ref, v_ref, gain_ref, tables_ref, out_ref):
    videos, tok_rows, width = k_ref.shape
    tables = [tables_ref[i] for i in range(3)]
    span = out_ref.shape[2]
    groups = out_ref.shape[0] // videos
    pairs = span // (2 * DH)
    for video in range(videos):
        for head, y in normed_heads(k_ref[video].astype(F32), gain_ref, tables):
            target, start = video * groups + head // pairs, head % pairs * 2 * DH
            out_ref[target, :, start : start + DH] = y
            out_ref[target, :, start + DH : start + 2 * DH] = v_ref[
                video, :, head * DH : (head + 1) * DH
            ]


def softmax_parts(scores):
    top = jnp.max(scores, axis=-1, keepdims=True)
    weights = jnp.exp(scores - top)
    total = jnp.sum(weights, axis=-1, keepdims=True)
    return weights.astype(BF16), 1.0 / total, top + jnp.log(total)


def stacked(refs, lanes):
    rows = [ref[:, lanes].astype(F32) for ref in refs]
    return jnp.concatenate(rows, axis=0).astype(BF16)


def fresh_kernel(groups, videos, *refs):
    queries = refs[:videos]
    fresh_ref, out_ref, log_ref = refs[videos:]
    me = lax.axis_index("patch")
    mine = me % groups
    _, tok_rows, width = out_ref.shape
    span = width // groups
    pairs = span // DH
    rows = videos * tok_rows
    scale = 1.0 / math.sqrt(DH)
    shape = (pairs * rows, rows)
    same = lax.broadcasted_iota(jnp.int32, shape, 0) % rows // tok_rows == (
        lax.broadcasted_iota(jnp.int32, shape, 1) // tok_rows
    )
    lane = lax.broadcasted_iota(jnp.int32, (rows, DH), 1)
    logs = jnp.zeros((rows, DH), F32)
    for t in range(groups):
        lanes = pl.ds(pl.multiple_of((mine ^ t) * span, DH), span)
        query = stacked(queries, lanes)
        fresh = stacked([fresh_ref.at[me ^ (s * groups) ^ t] for s in range(videos)], slice(None))
        scores = jnp.concatenate(
            [
                lax.dot_general(
                    query[:, pair * DH : (pair + 1) * DH],
                    fresh[:, 2 * pair * DH : (2 * pair + 1) * DH],
                    TRANSPOSED,
                    preferred_element_type=F32,
                )
                for pair in range(pairs)
            ],
            axis=0,
        )
        weights, inverse, log = softmax_parts(jnp.where(same, scores * scale, -jnp.inf))
        for pair in range(pairs):
            here = slice(pair * rows, (pair + 1) * rows)
            head = t * pairs + pair
            result = inverse[here] * jnp.dot(
                weights[here],
                fresh[:, (2 * pair + 1) * DH : (2 * pair + 2) * DH],
                preferred_element_type=F32,
            )
            logs = jnp.where(lane == head, log[here], logs)
            for s in range(videos):
                out_ref[s, :, head * DH : (head + 1) * DH] = result[s * tok_rows : (s + 1) * tok_rows]
    for s in range(videos):
        log_ref[s] = logs[s * tok_rows : (s + 1) * tok_rows]


def stale_kernel(groups, videos, *refs):
    queries, pieces, outs = refs[:videos], refs[videos : videos + groups], refs[videos + groups :]
    me = lax.axis_index("patch")
    mine = me % groups
    pairs, total_rows, _ = pieces[0].shape
    tok_rows, width = queries[0].shape
    span = pairs * DH
    rows = videos * tok_rows
    scale = 1.0 / math.sqrt(DH)
    shape = (pairs * rows, total_rows)
    patch = (lax.broadcasted_iota(jnp.int32, shape, 0) % rows // tok_rows * groups) ^ me
    own = patch == lax.broadcasted_iota(jnp.int32, shape, 1) // tok_rows
    lane = lax.broadcasted_iota(jnp.int32, (rows, DH), 1)
    logs = jnp.zeros((rows, DH), F32)
    for t in range(groups):
        start = pl.multiple_of((mine ^ t) * span, DH)
        query = stacked(queries, pl.ds(start, span))
        scores = jnp.concatenate(
            [
                lax.dot_general(
                    query[:, pair * DH : (pair + 1) * DH],
                    pieces[t][pair, :, :DH],
                    TRANSPOSED,
                    preferred_element_type=F32,
                )
                for pair in range(pairs)
            ],
            axis=0,
        )
        weights, inverse, log = softmax_parts(jnp.where(own, -jnp.inf, scores * scale))
        results = []
        for pair in range(pairs):
            here = slice(pair * rows, (pair + 1) * rows)
            results.append(
                inverse[here]
                * jnp.dot(weights[here], pieces[t][pair, :, DH:], preferred_element_type=F32)
            )
            logs = jnp.where(lane == t * pairs + pair, log[here], logs)
        result = jnp.concatenate(results, axis=1).astype(BF16)
        for s in range(videos):
            outs[s][:, t * span : (t + 1) * span] = result[s * tok_rows : (s + 1) * tok_rows]
    high = logs.astype(BF16).astype(F32)
    middle = (logs - high).astype(BF16).astype(F32)
    low = (logs - high - middle).astype(BF16).astype(F32)
    heads = groups * pairs
    terms = (high + pltpu.roll(middle, heads, 1) + pltpu.roll(low, 2 * heads, 1)).astype(BF16)
    for s in range(videos):
        outs[s][:, width:] = terms[s * tok_rows : (s + 1) * tok_rows]


def join_kernel(groups, videos, *refs):
    back = refs[:videos]
    fresh_ref, log_ref, out_ref, done_ref, sems = refs[videos:]
    me = lax.axis_index("patch")
    own, mine = me // groups, me % groups
    _, tok_rows, width = fresh_ref.shape
    heads = width // DH
    pairs = heads // groups
    span = pairs * DH
    copies = []
    for s in range(videos):
        terms = back[s][:, width:].astype(F32)
        stale_log = terms + pltpu.roll(terms, DH - heads, 1) + pltpu.roll(terms, DH - 2 * heads, 1)
        share = 1.0 / (1.0 + jnp.exp(stale_log - log_ref[s]))
        for t in range(groups):
            parts = []
            for pair in range(pairs):
                head = t * pairs + pair
                here = slice(head * DH, (head + 1) * DH)
                stale = back[s][:, here].astype(F32)
                parts.append(stale + share[:, head : head + 1] * (fresh_ref[s, :, here] - stale))
            lanes = pl.ds(pl.multiple_of((mine ^ t) * span, DH), span)
            done_ref[s, :, lanes] = jnp.concatenate(parts, axis=1).astype(BF16)
        copies.append(pltpu.make_async_copy(done_ref.at[s], out_ref.at[own ^ s], sems.at[s]))
        copies[-1].start()
    for copy in copies:
        copy.wait()


def cache_kernel(got_ref, out_ref, sems):
    copies = []
    for pair in range(out_ref.shape[0]):
        lanes = pl.ds(2 * pair * DH, 2 * DH)
        copies.append(
            pltpu.make_async_copy(got_ref.at[:, :, lanes], out_ref.at[pair], sems.at[pair])
        )
        copies[-1].start()
    for copy in copies:
        copy.wait()


def permuted(array, offset, patches):
    return lax.ppermute(array, "patch", [(i, i ^ offset) for i in range(patches)])


def exchange(arrays, stride, patches):
    half = len(arrays) // 2
    got = {0: arrays[0]}
    for s in (*range(half, 2 * half), *range(1, half)):
        got[s] = permuted(arrays[s], s * stride, patches)
    return [got[s] for s in range(2 * half)]


def local(queries, keys, values, q_gain, k_gain, stale_cache, coords):
    videos, tok_rows, width = queries.shape
    pairs_here, total_rows, _ = stale_cache.shape
    patches = total_rows // tok_rows
    groups = patches // videos
    rows = jax.ShapeDtypeStruct((tok_rows, width), BF16)

    def kernel(body, name, limit, cost=0, **kwargs):
        return pl.pallas_call(
            body,
            name=name,
            compiler_params=pltpu.CompilerParams(vmem_limit_bytes=limit * MIB),
            cost_estimate=pl.CostEstimate(flops=0, bytes_accessed=cost, transcendentals=0),
            **kwargs,
        )

    *query, tables = kernel(
        functools.partial(query_kernel, groups),
        "query",
        56,
        out_shape=[rows] * videos + [jax.ShapeDtypeStruct((3, tok_rows, DH), F32)],
        in_specs=[HBM] * 3,
        out_specs=[HBM] * videos + [VMEM],
        scratch_shapes=[
            pltpu.VMEM(queries.shape, BF16),
            pltpu.VMEM((1, width), F32),
            pltpu.SMEM(coords.shape, jnp.int32),
            pltpu.VMEM(queries.shape, BF16),
            pltpu.SemaphoreType.DMA((3,)),
            pltpu.SemaphoreType.DMA((videos,)),
        ],
    )(queries, q_gain.reshape(1, width), coords)
    query_got = exchange(query, groups, patches)
    stale_sent, tables = lax.optimization_barrier((stale_cache, tables))
    pieces = {0: stale_cache}
    bit = groups // 2
    pieces[bit] = permuted(stale_sent, bit, patches)
    fresh = kernel(
        key_kernel,
        "key",
        16,
        out_shape=jax.ShapeDtypeStruct((patches, tok_rows, 2 * pairs_here * DH), BF16),
        in_specs=[VMEM] * 4,
        out_specs=VMEM,
    )(keys, values, k_gain.reshape(1, width), tables)
    fresh_sent, query_got = lax.optimization_barrier((fresh, query_got))
    cached = lax.all_to_all(fresh_sent, "patch", split_axis=0, concat_axis=0, tiled=True)
    pieces, query_got = lax.optimization_barrier((pieces, query_got))
    while bit > 1:
        bit //= 2
        pieces.update({t | bit: permuted(piece, bit, patches) for t, piece in list(pieces.items())})
    result = kernel(
        functools.partial(stale_kernel, groups, videos),
        "stale",
        32,
        out_shape=[jax.ShapeDtypeStruct((tok_rows, width + DH), BF16)] * videos,
        in_specs=[VMEM] * (videos + groups),
        out_specs=[VMEM] * videos,
    )(*query_got, *[pieces[t] for t in range(groups)])
    result, fresh_late = lax.optimization_barrier((result, fresh))
    back = exchange(result, groups, patches)
    fresh_sum, fresh_log = kernel(
        functools.partial(fresh_kernel, groups, videos),
        "fresh",
        16,
        out_shape=(
            jax.ShapeDtypeStruct((videos, tok_rows, width), F32),
            jax.ShapeDtypeStruct((videos, tok_rows, DH), F32),
        ),
        in_specs=[VMEM] * (videos + 1),
        out_specs=(VMEM, VMEM),
    )(*query, fresh_late)
    next_cache = kernel(
        cache_kernel,
        "cache",
        16,
        out_shape=jax.ShapeDtypeStruct((pairs_here, patches, tok_rows, 2 * DH), BF16),
        in_specs=[VMEM],
        out_specs=HBM,
        scratch_shapes=[pltpu.SemaphoreType.DMA((pairs_here,))],
    )(cached)
    attended = kernel(
        functools.partial(join_kernel, groups, videos),
        "join",
        16,
        out_shape=jax.ShapeDtypeStruct(queries.shape, BF16),
        in_specs=[VMEM] * (videos + 2),
        out_specs=HBM,
        scratch_shapes=[
            pltpu.VMEM(queries.shape, BF16),
            pltpu.SemaphoreType.DMA((videos,)),
        ],
    )(*back, fresh_sum, fresh_log)
    return (attended, next_cache.reshape(stale_cache.shape))


def solution(mesh):
    in_specs = (
        P("req", "patch", None),
        P("req", "patch", None),
        P("req", "patch", None),
        P(),
        P(),
        P(("req", "patch"), None, None),
        P(None, "patch"),
    )
    out_specs = (P("req", "patch", None), P(("req", "patch"), None, None))
    return jax.shard_map(local, mesh=mesh, in_specs=in_specs, out_specs=out_specs, check_vma=False)
```

```python
import functools
import math

import jax
import jax.numpy as jnp
from jax import lax
from jax.experimental import pallas as pl
from jax.experimental.pallas import tpu as pltpu
from jax.sharding import PartitionSpec as P

DH = 128
VMEM = pl.BlockSpec(memory_space=pltpu.VMEM)
HBM = pl.BlockSpec(memory_space=pltpu.HBM)
SMEM = pl.BlockSpec(memory_space=pltpu.SMEM)
MIB = 1024 * 1024
BF16 = jnp.bfloat16
F32 = jnp.float32
TRANSPOSED = (((1,), (1,)), ((), ()))


def rope_tables(coords_ref, tok_rows):
    half = DH // 2
    side = DH // 6
    first = half - 2 * side
    shape = (tok_rows, DH)
    row = lax.broadcasted_iota(jnp.int32, shape, 0)
    lane = lax.broadcasted_iota(jnp.int32, shape, 1)
    pair = lane // 2
    axis = (pair >= first).astype(jnp.int32) + (pair >= first + side).astype(jnp.int32)
    place = jnp.zeros(shape, jnp.int32)
    for which in range(3):
        for token in range(tok_rows):
            place = jnp.where((axis == which) & (row == token), coords_ref[which, token], place)
    step = jnp.where(axis == 0, pair, jnp.where(axis == 1, pair - first, pair - first - side))
    count = jnp.where(axis == 0, float(first), float(side))
    freq = jnp.exp(step.astype(F32) / count * (-math.log(10000.0)))
    angle = place.astype(F32) * freq
    sine = jnp.sin(angle)
    even = lane % 2 == 0
    return jnp.cos(angle), jnp.where(even, -sine, 0.0), jnp.where(even, 0.0, sine)


def normed_heads(wide, gain_ref, tables):
    cosine, sine_even, sine_odd = tables
    width = wide.shape[-1]
    meansq = jnp.sum(wide * wide, axis=-1, keepdims=True) * (1.0 / width)
    inverse = lax.rsqrt(meansq + 1e-06)
    for head in range(width // DH):
        here = slice(head * DH, (head + 1) * DH)
        y = wide[:, here] * inverse * gain_ref[:, here]
        y = y * cosine + pltpu.roll(y, DH - 1, 1) * sine_even + pltpu.roll(y, 1, 1) * sine_odd
        yield head, y.astype(BF16)


def query_kernel(groups, q_hbm, gain_hbm, coords_hbm, *refs):
    videos, tok_rows, width = q_hbm.shape
    outs, tables_ref, refs = refs[:videos], refs[videos], refs[videos + 1 :]
    q_ref, gain_ref, coords_ref, done_ref, sems, out_sems = refs
    own = lax.axis_index("patch") // groups
    copies = [
        pltpu.make_async_copy(source, place, sems.at[i])
        for i, (source, place) in enumerate(
            ((coords_hbm, coords_ref), (q_hbm, q_ref), (gain_hbm, gain_ref))
        )
    ]
    for copy in copies:
        copy.start()
    copies[0].wait()
    tables = rope_tables(coords_ref, tok_rows)
    for i in range(3):
        tables_ref[i] = tables[i]
    copies[1].wait()
    copies[2].wait()
    sends = []
    for s in range(videos):
        for head, y in normed_heads(q_ref[own ^ s].astype(F32), gain_ref, tables):
            done_ref[s, :, head * DH : (head + 1) * DH] = y
        sends.append(pltpu.make_async_copy(done_ref.at[s], outs[s], out_sems.at[s]))
        sends[-1].start()
    for send in sends:
        send.wait()


def key_kernel(k_ref, v_ref, gain_ref, tables_ref, out_ref):
    videos, tok_rows, width = k_ref.shape
    tables = [tables_ref[i] for i in range(3)]
    span = out_ref.shape[2]
    groups = out_ref.shape[0] // videos
    pairs = span // (2 * DH)
    for video in range(videos):
        for head, y in normed_heads(k_ref[video].astype(F32), gain_ref, tables):
            target, start = video * groups + head // pairs, head % pairs * 2 * DH
            out_ref[target, :, start : start + DH] = y
            out_ref[target, :, start + DH : start + 2 * DH] = v_ref[
                video, :, head * DH : (head + 1) * DH
            ]


def softmax_parts(scores):
    top = jnp.max(scores, axis=-1, keepdims=True)
    weights = jnp.exp(scores - top)
    total = jnp.sum(weights, axis=-1, keepdims=True)
    return weights.astype(BF16), 1.0 / total, top + jnp.log(total)


def stacked(refs, lanes):
    rows = [ref[:, lanes].astype(F32) for ref in refs]
    return jnp.concatenate(rows, axis=0).astype(BF16)


def fresh_kernel(groups, videos, *refs):
    queries = refs[:videos]
    fresh_ref, out_ref, log_ref = refs[videos:]
    me = lax.axis_index("patch")
    mine = me % groups
    _, tok_rows, width = out_ref.shape
    span = width // groups
    pairs = span // DH
    rows = videos * tok_rows
    scale = 1.0 / math.sqrt(DH)
    shape = (pairs * rows, rows)
    same = lax.broadcasted_iota(jnp.int32, shape, 0) % rows // tok_rows == (
        lax.broadcasted_iota(jnp.int32, shape, 1) // tok_rows
    )
    lane = lax.broadcasted_iota(jnp.int32, (rows, DH), 1)
    logs = jnp.zeros((rows, DH), F32)
    for t in range(groups):
        lanes = pl.ds(pl.multiple_of((mine ^ t) * span, DH), span)
        query = stacked(queries, lanes)
        fresh = stacked([fresh_ref.at[me ^ (s * groups) ^ t] for s in range(videos)], slice(None))
        scores = jnp.concatenate(
            [
                lax.dot_general(
                    query[:, pair * DH : (pair + 1) * DH],
                    fresh[:, 2 * pair * DH : (2 * pair + 1) * DH],
                    TRANSPOSED,
                    preferred_element_type=F32,
                )
                for pair in range(pairs)
            ],
            axis=0,
        )
        weights, inverse, log = softmax_parts(jnp.where(same, scores * scale, -jnp.inf))
        for pair in range(pairs):
            here = slice(pair * rows, (pair + 1) * rows)
            head = t * pairs + pair
            result = inverse[here] * jnp.dot(
                weights[here],
                fresh[:, (2 * pair + 1) * DH : (2 * pair + 2) * DH],
                preferred_element_type=F32,
            )
            logs = jnp.where(lane == head, log[here], logs)
            for s in range(videos):
                out_ref[s, :, head * DH : (head + 1) * DH] = result[s * tok_rows : (s + 1) * tok_rows]
    for s in range(videos):
        log_ref[s] = logs[s * tok_rows : (s + 1) * tok_rows]


def stale_kernel(groups, videos, *refs):
    queries, pieces, outs = in_order(refs[:videos]), refs[videos : videos + groups], refs[videos + groups :]
    me = lax.axis_index("patch")
    mine = me % groups
    pairs, total_rows, _ = pieces[0].shape
    tok_rows, width = queries[0].shape
    span = pairs * DH
    rows = videos * tok_rows
    scale = 1.0 / math.sqrt(DH)
    shape = (pairs * rows, total_rows)
    patch = (lax.broadcasted_iota(jnp.int32, shape, 0) % rows // tok_rows * groups) ^ me
    own = patch == lax.broadcasted_iota(jnp.int32, shape, 1) // tok_rows
    lane = lax.broadcasted_iota(jnp.int32, (rows, DH), 1)
    logs = jnp.zeros((rows, DH), F32)
    for t in range(groups):
        start = pl.multiple_of((mine ^ t) * span, DH)
        query = stacked(queries, pl.ds(start, span))
        scores = jnp.concatenate(
            [
                lax.dot_general(
                    query[:, pair * DH : (pair + 1) * DH],
                    pieces[t][pair, :, :DH],
                    TRANSPOSED,
                    preferred_element_type=F32,
                )
                for pair in range(pairs)
            ],
            axis=0,
        )
        weights, inverse, log = softmax_parts(jnp.where(own, -jnp.inf, scores * scale))
        results = []
        for pair in range(pairs):
            here = slice(pair * rows, (pair + 1) * rows)
            results.append(
                inverse[here]
                * jnp.dot(weights[here], pieces[t][pair, :, DH:], preferred_element_type=F32)
            )
            logs = jnp.where(lane == t * pairs + pair, log[here], logs)
        result = jnp.concatenate(results, axis=1).astype(BF16)
        for s in range(videos):
            outs[s][:, t * span : (t + 1) * span] = result[s * tok_rows : (s + 1) * tok_rows]
    high = logs.astype(BF16).astype(F32)
    middle = (logs - high).astype(BF16).astype(F32)
    low = (logs - high - middle).astype(BF16).astype(F32)
    heads = groups * pairs
    terms = (high + pltpu.roll(middle, heads, 1) + pltpu.roll(low, 2 * heads, 1)).astype(BF16)
    for s in range(videos):
        outs[s][:, width:] = terms[s * tok_rows : (s + 1) * tok_rows]


def join_kernel(groups, videos, *refs):
    back = in_order(refs[:videos])
    fresh_ref, log_ref, out_ref, done_ref, sems = refs[videos:]
    me = lax.axis_index("patch")
    own, mine = me // groups, me % groups
    _, tok_rows, width = fresh_ref.shape
    heads = width // DH
    pairs = heads // groups
    span = pairs * DH
    copies = []
    for s in range(videos):
        terms = back[s][:, width:].astype(F32)
        stale_log = terms + pltpu.roll(terms, DH - heads, 1) + pltpu.roll(terms, DH - 2 * heads, 1)
        share = 1.0 / (1.0 + jnp.exp(stale_log - log_ref[s]))
        for t in range(groups):
            parts = []
            for pair in range(pairs):
                head = t * pairs + pair
                here = slice(head * DH, (head + 1) * DH)
                stale = back[s][:, here].astype(F32)
                parts.append(stale + share[:, head : head + 1] * (fresh_ref[s, :, here] - stale))
            lanes = pl.ds(pl.multiple_of((mine ^ t) * span, DH), span)
            done_ref[s, :, lanes] = jnp.concatenate(parts, axis=1).astype(BF16)
        copies.append(pltpu.make_async_copy(done_ref.at[s], out_ref.at[own ^ s], sems.at[s]))
        copies[-1].start()
    for copy in copies:
        copy.wait()


def cache_kernel(got_ref, out_ref, sems):
    copies = []
    for pair in range(out_ref.shape[0]):
        lanes = pl.ds(2 * pair * DH, 2 * DH)
        copies.append(
            pltpu.make_async_copy(got_ref.at[:, :, lanes], out_ref.at[pair], sems.at[pair])
        )
        copies[-1].start()
    for copy in copies:
        copy.wait()


def permuted(array, offset, patches):
    return lax.ppermute(array, "patch", [(i, i ^ offset) for i in range(patches)])


def far_first(arrays):
    half = len(arrays) // 2
    return [*arrays[half:], *arrays[1:half], arrays[0]]


def in_order(arrays):
    half = len(arrays) // 2
    return [arrays[-1], *arrays[half:-1], *arrays[:half]]


def exchange(arrays, stride, patches):
    return [arrays[0]] + [
        permuted(arrays[s], s * stride, patches) for s in range(1, len(arrays))
    ]


def local(queries, keys, values, q_gain, k_gain, stale_cache, coords):
    videos, tok_rows, width = queries.shape
    pairs_here, total_rows, _ = stale_cache.shape
    patches = total_rows // tok_rows
    groups = patches // videos
    rows = jax.ShapeDtypeStruct((tok_rows, width), BF16)

    def kernel(body, name, limit, cost=0, **kwargs):
        return pl.pallas_call(
            body,
            name=name,
            compiler_params=pltpu.CompilerParams(vmem_limit_bytes=limit * MIB),
            cost_estimate=pl.CostEstimate(flops=0, bytes_accessed=cost, transcendentals=0),
            **kwargs,
        )

    *query, tables = kernel(
        functools.partial(query_kernel, groups),
        "query",
        56,
        out_shape=[rows] * videos + [jax.ShapeDtypeStruct((3, tok_rows, DH), F32)],
        in_specs=[HBM] * 3,
        out_specs=[HBM] * videos + [VMEM],
        scratch_shapes=[
            pltpu.VMEM(queries.shape, BF16),
            pltpu.VMEM((1, width), F32),
            pltpu.SMEM(coords.shape, jnp.int32),
            pltpu.VMEM(queries.shape, BF16),
            pltpu.SemaphoreType.DMA((3,)),
            pltpu.SemaphoreType.DMA((videos,)),
        ],
    )(queries, q_gain.reshape(1, width), coords)
    query_got = far_first(exchange(query, groups, patches))
    stale_sent, tables = lax.optimization_barrier((stale_cache, tables))
    pieces = {0: stale_cache}
    bit = groups // 2
    pieces[bit] = permuted(stale_sent, bit, patches)
    fresh = kernel(
        key_kernel,
        "key",
        16,
        out_shape=jax.ShapeDtypeStruct((patches, tok_rows, 2 * pairs_here * DH), BF16),
        in_specs=[VMEM] * 4,
        out_specs=VMEM,
    )(keys, values, k_gain.reshape(1, width), tables)
    fresh_sent, query_got = lax.optimization_barrier((fresh, query_got))
    cached = lax.all_to_all(fresh_sent, "patch", split_axis=0, concat_axis=0, tiled=True)
    pieces, query_got = lax.optimization_barrier((pieces, query_got))
    while bit > 1:
        bit //= 2
        pieces.update({t | bit: permuted(piece, bit, patches) for t, piece in list(pieces.items())})
    result = kernel(
        functools.partial(stale_kernel, groups, videos),
        "stale",
        32,
        out_shape=[jax.ShapeDtypeStruct((tok_rows, width + DH), BF16)] * videos,
        in_specs=[VMEM] * (videos + groups),
        out_specs=[VMEM] * videos,
    )(*query_got, *[pieces[t] for t in range(groups)])
    result, fresh_late = lax.optimization_barrier((result, fresh))
    back = far_first(exchange(result, groups, patches))
    fresh_sum, fresh_log = kernel(
        functools.partial(fresh_kernel, groups, videos),
        "fresh",
        16,
        out_shape=(
            jax.ShapeDtypeStruct((videos, tok_rows, width), F32),
            jax.ShapeDtypeStruct((videos, tok_rows, DH), F32),
        ),
        in_specs=[VMEM] * (videos + 1),
        out_specs=(VMEM, VMEM),
    )(*query, fresh_late)
    next_cache = kernel(
        cache_kernel,
        "cache",
        16,
        out_shape=jax.ShapeDtypeStruct((pairs_here, patches, tok_rows, 2 * DH), BF16),
        in_specs=[VMEM],
        out_specs=HBM,
        scratch_shapes=[pltpu.SemaphoreType.DMA((pairs_here,))],
    )(cached)
    attended = kernel(
        functools.partial(join_kernel, groups, videos),
        "join",
        16,
        out_shape=jax.ShapeDtypeStruct(queries.shape, BF16),
        in_specs=[VMEM] * (videos + 2),
        out_specs=HBM,
        scratch_shapes=[
            pltpu.VMEM(queries.shape, BF16),
            pltpu.SemaphoreType.DMA((videos,)),
        ],
    )(*back, fresh_sum, fresh_log)
    return (attended, next_cache.reshape(stale_cache.shape))


def solution(mesh):
    in_specs = (
        P("req", "patch", None),
        P("req", "patch", None),
        P("req", "patch", None),
        P(),
        P(),
        P(("req", "patch"), None, None),
        P(None, "patch"),
    )
    out_specs = (P("req", "patch", None), P(("req", "patch"), None, None))
    return jax.shard_map(local, mesh=mesh, in_specs=in_specs, out_specs=out_specs, check_vma=False)
```

```python
import functools
import math

import jax
import jax.numpy as jnp
from jax import lax
from jax.experimental import pallas as pl
from jax.experimental.pallas import tpu as pltpu
from jax.sharding import PartitionSpec as P

DH = 128
VMEM = pl.BlockSpec(memory_space=pltpu.VMEM)
HBM = pl.BlockSpec(memory_space=pltpu.HBM)
SMEM = pl.BlockSpec(memory_space=pltpu.SMEM)
MIB = 1024 * 1024
BF16 = jnp.bfloat16
F32 = jnp.float32
TRANSPOSED = (((1,), (1,)), ((), ()))


def rope_tables(coords, tok_rows):
    half = DH // 2
    side = DH // 6
    first = half - 2 * side
    shape = (len(coords) * tok_rows, DH)
    row = lax.broadcasted_iota(jnp.int32, shape, 0)
    lane = lax.broadcasted_iota(jnp.int32, shape, 1)
    pair = lane // 2
    axis = (pair >= first).astype(jnp.int32) + (pair >= first + side).astype(jnp.int32)
    places = []
    for ref in coords:
        place = jnp.zeros((tok_rows, DH), jnp.int32)
        for which in range(3):
            for token in range(tok_rows):
                here = (axis[:tok_rows] == which) & (row[:tok_rows] == token)
                place = jnp.where(here, ref[which, token], place)
        places.append(place)
    place = jnp.concatenate(places, axis=0)
    step = jnp.where(axis == 0, pair, jnp.where(axis == 1, pair - first, pair - first - side))
    count = jnp.where(axis == 0, float(first), float(side))
    freq = jnp.exp(step.astype(F32) / count * (-math.log(10000.0)))
    angle = place.astype(F32) * freq
    sine = jnp.sin(angle)
    even = lane % 2 == 0
    return jnp.cos(angle), jnp.where(even, -sine, 0.0), jnp.where(even, 0.0, sine)


def normed_heads(wide, gain_ref, tables):
    cosine, sine_even, sine_odd = tables
    width = wide.shape[-1]
    meansq = jnp.sum(wide * wide, axis=-1, keepdims=True) * (1.0 / width)
    inverse = lax.rsqrt(meansq + 1e-06)
    for head in range(width // DH):
        here = slice(head * DH, (head + 1) * DH)
        y = wide[:, here] * inverse * gain_ref[:, here]
        y = y * cosine + pltpu.roll(y, DH - 1, 1) * sine_even + pltpu.roll(y, 1, 1) * sine_odd
        yield head, y.astype(BF16)


def own_kernel(q_ref, k_ref, v_ref, q_gain_ref, k_gain_ref, coords_ref, query_ref, fresh_ref):
    videos, tok_rows, width = k_ref.shape
    tables = rope_tables([coords_ref], tok_rows)
    span = fresh_ref.shape[2]
    groups = fresh_ref.shape[0] // videos
    pairs = span // (2 * DH)
    for video in range(videos):
        for head, y in normed_heads(k_ref[video].astype(F32), k_gain_ref, tables):
            target, start = video * groups + head // pairs, head % pairs * 2 * DH
            fresh_ref[target, :, start : start + DH] = y
            fresh_ref[target, :, start + DH : start + 2 * DH] = v_ref[
                video, :, head * DH : (head + 1) * DH
            ]
    for video in range(videos):
        for head, y in normed_heads(q_ref[video].astype(F32), q_gain_ref, tables):
            query_ref[video, :, head * DH : (head + 1) * DH] = y


def turn_kernel(groups, q_ref, gain_ref, *refs):
    coords, out_ref = refs[:-1], refs[-1]
    videos, tok_rows, _ = q_ref.shape
    own = lax.axis_index("patch") // groups
    tables = rope_tables(coords, tok_rows)
    for s in range(videos):
        mine = [table[s * tok_rows : (s + 1) * tok_rows] for table in tables]
        for head, y in normed_heads(q_ref[own ^ s].astype(F32), gain_ref, mine):
            out_ref[s, :, head * DH : (head + 1) * DH] = y


def softmax_parts(scores):
    top = jnp.max(scores, axis=-1, keepdims=True)
    weights = jnp.exp(scores - top)
    total = jnp.sum(weights, axis=-1, keepdims=True)
    return weights.astype(BF16), 1.0 / total, top + jnp.log(total)


def stacked(refs, lanes):
    rows = [ref[:, lanes].astype(F32) for ref in refs]
    return jnp.concatenate(rows, axis=0).astype(BF16)


def fresh_kernel(groups, videos, query_ref, fresh_ref, out_ref, log_ref):
    me = lax.axis_index("patch")
    own, mine = me // groups, me % groups
    queries = [query_ref.at[own ^ s] for s in range(videos)]
    _, tok_rows, width = out_ref.shape
    span = width // groups
    pairs = span // DH
    rows = videos * tok_rows
    scale = 1.0 / math.sqrt(DH)
    shape = (pairs * rows, rows)
    same = lax.broadcasted_iota(jnp.int32, shape, 0) % rows // tok_rows == (
        lax.broadcasted_iota(jnp.int32, shape, 1) // tok_rows
    )
    lane = lax.broadcasted_iota(jnp.int32, (rows, DH), 1)
    logs = jnp.zeros((rows, DH), F32)
    for t in range(groups):
        lanes = pl.ds(pl.multiple_of((mine ^ t) * span, DH), span)
        query = stacked(queries, lanes)
        fresh = stacked([fresh_ref.at[me ^ (s * groups) ^ t] for s in range(videos)], slice(None))
        scores = jnp.concatenate(
            [
                lax.dot_general(
                    query[:, pair * DH : (pair + 1) * DH],
                    fresh[:, 2 * pair * DH : (2 * pair + 1) * DH],
                    TRANSPOSED,
                    preferred_element_type=F32,
                )
                for pair in range(pairs)
            ],
            axis=0,
        )
        weights, inverse, log = softmax_parts(jnp.where(same, scores * scale, -jnp.inf))
        for pair in range(pairs):
            here = slice(pair * rows, (pair + 1) * rows)
            head = t * pairs + pair
            result = inverse[here] * jnp.dot(
                weights[here],
                fresh[:, (2 * pair + 1) * DH : (2 * pair + 2) * DH],
                preferred_element_type=F32,
            )
            logs = jnp.where(lane == head, log[here], logs)
            for s in range(videos):
                out_ref[s, :, head * DH : (head + 1) * DH] = result[s * tok_rows : (s + 1) * tok_rows]
    for s in range(videos):
        log_ref[s] = logs[s * tok_rows : (s + 1) * tok_rows]


def stale_kernel(groups, videos, query_ref, *refs):
    queries = [query_ref.at[s] for s in range(videos)]
    pieces, outs = refs[:groups], refs[groups:]
    me = lax.axis_index("patch")
    mine = me % groups
    pairs, total_rows, _ = pieces[0].shape
    tok_rows, width = queries[0].shape
    span = pairs * DH
    rows = videos * tok_rows
    scale = 1.0 / math.sqrt(DH)
    shape = (pairs * rows, total_rows)
    patch = (lax.broadcasted_iota(jnp.int32, shape, 0) % rows // tok_rows * groups) ^ me
    own = patch == lax.broadcasted_iota(jnp.int32, shape, 1) // tok_rows
    lane = lax.broadcasted_iota(jnp.int32, (rows, DH), 1)
    logs = jnp.zeros((rows, DH), F32)
    for t in range(groups):
        start = pl.multiple_of((mine ^ t) * span, DH)
        query = stacked(queries, pl.ds(start, span))
        scores = jnp.concatenate(
            [
                lax.dot_general(
                    query[:, pair * DH : (pair + 1) * DH],
                    pieces[t][pair, :, :DH],
                    TRANSPOSED,
                    preferred_element_type=F32,
                )
                for pair in range(pairs)
            ],
            axis=0,
        )
        weights, inverse, log = softmax_parts(jnp.where(own, -jnp.inf, scores * scale))
        results = []
        for pair in range(pairs):
            here = slice(pair * rows, (pair + 1) * rows)
            results.append(
                inverse[here]
                * jnp.dot(weights[here], pieces[t][pair, :, DH:], preferred_element_type=F32)
            )
            logs = jnp.where(lane == t * pairs + pair, log[here], logs)
        result = jnp.concatenate(results, axis=1).astype(BF16)
        for s in range(videos):
            outs[s][:, t * span : (t + 1) * span] = result[s * tok_rows : (s + 1) * tok_rows]
    high = logs.astype(BF16).astype(F32)
    middle = (logs - high).astype(BF16).astype(F32)
    low = (logs - high - middle).astype(BF16).astype(F32)
    heads = groups * pairs
    terms = (high + pltpu.roll(middle, heads, 1) + pltpu.roll(low, 2 * heads, 1)).astype(BF16)
    for s in range(videos):
        outs[s][:, width:] = terms[s * tok_rows : (s + 1) * tok_rows]


def join_kernel(groups, videos, *refs):
    back = in_order(refs[:videos])
    fresh_ref, log_ref, out_ref, done_ref, sems = refs[videos:]
    me = lax.axis_index("patch")
    own, mine = me // groups, me % groups
    _, tok_rows, width = fresh_ref.shape
    heads = width // DH
    pairs = heads // groups
    span = pairs * DH
    copies = []
    for s in range(videos):
        terms = back[s][:, width:].astype(F32)
        stale_log = terms + pltpu.roll(terms, DH - heads, 1) + pltpu.roll(terms, DH - 2 * heads, 1)
        share = 1.0 / (1.0 + jnp.exp(stale_log - log_ref[s]))
        for t in range(groups):
            parts = []
            for pair in range(pairs):
                head = t * pairs + pair
                here = slice(head * DH, (head + 1) * DH)
                stale = back[s][:, here].astype(F32)
                parts.append(stale + share[:, head : head + 1] * (fresh_ref[s, :, here] - stale))
            lanes = pl.ds(pl.multiple_of((mine ^ t) * span, DH), span)
            done_ref[s, :, lanes] = jnp.concatenate(parts, axis=1).astype(BF16)
        copies.append(pltpu.make_async_copy(done_ref.at[s], out_ref.at[own ^ s], sems.at[s]))
        copies[-1].start()
    for copy in copies:
        copy.wait()


def cache_kernel(got_ref, out_ref, sems):
    copies = []
    for pair in range(out_ref.shape[0]):
        lanes = pl.ds(2 * pair * DH, 2 * DH)
        copies.append(
            pltpu.make_async_copy(got_ref.at[:, :, lanes], out_ref.at[pair], sems.at[pair])
        )
        copies[-1].start()
    for copy in copies:
        copy.wait()


def permuted(array, offset, patches):
    return lax.ppermute(array, "patch", [(i, i ^ offset) for i in range(patches)])


def far_first(arrays):
    half = len(arrays) // 2
    return [*arrays[half:], *arrays[1:half], arrays[0]]


def in_order(arrays):
    half = len(arrays) // 2
    return [arrays[-1], *arrays[half:-1], *arrays[:half]]


def exchange(arrays, stride, patches):
    return [arrays[0]] + [
        permuted(arrays[s], s * stride, patches) for s in range(1, len(arrays))
    ]


def local(queries, keys, values, q_gain, k_gain, stale_cache, coords):
    videos, tok_rows, width = queries.shape
    pairs_here, total_rows, _ = stale_cache.shape
    patches = total_rows // tok_rows
    groups = patches // videos

    def kernel(body, name, limit, cost=0, **kwargs):
        return pl.pallas_call(
            body,
            name=name,
            compiler_params=pltpu.CompilerParams(vmem_limit_bytes=limit * MIB),
            cost_estimate=pl.CostEstimate(flops=0, bytes_accessed=cost, transcendentals=0),
            **kwargs,
        )

    columns = [[v * groups + g for v in range(videos)] for g in range(groups)]
    query_raw = lax.all_to_all(
        queries, "patch", split_axis=0, concat_axis=0, axis_index_groups=columns, tiled=True
    )
    coords_got = exchange([coords] * videos, groups, patches)
    pieces = {0: stale_cache}
    bit = groups // 2
    pieces[bit] = permuted(stale_cache, bit, patches)
    gains = q_gain.reshape(1, width), k_gain.reshape(1, width)
    query, fresh = kernel(
        own_kernel,
        "own",
        16,
        out_shape=(
            jax.ShapeDtypeStruct(queries.shape, BF16),
            jax.ShapeDtypeStruct((patches, tok_rows, 2 * pairs_here * DH), BF16),
        ),
        in_specs=[VMEM] * 5 + [SMEM],
        out_specs=(VMEM, VMEM),
    )(queries, keys, values, *gains, coords)
    fresh_sent, query_raw, coords_got = lax.optimization_barrier((fresh, query_raw, coords_got))
    cached = lax.all_to_all(fresh_sent, "patch", split_axis=0, concat_axis=0, tiled=True)
    query_got = kernel(
        functools.partial(turn_kernel, groups),
        "turn",
        16,
        out_shape=jax.ShapeDtypeStruct(queries.shape, BF16),
        in_specs=[VMEM] * 2 + [SMEM] * videos,
        out_specs=VMEM,
    )(query_raw, gains[0], *coords_got)
    pieces, query_got = lax.optimization_barrier((pieces, query_got))
    while bit > 1:
        bit //= 2
        pieces.update({t | bit: permuted(piece, bit, patches) for t, piece in list(pieces.items())})
    result = kernel(
        functools.partial(stale_kernel, groups, videos),
        "stale",
        32,
        out_shape=[jax.ShapeDtypeStruct((tok_rows, width + DH), BF16)] * videos,
        in_specs=[VMEM] * (1 + groups),
        out_specs=[VMEM] * videos,
    )(query_got, *[pieces[t] for t in range(groups)])
    result, fresh_late = lax.optimization_barrier((result, fresh))
    back = far_first(exchange(result, groups, patches))
    fresh_sum, fresh_log = kernel(
        functools.partial(fresh_kernel, groups, videos),
        "fresh",
        16,
        out_shape=(
            jax.ShapeDtypeStruct((videos, tok_rows, width), F32),
            jax.ShapeDtypeStruct((videos, tok_rows, DH), F32),
        ),
        in_specs=[VMEM] * 2,
        out_specs=(VMEM, VMEM),
    )(query, fresh_late)
    next_cache = kernel(
        cache_kernel,
        "cache",
        16,
        out_shape=jax.ShapeDtypeStruct((pairs_here, patches, tok_rows, 2 * DH), BF16),
        in_specs=[VMEM],
        out_specs=HBM,
        scratch_shapes=[pltpu.SemaphoreType.DMA((pairs_here,))],
    )(cached)
    attended = kernel(
        functools.partial(join_kernel, groups, videos),
        "join",
        16,
        out_shape=jax.ShapeDtypeStruct(queries.shape, BF16),
        in_specs=[VMEM] * (videos + 2),
        out_specs=HBM,
        scratch_shapes=[
            pltpu.VMEM(queries.shape, BF16),
            pltpu.SemaphoreType.DMA((videos,)),
        ],
    )(*back, fresh_sum, fresh_log)
    return (attended, next_cache.reshape(stale_cache.shape))


def solution(mesh):
    in_specs = (
        P("req", "patch", None),
        P("req", "patch", None),
        P("req", "patch", None),
        P(),
        P(),
        P(("req", "patch"), None, None),
        P(None, "patch"),
    )
    out_specs = (P("req", "patch", None), P(("req", "patch"), None, None))
    return jax.shard_map(local, mesh=mesh, in_specs=in_specs, out_specs=out_specs, check_vma=False)
```

```python
import functools
import math

import jax
import jax.numpy as jnp
from jax import lax
from jax.experimental import pallas as pl
from jax.experimental.pallas import tpu as pltpu
from jax.sharding import PartitionSpec as P

DH = 128
VMEM = pl.BlockSpec(memory_space=pltpu.VMEM)
HBM = pl.BlockSpec(memory_space=pltpu.HBM)
SMEM = pl.BlockSpec(memory_space=pltpu.SMEM)
MIB = 1024 * 1024
BF16 = jnp.bfloat16
F32 = jnp.float32
TRANSPOSED = (((1,), (1,)), ((), ()))


def lane_axis(shape):
    side = DH // 6
    first = DH // 2 - 2 * side
    pair = lax.broadcasted_iota(jnp.int32, shape, 1) // 2
    return pair, (pair >= first).astype(jnp.int32) + (pair >= first + side).astype(jnp.int32)


def lane_places(coords_ref, tok_rows):
    shape = (tok_rows, DH)
    row = lax.broadcasted_iota(jnp.int32, shape, 0)
    _, axis = lane_axis(shape)
    place = jnp.zeros(shape, jnp.int32)
    for which in range(3):
        for token in range(tok_rows):
            place = jnp.where((axis == which) & (row == token), coords_ref[which, token], place)
    return place.astype(F32)


def rope_tables(place):
    side = DH // 6
    first = DH // 2 - 2 * side
    pair, axis = lane_axis(place.shape)
    step = jnp.where(axis == 0, pair, jnp.where(axis == 1, pair - first, pair - first - side))
    count = jnp.where(axis == 0, float(first), float(side))
    angle = place * jnp.exp(step.astype(F32) / count * (-math.log(10000.0)))
    sine = jnp.sin(angle)
    even = lax.broadcasted_iota(jnp.int32, place.shape, 1) % 2 == 0
    return jnp.cos(angle), jnp.where(even, -sine, 0.0), jnp.where(even, 0.0, sine)


def normed_heads(wide, gain_ref, tables):
    cosine, sine_even, sine_odd = tables
    width = wide.shape[-1]
    meansq = jnp.sum(wide * wide, axis=-1, keepdims=True) * (1.0 / width)
    inverse = lax.rsqrt(meansq + 1e-06)
    for head in range(width // DH):
        here = slice(head * DH, (head + 1) * DH)
        y = wide[:, here] * inverse * gain_ref[:, here]
        y = y * cosine + pltpu.roll(y, DH - 1, 1) * sine_even + pltpu.roll(y, 1, 1) * sine_odd
        yield head, y.astype(BF16)


def lay_kernel(groups, q_hbm, coords_hbm, *refs):
    videos, tok_rows, width = q_hbm.shape
    outs, (held, coords_ref, sems, coords_sem) = refs[:videos], refs[videos:]
    own = lax.axis_index("patch") // groups
    first = pltpu.make_async_copy(coords_hbm, coords_ref, coords_sem)
    first.start()
    reads = [
        pltpu.make_async_copy(q_hbm.at[own ^ s], held.at[s, :, pl.ds(0, width)], sems.at[0, s])
        for s in range(videos)
    ]
    writes = [pltpu.make_async_copy(held.at[s], outs[s], sems.at[1, s]) for s in range(videos)]
    for read in reads:
        read.start()
    first.wait()
    place = lane_places(coords_ref, tok_rows).astype(BF16)
    for s in range(videos):
        held[s, :, width:] = place
    for read, write in zip(reads, writes):
        read.wait()
        write.start()
    for write in writes:
        write.wait()


def key_kernel(k_hbm, v_hbm, gain_hbm, coords_hbm, out_hbm, k_ref, v_ref, gain_ref, coords_ref, done_ref, sems):
    videos, tok_rows, width = k_hbm.shape
    pairs = out_hbm.shape[2] // (2 * DH)
    groups = out_hbm.shape[0] // videos
    sources, places = (coords_hbm, k_hbm, gain_hbm, v_hbm), (coords_ref, k_ref, gain_ref, v_ref)
    reads = [
        pltpu.make_async_copy(source, place, sems.at[i])
        for i, (source, place) in enumerate(zip(sources, places))
    ]
    for read in reads:
        read.start()
    for read in reads:
        read.wait()
    tables = rope_tables(lane_places(coords_ref, tok_rows))
    writes = []
    for video in range(videos):
        for head, y in normed_heads(k_ref[video].astype(F32), gain_ref, tables):
            target, start = video * groups + head // pairs, head % pairs * 2 * DH
            done_ref[target, :, start : start + DH] = y
            done_ref[target, :, start + DH : start + 2 * DH] = v_ref[
                video, :, head * DH : (head + 1) * DH
            ]
        part = pl.ds(video * groups, groups)
        writes.append(pltpu.make_async_copy(done_ref.at[part], out_hbm.at[part], sems.at[4 + video]))
        writes[-1].start()
    for write in writes:
        write.wait()


def turn_kernel(gain_ref, *refs):
    got, out_ref = in_order(refs[:-1]), refs[-1]
    videos, tok_rows, width = out_ref.shape
    place = jnp.concatenate([ref[:, width:].astype(F32) for ref in got], axis=0)
    tables = rope_tables(place)
    for s in range(videos):
        mine = [table[s * tok_rows : (s + 1) * tok_rows] for table in tables]
        for head, y in normed_heads(got[s][:, :width].astype(F32), gain_ref, mine):
            out_ref[s, :, head * DH : (head + 1) * DH] = y


def query_kernel(q_ref, gain_ref, coords_ref, out_ref):
    videos, tok_rows, _ = q_ref.shape
    tables = rope_tables(lane_places(coords_ref, tok_rows))
    for video in range(videos):
        for head, y in normed_heads(q_ref[video].astype(F32), gain_ref, tables):
            out_ref[video, :, head * DH : (head + 1) * DH] = y


def softmax_parts(scores):
    top = jnp.max(scores, axis=-1, keepdims=True)
    weights = jnp.exp(scores - top)
    total = jnp.sum(weights, axis=-1, keepdims=True)
    return weights.astype(BF16), 1.0 / total, top + jnp.log(total)


def stacked(refs, lanes):
    rows = [ref[:, lanes].astype(F32) for ref in refs]
    return jnp.concatenate(rows, axis=0).astype(BF16)


def fresh_kernel(groups, videos, query_ref, fresh_ref, out_ref, log_ref):
    me = lax.axis_index("patch")
    own, mine = me // groups, me % groups
    queries = [query_ref.at[own ^ s] for s in range(videos)]
    _, tok_rows, width = out_ref.shape
    span = width // groups
    pairs = span // DH
    rows = videos * tok_rows
    scale = 1.0 / math.sqrt(DH)
    shape = (pairs * rows, rows)
    same = lax.broadcasted_iota(jnp.int32, shape, 0) % rows // tok_rows == (
        lax.broadcasted_iota(jnp.int32, shape, 1) // tok_rows
    )
    lane = lax.broadcasted_iota(jnp.int32, (rows, DH), 1)
    logs = jnp.zeros((rows, DH), F32)
    for t in range(groups):
        lanes = pl.ds(pl.multiple_of((mine ^ t) * span, DH), span)
        query = stacked(queries, lanes)
        fresh = stacked([fresh_ref.at[me ^ (s * groups) ^ t] for s in range(videos)], slice(None))
        scores = jnp.concatenate(
            [
                lax.dot_general(
                    query[:, pair * DH : (pair + 1) * DH],
                    fresh[:, 2 * pair * DH : (2 * pair + 1) * DH],
                    TRANSPOSED,
                    preferred_element_type=F32,
                )
                for pair in range(pairs)
            ],
            axis=0,
        )
        weights, inverse, log = softmax_parts(jnp.where(same, scores * scale, -jnp.inf))
        for pair in range(pairs):
            here = slice(pair * rows, (pair + 1) * rows)
            head = t * pairs + pair
            result = inverse[here] * jnp.dot(
                weights[here],
                fresh[:, (2 * pair + 1) * DH : (2 * pair + 2) * DH],
                preferred_element_type=F32,
            )
            logs = jnp.where(lane == head, log[here], logs)
            for s in range(videos):
                out_ref[s, :, head * DH : (head + 1) * DH] = result[s * tok_rows : (s + 1) * tok_rows]
    for s in range(videos):
        log_ref[s] = logs[s * tok_rows : (s + 1) * tok_rows]


def stale_kernel(groups, videos, query_ref, *refs):
    queries = [query_ref.at[s] for s in range(videos)]
    pieces, outs = refs[:groups], refs[groups:]
    me = lax.axis_index("patch")
    mine = me % groups
    pairs, total_rows, _ = pieces[0].shape
    tok_rows, width = queries[0].shape
    span = pairs * DH
    rows = videos * tok_rows
    scale = 1.0 / math.sqrt(DH)
    shape = (pairs * rows, total_rows)
    patch = (lax.broadcasted_iota(jnp.int32, shape, 0) % rows // tok_rows * groups) ^ me
    own = patch == lax.broadcasted_iota(jnp.int32, shape, 1) // tok_rows
    lane = lax.broadcasted_iota(jnp.int32, (rows, DH), 1)
    logs = jnp.zeros((rows, DH), F32)
    for t in range(groups):
        start = pl.multiple_of((mine ^ t) * span, DH)
        query = stacked(queries, pl.ds(start, span))
        scores = jnp.concatenate(
            [
                lax.dot_general(
                    query[:, pair * DH : (pair + 1) * DH],
                    pieces[t][pair, :, :DH],
                    TRANSPOSED,
                    preferred_element_type=F32,
                )
                for pair in range(pairs)
            ],
            axis=0,
        )
        weights, inverse, log = softmax_parts(jnp.where(own, -jnp.inf, scores * scale))
        results = []
        for pair in range(pairs):
            here = slice(pair * rows, (pair + 1) * rows)
            results.append(
                inverse[here]
                * jnp.dot(weights[here], pieces[t][pair, :, DH:], preferred_element_type=F32)
            )
            logs = jnp.where(lane == t * pairs + pair, log[here], logs)
        result = jnp.concatenate(results, axis=1).astype(BF16)
        for s in range(videos):
            outs[s][:, t * span : (t + 1) * span] = result[s * tok_rows : (s + 1) * tok_rows]
    high = logs.astype(BF16).astype(F32)
    middle = (logs - high).astype(BF16).astype(F32)
    low = (logs - high - middle).astype(BF16).astype(F32)
    heads = groups * pairs
    terms = (high + pltpu.roll(middle, heads, 1) + pltpu.roll(low, 2 * heads, 1)).astype(BF16)
    for s in range(videos):
        outs[s][:, width:] = terms[s * tok_rows : (s + 1) * tok_rows]


def join_kernel(groups, videos, *refs):
    back = in_order(refs[:videos])
    fresh_ref, log_ref, out_ref, done_ref, sems = refs[videos:]
    me = lax.axis_index("patch")
    own, mine = me // groups, me % groups
    _, tok_rows, width = fresh_ref.shape
    heads = width // DH
    pairs = heads // groups
    span = pairs * DH
    copies = []
    for s in range(videos):
        terms = back[s][:, width:].astype(F32)
        stale_log = terms + pltpu.roll(terms, DH - heads, 1) + pltpu.roll(terms, DH - 2 * heads, 1)
        share = 1.0 / (1.0 + jnp.exp(stale_log - log_ref[s]))
        for t in range(groups):
            parts = []
            for pair in range(pairs):
                head = t * pairs + pair
                here = slice(head * DH, (head + 1) * DH)
                stale = back[s][:, here].astype(F32)
                parts.append(stale + share[:, head : head + 1] * (fresh_ref[s, :, here] - stale))
            lanes = pl.ds(pl.multiple_of((mine ^ t) * span, DH), span)
            done_ref[s, :, lanes] = jnp.concatenate(parts, axis=1).astype(BF16)
        copies.append(pltpu.make_async_copy(done_ref.at[s], out_ref.at[own ^ s], sems.at[s]))
        copies[-1].start()
    for copy in copies:
        copy.wait()


def cache_kernel(got_ref, out_ref, sems):
    copies = []
    for pair in range(out_ref.shape[0]):
        lanes = pl.ds(2 * pair * DH, 2 * DH)
        copies.append(
            pltpu.make_async_copy(got_ref.at[:, :, lanes], out_ref.at[pair], sems.at[pair])
        )
        copies[-1].start()
    for copy in copies:
        copy.wait()


def permuted(array, offset, patches):
    return lax.ppermute(array, "patch", [(i, i ^ offset) for i in range(patches)])


def far_first(arrays):
    half = len(arrays) // 2
    return [*arrays[half:], *arrays[1:half], arrays[0]]


def in_order(arrays):
    half = len(arrays) // 2
    return [arrays[-1], *arrays[half:-1], *arrays[:half]]


def exchange(arrays, stride, patches):
    return [arrays[0]] + [
        permuted(arrays[s], s * stride, patches) for s in range(1, len(arrays))
    ]


def local(queries, keys, values, q_gain, k_gain, stale_cache, coords):
    videos, tok_rows, width = queries.shape
    pairs_here, total_rows, _ = stale_cache.shape
    patches = total_rows // tok_rows
    groups = patches // videos

    def kernel(body, name, limit, cost=0, **kwargs):
        return pl.pallas_call(
            body,
            name=name,
            compiler_params=pltpu.CompilerParams(vmem_limit_bytes=limit * MIB),
            cost_estimate=pl.CostEstimate(flops=0, bytes_accessed=cost, transcendentals=0),
            **kwargs,
        )

    gains = q_gain.reshape(1, width), k_gain.reshape(1, width)
    sent = kernel(
        functools.partial(lay_kernel, groups),
        "lay",
        56,
        out_shape=[jax.ShapeDtypeStruct((tok_rows, width + DH), BF16)] * videos,
        in_specs=[HBM] * 2,
        out_specs=[HBM] * videos,
        scratch_shapes=[
            pltpu.VMEM((videos, tok_rows, width + DH), BF16),
            pltpu.SMEM(coords.shape, jnp.int32),
            pltpu.SemaphoreType.DMA((2, videos)),
            pltpu.SemaphoreType.DMA,
        ],
    )(queries, coords)
    stale_sent, kept = lax.optimization_barrier((stale_cache, sent[0]))
    pieces = {0: stale_cache}
    bit = groups // 2
    pieces[bit] = permuted(stale_sent, bit, patches)
    query_raw = far_first(exchange([kept, *sent[1:]], groups, patches))
    fresh = kernel(
        key_kernel,
        "key",
        56,
        out_shape=jax.ShapeDtypeStruct((patches, tok_rows, 2 * pairs_here * DH), BF16),
        in_specs=[HBM] * 4,
        out_specs=HBM,
        scratch_shapes=[
            pltpu.VMEM(keys.shape, BF16),
            pltpu.VMEM(keys.shape, BF16),
            pltpu.VMEM((1, width), F32),
            pltpu.SMEM(coords.shape, jnp.int32),
            pltpu.VMEM((patches, tok_rows, 2 * pairs_here * DH), BF16),
            pltpu.SemaphoreType.DMA((4 + videos,)),
        ],
    )(keys, values, gains[1], coords)
    fresh_sent, query_raw = lax.optimization_barrier((fresh, query_raw))
    cached = lax.all_to_all(fresh_sent, "patch", split_axis=0, concat_axis=0, tiled=True)
    query_got = kernel(
        turn_kernel,
        "turn",
        16,
        out_shape=jax.ShapeDtypeStruct(queries.shape, BF16),
        in_specs=[VMEM] * (1 + videos),
        out_specs=VMEM,
    )(gains[0], *query_raw)
    pieces, query_got = lax.optimization_barrier((pieces, query_got))
    while bit > 1:
        bit //= 2
        pieces.update({t | bit: permuted(piece, bit, patches) for t, piece in list(pieces.items())})
    result = kernel(
        functools.partial(stale_kernel, groups, videos),
        "stale",
        32,
        out_shape=[jax.ShapeDtypeStruct((tok_rows, width + DH), BF16)] * videos,
        in_specs=[VMEM] * (1 + groups),
        out_specs=[VMEM] * videos,
    )(query_got, *[pieces[t] for t in range(groups)])
    result, fresh_late, queries_late = lax.optimization_barrier((result, fresh, queries))
    query = kernel(
        query_kernel,
        "query",
        16,
        out_shape=jax.ShapeDtypeStruct(queries.shape, BF16),
        in_specs=[VMEM] * 2 + [SMEM],
        out_specs=VMEM,
    )(queries_late, gains[0], coords)
    back = far_first(exchange(result, groups, patches))
    fresh_sum, fresh_log = kernel(
        functools.partial(fresh_kernel, groups, videos),
        "fresh",
        16,
        out_shape=(
            jax.ShapeDtypeStruct((videos, tok_rows, width), F32),
            jax.ShapeDtypeStruct((videos, tok_rows, DH), F32),
        ),
        in_specs=[VMEM] * 2,
        out_specs=(VMEM, VMEM),
    )(query, fresh_late)
    next_cache = kernel(
        cache_kernel,
        "cache",
        16,
        out_shape=jax.ShapeDtypeStruct((pairs_here, patches, tok_rows, 2 * DH), BF16),
        in_specs=[VMEM],
        out_specs=HBM,
        scratch_shapes=[pltpu.SemaphoreType.DMA((pairs_here,))],
    )(cached)
    attended = kernel(
        functools.partial(join_kernel, groups, videos),
        "join",
        16,
        out_shape=jax.ShapeDtypeStruct(queries.shape, BF16),
        in_specs=[VMEM] * (videos + 2),
        out_specs=HBM,
        scratch_shapes=[
            pltpu.VMEM(queries.shape, BF16),
            pltpu.SemaphoreType.DMA((videos,)),
        ],
    )(*back, fresh_sum, fresh_log)
    return (attended, next_cache.reshape(stale_cache.shape))


def solution(mesh):
    in_specs = (
        P("req", "patch", None),
        P("req", "patch", None),
        P("req", "patch", None),
        P(),
        P(),
        P(("req", "patch"), None, None),
        P(None, "patch"),
    )
    out_specs = (P("req", "patch", None), P(("req", "patch"), None, None))
    return jax.shard_map(local, mesh=mesh, in_specs=in_specs, out_specs=out_specs, check_vma=False)
```

```python
import functools
import math

import jax
import jax.numpy as jnp
from jax import lax
from jax.experimental import pallas as pl
from jax.experimental.pallas import tpu as pltpu
from jax.sharding import PartitionSpec as P

DH = 128
VMEM = pl.BlockSpec(memory_space=pltpu.VMEM)
HBM = pl.BlockSpec(memory_space=pltpu.HBM)
SMEM = pl.BlockSpec(memory_space=pltpu.SMEM)
MIB = 1024 * 1024
BF16 = jnp.bfloat16
F32 = jnp.float32
TRANSPOSED = (((1,), (1,)), ((), ()))


def lane_axis(shape):
    side = DH // 6
    first = DH // 2 - 2 * side
    pair = lax.broadcasted_iota(jnp.int32, shape, 1) // 2
    return pair, (pair >= first).astype(jnp.int32) + (pair >= first + side).astype(jnp.int32)


def lane_places(coords_ref, tok_rows):
    shape = (tok_rows, DH)
    row = lax.broadcasted_iota(jnp.int32, shape, 0)
    _, axis = lane_axis(shape)
    place = jnp.zeros(shape, jnp.int32)
    for which in range(3):
        for token in range(tok_rows):
            place = jnp.where((axis == which) & (row == token), coords_ref[which, token], place)
    return place.astype(F32)


def rope_tables(place):
    side = DH // 6
    first = DH // 2 - 2 * side
    pair, axis = lane_axis(place.shape)
    step = jnp.where(axis == 0, pair, jnp.where(axis == 1, pair - first, pair - first - side))
    count = jnp.where(axis == 0, float(first), float(side))
    angle = place * jnp.exp(step.astype(F32) / count * (-math.log(10000.0)))
    sine = jnp.sin(angle)
    even = lax.broadcasted_iota(jnp.int32, place.shape, 1) % 2 == 0
    return jnp.cos(angle), jnp.where(even, -sine, 0.0), jnp.where(even, 0.0, sine)


def normed_heads(wide, gain_ref, tables):
    cosine, sine_even, sine_odd = tables
    width = wide.shape[-1]
    meansq = jnp.sum(wide * wide, axis=-1, keepdims=True) * (1.0 / width)
    inverse = lax.rsqrt(meansq + 1e-06)
    for head in range(width // DH):
        here = slice(head * DH, (head + 1) * DH)
        y = wide[:, here] * inverse * gain_ref[:, here]
        y = y * cosine + pltpu.roll(y, DH - 1, 1) * sine_even + pltpu.roll(y, 1, 1) * sine_odd
        yield head, y.astype(BF16)


def lay_kernel(groups, q_hbm, coords_hbm, *refs):
    videos, tok_rows, width = q_hbm.shape
    outs, (held, coords_ref, sems, coords_sem) = refs[:videos], refs[videos:]
    own = lax.axis_index("patch") // groups
    first = pltpu.make_async_copy(coords_hbm, coords_ref, coords_sem)
    first.start()
    reads = [
        pltpu.make_async_copy(q_hbm.at[own ^ s], held.at[s, :, pl.ds(0, width)], sems.at[0, s])
        for s in range(videos)
    ]
    writes = [pltpu.make_async_copy(held.at[s], outs[s], sems.at[1, s]) for s in range(videos)]
    for read in reads:
        read.start()
    first.wait()
    place = lane_places(coords_ref, tok_rows).astype(BF16)
    for s in range(videos):
        held[s, :, width:] = place
    for read, write in zip(reads, writes):
        read.wait()
        write.start()
    for write in writes:
        write.wait()


def key_kernel(k_hbm, v_hbm, gain_hbm, coords_hbm, out_hbm, k_ref, v_ref, gain_ref, coords_ref, done_ref, sems):
    videos, tok_rows, width = k_hbm.shape
    pairs = out_hbm.shape[2] // (2 * DH)
    groups = out_hbm.shape[0] // videos
    sources, places = (coords_hbm, k_hbm, gain_hbm, v_hbm), (coords_ref, k_ref, gain_ref, v_ref)
    reads = [
        pltpu.make_async_copy(source, place, sems.at[i])
        for i, (source, place) in enumerate(zip(sources, places))
    ]
    for read in reads:
        read.start()
    for read in reads:
        read.wait()
    tables = rope_tables(lane_places(coords_ref, tok_rows))
    writes = []
    for video in range(videos):
        for head, y in normed_heads(k_ref[video].astype(F32), gain_ref, tables):
            target, start = video * groups + head // pairs, head % pairs * 2 * DH
            done_ref[target, :, start : start + DH] = y
            done_ref[target, :, start + DH : start + 2 * DH] = v_ref[
                video, :, head * DH : (head + 1) * DH
            ]
        part = pl.ds(video * groups, groups)
        writes.append(pltpu.make_async_copy(done_ref.at[part], out_hbm.at[part], sems.at[4 + video]))
        writes[-1].start()
    for write in writes:
        write.wait()


def turn_kernel(gain_ref, *refs):
    got, out_ref = in_order(refs[:-1]), refs[-1]
    videos, tok_rows, width = out_ref.shape
    place = jnp.concatenate([ref[:, width:].astype(F32) for ref in got], axis=0)
    tables = rope_tables(place)
    for s in range(videos):
        mine = [table[s * tok_rows : (s + 1) * tok_rows] for table in tables]
        for head, y in normed_heads(got[s][:, :width].astype(F32), gain_ref, mine):
            out_ref[s, :, head * DH : (head + 1) * DH] = y


def query_kernel(q_ref, gain_ref, coords_ref, out_ref):
    videos, tok_rows, _ = q_ref.shape
    tables = rope_tables(lane_places(coords_ref, tok_rows))
    for video in range(videos):
        for head, y in normed_heads(q_ref[video].astype(F32), gain_ref, tables):
            out_ref[video, :, head * DH : (head + 1) * DH] = y


def softmax_parts(scores):
    top = jnp.max(scores, axis=-1, keepdims=True)
    weights = jnp.exp(scores - top)
    total = jnp.sum(weights, axis=-1, keepdims=True)
    return weights.astype(BF16), 1.0 / total, top + jnp.log(total)


def stacked(refs, lanes):
    rows = [ref[:, lanes].astype(F32) for ref in refs]
    return jnp.concatenate(rows, axis=0).astype(BF16)


def fresh_kernel(groups, videos, query_ref, fresh_ref, out_ref, log_ref):
    me = lax.axis_index("patch")
    own, mine = me // groups, me % groups
    queries = [query_ref.at[own ^ s] for s in range(videos)]
    _, tok_rows, width = out_ref.shape
    span = width // groups
    pairs = span // DH
    rows = videos * tok_rows
    scale = 1.0 / math.sqrt(DH)
    shape = (pairs * rows, rows)
    same = lax.broadcasted_iota(jnp.int32, shape, 0) % rows // tok_rows == (
        lax.broadcasted_iota(jnp.int32, shape, 1) // tok_rows
    )
    lane = lax.broadcasted_iota(jnp.int32, (rows, DH), 1)
    logs = jnp.zeros((rows, DH), F32)
    for t in range(groups):
        lanes = pl.ds(pl.multiple_of((mine ^ t) * span, DH), span)
        query = stacked(queries, lanes)
        fresh = stacked([fresh_ref.at[me ^ (s * groups) ^ t] for s in range(videos)], slice(None))
        scores = jnp.concatenate(
            [
                lax.dot_general(
                    query[:, pair * DH : (pair + 1) * DH],
                    fresh[:, 2 * pair * DH : (2 * pair + 1) * DH],
                    TRANSPOSED,
                    preferred_element_type=F32,
                )
                for pair in range(pairs)
            ],
            axis=0,
        )
        weights, inverse, log = softmax_parts(jnp.where(same, scores * scale, -jnp.inf))
        for pair in range(pairs):
            here = slice(pair * rows, (pair + 1) * rows)
            head = t * pairs + pair
            result = inverse[here] * jnp.dot(
                weights[here],
                fresh[:, (2 * pair + 1) * DH : (2 * pair + 2) * DH],
                preferred_element_type=F32,
            )
            logs = jnp.where(lane == head, log[here], logs)
            for s in range(videos):
                out_ref[s, :, head * DH : (head + 1) * DH] = result[s * tok_rows : (s + 1) * tok_rows]
    for s in range(videos):
        log_ref[s] = logs[s * tok_rows : (s + 1) * tok_rows]


def stale_kernel(groups, videos, query_ref, *refs):
    queries = [query_ref.at[s] for s in range(videos)]
    pieces, outs = refs[:groups], refs[groups:]
    me = lax.axis_index("patch")
    mine = me % groups
    pairs, total_rows, _ = pieces[0].shape
    tok_rows, width = queries[0].shape
    span = pairs * DH
    rows = videos * tok_rows
    scale = 1.0 / math.sqrt(DH)
    shape = (pairs * rows, total_rows)
    patch = (lax.broadcasted_iota(jnp.int32, shape, 0) % rows // tok_rows * groups) ^ me
    own = patch == lax.broadcasted_iota(jnp.int32, shape, 1) // tok_rows
    lane = lax.broadcasted_iota(jnp.int32, (rows, DH), 1)
    logs = jnp.zeros((rows, DH), F32)
    for t in range(groups):
        start = pl.multiple_of((mine ^ t) * span, DH)
        query = stacked(queries, pl.ds(start, span))
        scores = jnp.concatenate(
            [
                lax.dot_general(
                    query[:, pair * DH : (pair + 1) * DH],
                    pieces[t][pair, :, :DH],
                    TRANSPOSED,
                    preferred_element_type=F32,
                )
                for pair in range(pairs)
            ],
            axis=0,
        )
        weights, inverse, log = softmax_parts(jnp.where(own, -jnp.inf, scores * scale))
        results = []
        for pair in range(pairs):
            here = slice(pair * rows, (pair + 1) * rows)
            results.append(
                inverse[here]
                * jnp.dot(weights[here], pieces[t][pair, :, DH:], preferred_element_type=F32)
            )
            logs = jnp.where(lane == t * pairs + pair, log[here], logs)
        result = jnp.concatenate(results, axis=1).astype(BF16)
        for s in range(videos):
            outs[s][:, t * span : (t + 1) * span] = result[s * tok_rows : (s + 1) * tok_rows]
    high = logs.astype(BF16).astype(F32)
    middle = (logs - high).astype(BF16).astype(F32)
    low = (logs - high - middle).astype(BF16).astype(F32)
    heads = groups * pairs
    terms = (high + pltpu.roll(middle, heads, 1) + pltpu.roll(low, 2 * heads, 1)).astype(BF16)
    for s in range(videos):
        outs[s][:, width:] = terms[s * tok_rows : (s + 1) * tok_rows]


def join_kernel(groups, videos, *refs):
    back = in_order(refs[:videos])
    fresh_ref, log_ref, out_ref, done_ref, sems = refs[videos:]
    me = lax.axis_index("patch")
    own, mine = me // groups, me % groups
    _, tok_rows, width = fresh_ref.shape
    heads = width // DH
    pairs = heads // groups
    span = pairs * DH
    copies = []
    for s in range(videos):
        terms = back[s][:, width:].astype(F32)
        stale_log = terms + pltpu.roll(terms, DH - heads, 1) + pltpu.roll(terms, DH - 2 * heads, 1)
        share = 1.0 / (1.0 + jnp.exp(stale_log - log_ref[s]))
        for t in range(groups):
            parts = []
            for pair in range(pairs):
                head = t * pairs + pair
                here = slice(head * DH, (head + 1) * DH)
                stale = back[s][:, here].astype(F32)
                parts.append(stale + share[:, head : head + 1] * (fresh_ref[s, :, here] - stale))
            lanes = pl.ds(pl.multiple_of((mine ^ t) * span, DH), span)
            done_ref[s, :, lanes] = jnp.concatenate(parts, axis=1).astype(BF16)
        copies.append(pltpu.make_async_copy(done_ref.at[s], out_ref.at[own ^ s], sems.at[s]))
        copies[-1].start()
    for copy in copies:
        copy.wait()


def cache_kernel(got_ref, out_ref, sems):
    copies = []
    for pair in range(out_ref.shape[0]):
        lanes = pl.ds(2 * pair * DH, 2 * DH)
        copies.append(
            pltpu.make_async_copy(got_ref.at[:, :, lanes], out_ref.at[pair], sems.at[pair])
        )
        copies[-1].start()
    for copy in copies:
        copy.wait()


def permuted(array, offset, patches):
    return lax.ppermute(array, "patch", [(i, i ^ offset) for i in range(patches)])


def far_first(arrays):
    half = len(arrays) // 2
    return [*arrays[half:], *arrays[1:half], arrays[0]]


def in_order(arrays):
    half = len(arrays) // 2
    return [arrays[-1], *arrays[half:-1], *arrays[:half]]


def exchange(arrays, stride, patches):
    return [arrays[0]] + [
        permuted(arrays[s], s * stride, patches) for s in range(1, len(arrays))
    ]


def local(queries, keys, values, q_gain, k_gain, stale_cache, coords):
    videos, tok_rows, width = queries.shape
    pairs_here, total_rows, _ = stale_cache.shape
    patches = total_rows // tok_rows
    groups = patches // videos

    def kernel(body, name, limit, cost=0, **kwargs):
        return pl.pallas_call(
            body,
            name=name,
            compiler_params=pltpu.CompilerParams(vmem_limit_bytes=limit * MIB),
            cost_estimate=pl.CostEstimate(flops=cost, bytes_accessed=0, transcendentals=0),
            **kwargs,
        )

    gains = q_gain.reshape(1, width), k_gain.reshape(1, width)
    sent = kernel(
        functools.partial(lay_kernel, groups),
        "lay",
        56,
        out_shape=[jax.ShapeDtypeStruct((tok_rows, width + DH), BF16)] * videos,
        in_specs=[HBM] * 2,
        out_specs=[HBM] * videos,
        scratch_shapes=[
            pltpu.VMEM((videos, tok_rows, width + DH), BF16),
            pltpu.SMEM(coords.shape, jnp.int32),
            pltpu.SemaphoreType.DMA((2, videos)),
            pltpu.SemaphoreType.DMA,
        ],
    )(queries, coords)
    stale_sent, kept = lax.optimization_barrier((stale_cache, sent[0]))
    pieces = {0: stale_cache}
    bit = groups // 2
    pieces[bit] = permuted(stale_sent, bit, patches)
    query_raw = far_first(exchange([kept, *sent[1:]], groups, patches))
    fresh = kernel(
        key_kernel,
        "key",
        56,
        out_shape=jax.ShapeDtypeStruct((patches, tok_rows, 2 * pairs_here * DH), BF16),
        in_specs=[HBM] * 4,
        out_specs=HBM,
        scratch_shapes=[
            pltpu.VMEM(keys.shape, BF16),
            pltpu.VMEM(keys.shape, BF16),
            pltpu.VMEM((1, width), F32),
            pltpu.SMEM(coords.shape, jnp.int32),
            pltpu.VMEM((patches, tok_rows, 2 * pairs_here * DH), BF16),
            pltpu.SemaphoreType.DMA((4 + videos,)),
        ],
    )(keys, values, gains[1], coords)
    cached = lax.all_to_all(fresh, "patch", split_axis=0, concat_axis=0, tiled=True)
    query_raw, pieces, fresh = lax.optimization_barrier((query_raw, pieces, fresh))
    query_got = kernel(
        turn_kernel,
        "turn",
        16,
        cost=10**12,
        out_shape=jax.ShapeDtypeStruct(queries.shape, BF16),
        in_specs=[VMEM] * (1 + videos),
        out_specs=VMEM,
    )(gains[0], *query_raw)
    pieces, query_got = lax.optimization_barrier((pieces, query_got))
    while bit > 1:
        bit //= 2
        pieces.update({t | bit: permuted(piece, bit, patches) for t, piece in list(pieces.items())})
    result = kernel(
        functools.partial(stale_kernel, groups, videos),
        "stale",
        32,
        out_shape=[jax.ShapeDtypeStruct((tok_rows, width + DH), BF16)] * videos,
        in_specs=[VMEM] * (1 + groups),
        out_specs=[VMEM] * videos,
    )(query_got, *[pieces[t] for t in range(groups)])
    result, fresh_late, queries_late = lax.optimization_barrier((result, fresh, queries))
    query = kernel(
        query_kernel,
        "query",
        16,
        out_shape=jax.ShapeDtypeStruct(queries.shape, BF16),
        in_specs=[VMEM] * 2 + [SMEM],
        out_specs=VMEM,
    )(queries_late, gains[0], coords)
    back = far_first(exchange(result, groups, patches))
    fresh_sum, fresh_log = kernel(
        functools.partial(fresh_kernel, groups, videos),
        "fresh",
        16,
        out_shape=(
            jax.ShapeDtypeStruct((videos, tok_rows, width), F32),
            jax.ShapeDtypeStruct((videos, tok_rows, DH), F32),
        ),
        in_specs=[VMEM] * 2,
        out_specs=(VMEM, VMEM),
    )(query, fresh_late)
    next_cache = kernel(
        cache_kernel,
        "cache",
        16,
        out_shape=jax.ShapeDtypeStruct((pairs_here, patches, tok_rows, 2 * DH), BF16),
        in_specs=[VMEM],
        out_specs=HBM,
        scratch_shapes=[pltpu.SemaphoreType.DMA((pairs_here,))],
    )(cached)
    attended = kernel(
        functools.partial(join_kernel, groups, videos),
        "join",
        16,
        out_shape=jax.ShapeDtypeStruct(queries.shape, BF16),
        in_specs=[VMEM] * (videos + 2),
        out_specs=HBM,
        scratch_shapes=[
            pltpu.VMEM(queries.shape, BF16),
            pltpu.SemaphoreType.DMA((videos,)),
        ],
    )(*back, fresh_sum, fresh_log)
    return (attended, next_cache.reshape(stale_cache.shape))


def solution(mesh):
    in_specs = (
        P("req", "patch", None),
        P("req", "patch", None),
        P("req", "patch", None),
        P(),
        P(),
        P(("req", "patch"), None, None),
        P(None, "patch"),
    )
    out_specs = (P("req", "patch", None), P(("req", "patch"), None, None))
    return jax.shard_map(local, mesh=mesh, in_specs=in_specs, out_specs=out_specs, check_vma=False)
```

```python
import functools
import math

import jax
import jax.numpy as jnp
from jax import lax
from jax.experimental import pallas as pl
from jax.experimental.pallas import tpu as pltpu
from jax.sharding import PartitionSpec as P

DH = 128
VMEM = pl.BlockSpec(memory_space=pltpu.VMEM)
HBM = pl.BlockSpec(memory_space=pltpu.HBM)
SMEM = pl.BlockSpec(memory_space=pltpu.SMEM)
MIB = 1024 * 1024
BF16 = jnp.bfloat16
F32 = jnp.float32
TRANSPOSED = (((1,), (1,)), ((), ()))


def lane_axis(shape):
    side = DH // 6
    first = DH // 2 - 2 * side
    pair = lax.broadcasted_iota(jnp.int32, shape, 1) // 2
    return pair, (pair >= first).astype(jnp.int32) + (pair >= first + side).astype(jnp.int32)


def lane_places(coords_ref, tok_rows):
    shape = (tok_rows, DH)
    row = lax.broadcasted_iota(jnp.int32, shape, 0)
    _, axis = lane_axis(shape)
    place = jnp.zeros(shape, jnp.int32)
    for which in range(3):
        for token in range(tok_rows):
            place = jnp.where((axis == which) & (row == token), coords_ref[which, token], place)
    return place.astype(F32)


def rope_tables(place):
    side = DH // 6
    first = DH // 2 - 2 * side
    pair, axis = lane_axis(place.shape)
    step = jnp.where(axis == 0, pair, jnp.where(axis == 1, pair - first, pair - first - side))
    count = jnp.where(axis == 0, float(first), float(side))
    angle = place * jnp.exp(step.astype(F32) / count * (-math.log(10000.0)))
    sine = jnp.sin(angle)
    even = lax.broadcasted_iota(jnp.int32, place.shape, 1) % 2 == 0
    return jnp.cos(angle), jnp.where(even, -sine, 0.0), jnp.where(even, 0.0, sine)


def normed_heads(wide, gain_ref, tables):
    cosine, sine_even, sine_odd = tables
    width = wide.shape[-1]
    meansq = jnp.sum(wide * wide, axis=-1, keepdims=True) * (1.0 / width)
    inverse = lax.rsqrt(meansq + 1e-06)
    for head in range(width // DH):
        here = slice(head * DH, (head + 1) * DH)
        y = wide[:, here] * inverse * gain_ref[:, here]
        y = y * cosine + pltpu.roll(y, DH - 1, 1) * sine_even + pltpu.roll(y, 1, 1) * sine_odd
        yield head, y.astype(BF16)


def lay_kernel(groups, q_hbm, coords_hbm, *refs):
    videos, tok_rows, width = q_hbm.shape
    outs, (held, coords_ref, sems, coords_sem) = refs[:videos], refs[videos:]
    own = lax.axis_index("patch") // groups
    first = pltpu.make_async_copy(coords_hbm, coords_ref, coords_sem)
    first.start()
    reads = [
        pltpu.make_async_copy(q_hbm.at[own ^ s], held.at[s, :, pl.ds(0, width)], sems.at[0, s])
        for s in range(videos)
    ]
    writes = [pltpu.make_async_copy(held.at[s], outs[s], sems.at[1, s]) for s in range(videos)]
    for read in reads:
        read.start()
    first.wait()
    place = lane_places(coords_ref, tok_rows).astype(BF16)
    for s in range(videos):
        held[s, :, width:] = place
    for read, write in zip(reads, writes):
        read.wait()
        write.start()
    for write in writes:
        write.wait()


def key_kernel(k_hbm, gain_hbm, coords_hbm, out_hbm, k_ref, gain_ref, coords_ref, done_ref, sems):
    videos, tok_rows, width = k_hbm.shape
    pairs = out_hbm.shape[2] // DH
    groups = out_hbm.shape[0] // videos
    reads = [
        pltpu.make_async_copy(source, place, sems.at[i])
        for i, (source, place) in enumerate(
            ((coords_hbm, coords_ref), (k_hbm, k_ref), (gain_hbm, gain_ref))
        )
    ]
    for read in reads:
        read.start()
    for read in reads:
        read.wait()
    tables = rope_tables(lane_places(coords_ref, tok_rows))
    writes = []
    for video in range(videos):
        for head, y in normed_heads(k_ref[video].astype(F32), gain_ref, tables):
            start = head % pairs * DH
            done_ref[video * groups + head // pairs, :, start : start + DH] = y
        part = pl.ds(video * groups, groups)
        writes.append(pltpu.make_async_copy(done_ref.at[part], out_hbm.at[part], sems.at[3 + video]))
        writes[-1].start()
    for write in writes:
        write.wait()


def turn_kernel(gain_ref, *refs):
    got, out_ref = in_order(refs[:-1]), refs[-1]
    videos, tok_rows, width = out_ref.shape
    place = jnp.concatenate([ref[:, width:].astype(F32) for ref in got], axis=0)
    tables = rope_tables(place)
    for s in range(videos):
        mine = [table[s * tok_rows : (s + 1) * tok_rows] for table in tables]
        for head, y in normed_heads(got[s][:, :width].astype(F32), gain_ref, mine):
            out_ref[s, :, head * DH : (head + 1) * DH] = y


def query_kernel(q_ref, gain_ref, coords_ref, out_ref):
    videos, tok_rows, _ = q_ref.shape
    tables = rope_tables(lane_places(coords_ref, tok_rows))
    for video in range(videos):
        for head, y in normed_heads(q_ref[video].astype(F32), gain_ref, tables):
            out_ref[video, :, head * DH : (head + 1) * DH] = y


def softmax_parts(scores):
    top = jnp.max(scores, axis=-1, keepdims=True)
    weights = jnp.exp(scores - top)
    total = jnp.sum(weights, axis=-1, keepdims=True)
    return weights.astype(BF16), 1.0 / total, top + jnp.log(total)


def stacked(refs, lanes):
    rows = [ref[:, lanes].astype(F32) for ref in refs]
    return jnp.concatenate(rows, axis=0).astype(BF16)


def fresh_kernel(groups, videos, query_ref, key_ref, value_ref, out_ref, log_ref):
    me = lax.axis_index("patch")
    own, mine = me // groups, me % groups
    queries = [query_ref.at[own ^ s] for s in range(videos)]
    _, tok_rows, width = out_ref.shape
    span = width // groups
    pairs = span // DH
    rows = videos * tok_rows
    scale = 1.0 / math.sqrt(DH)
    shape = (pairs * rows, rows)
    same = lax.broadcasted_iota(jnp.int32, shape, 0) % rows // tok_rows == (
        lax.broadcasted_iota(jnp.int32, shape, 1) // tok_rows
    )
    lane = lax.broadcasted_iota(jnp.int32, (rows, DH), 1)
    logs = jnp.zeros((rows, DH), F32)
    for t in range(groups):
        lanes = pl.ds(pl.multiple_of((mine ^ t) * span, DH), span)
        query = stacked(queries, lanes)
        key = stacked([key_ref.at[me ^ (s * groups) ^ t] for s in range(videos)], slice(None))
        value = stacked([value_ref.at[own ^ s] for s in range(videos)], lanes)
        scores = jnp.concatenate(
            [
                lax.dot_general(
                    query[:, pair * DH : (pair + 1) * DH],
                    key[:, pair * DH : (pair + 1) * DH],
                    TRANSPOSED,
                    preferred_element_type=F32,
                )
                for pair in range(pairs)
            ],
            axis=0,
        )
        weights, inverse, log = softmax_parts(jnp.where(same, scores * scale, -jnp.inf))
        for pair in range(pairs):
            here = slice(pair * rows, (pair + 1) * rows)
            head = t * pairs + pair
            result = inverse[here] * jnp.dot(
                weights[here],
                value[:, pair * DH : (pair + 1) * DH],
                preferred_element_type=F32,
            )
            logs = jnp.where(lane == head, log[here], logs)
            for s in range(videos):
                out_ref[s, :, head * DH : (head + 1) * DH] = result[s * tok_rows : (s + 1) * tok_rows]
    for s in range(videos):
        log_ref[s] = logs[s * tok_rows : (s + 1) * tok_rows]


def stale_kernel(groups, videos, query_ref, *refs):
    queries = [query_ref.at[s] for s in range(videos)]
    pieces, outs = refs[:groups], refs[groups:]
    me = lax.axis_index("patch")
    mine = me % groups
    pairs, total_rows, _ = pieces[0].shape
    tok_rows, width = queries[0].shape
    span = pairs * DH
    rows = videos * tok_rows
    scale = 1.0 / math.sqrt(DH)
    shape = (pairs * rows, total_rows)
    patch = (lax.broadcasted_iota(jnp.int32, shape, 0) % rows // tok_rows * groups) ^ me
    own = patch == lax.broadcasted_iota(jnp.int32, shape, 1) // tok_rows
    lane = lax.broadcasted_iota(jnp.int32, (rows, DH), 1)
    logs = jnp.zeros((rows, DH), F32)
    for t in range(groups):
        start = pl.multiple_of((mine ^ t) * span, DH)
        query = stacked(queries, pl.ds(start, span))
        scores = jnp.concatenate(
            [
                lax.dot_general(
                    query[:, pair * DH : (pair + 1) * DH],
                    pieces[t][pair, :, :DH],
                    TRANSPOSED,
                    preferred_element_type=F32,
                )
                for pair in range(pairs)
            ],
            axis=0,
        )
        weights, inverse, log = softmax_parts(jnp.where(own, -jnp.inf, scores * scale))
        results = []
        for pair in range(pairs):
            here = slice(pair * rows, (pair + 1) * rows)
            results.append(
                inverse[here]
                * jnp.dot(weights[here], pieces[t][pair, :, DH:], preferred_element_type=F32)
            )
            logs = jnp.where(lane == t * pairs + pair, log[here], logs)
        result = jnp.concatenate(results, axis=1).astype(BF16)
        for s in range(videos):
            outs[s][:, t * span : (t + 1) * span] = result[s * tok_rows : (s + 1) * tok_rows]
    high = logs.astype(BF16).astype(F32)
    middle = (logs - high).astype(BF16).astype(F32)
    low = (logs - high - middle).astype(BF16).astype(F32)
    heads = groups * pairs
    terms = (high + pltpu.roll(middle, heads, 1) + pltpu.roll(low, 2 * heads, 1)).astype(BF16)
    for s in range(videos):
        outs[s][:, width:] = terms[s * tok_rows : (s + 1) * tok_rows]


def join_kernel(groups, videos, *refs):
    back = in_order(refs[:videos])
    fresh_ref, log_ref, out_ref, done_ref, sems = refs[videos:]
    me = lax.axis_index("patch")
    own, mine = me // groups, me % groups
    _, tok_rows, width = fresh_ref.shape
    heads = width // DH
    pairs = heads // groups
    span = pairs * DH
    copies = []
    for s in range(videos):
        terms = back[s][:, width:].astype(F32)
        stale_log = terms + pltpu.roll(terms, DH - heads, 1) + pltpu.roll(terms, DH - 2 * heads, 1)
        share = 1.0 / (1.0 + jnp.exp(stale_log - log_ref[s]))
        for t in range(groups):
            parts = []
            for pair in range(pairs):
                head = t * pairs + pair
                here = slice(head * DH, (head + 1) * DH)
                stale = back[s][:, here].astype(F32)
                parts.append(stale + share[:, head : head + 1] * (fresh_ref[s, :, here] - stale))
            lanes = pl.ds(pl.multiple_of((mine ^ t) * span, DH), span)
            done_ref[s, :, lanes] = jnp.concatenate(parts, axis=1).astype(BF16)
        copies.append(pltpu.make_async_copy(done_ref.at[s], out_ref.at[own ^ s], sems.at[s]))
        copies[-1].start()
    for copy in copies:
        copy.wait()


def cache_kernel(key_ref, value_ref, out_ref, sems):
    copies = []
    for pair in range(out_ref.shape[0]):
        for part, source in enumerate((key_ref.at[:, :, pl.ds(pair * DH, DH)], value_ref.at[:, pair])):
            target = out_ref.at[pair, :, :, pl.ds(part * DH, DH)]
            copies.append(pltpu.make_async_copy(source, target, sems.at[part, pair]))
            copies[-1].start()
    for copy in copies:
        copy.wait()


def permuted(array, offset, patches):
    return lax.ppermute(array, "patch", [(i, i ^ offset) for i in range(patches)])


def far_first(arrays):
    half = len(arrays) // 2
    return [*arrays[half:], *arrays[1:half], arrays[0]]


def in_order(arrays):
    half = len(arrays) // 2
    return [arrays[-1], *arrays[half:-1], *arrays[:half]]


def exchange(arrays, stride, patches):
    return [arrays[0]] + [
        permuted(arrays[s], s * stride, patches) for s in range(1, len(arrays))
    ]


def local(queries, keys, values, q_gain, k_gain, stale_cache, coords):
    videos, tok_rows, width = queries.shape
    pairs_here, total_rows, _ = stale_cache.shape
    patches = total_rows // tok_rows
    groups = patches // videos

    def kernel(body, name, limit, cost=0, **kwargs):
        return pl.pallas_call(
            body,
            name=name,
            compiler_params=pltpu.CompilerParams(vmem_limit_bytes=limit * MIB),
            cost_estimate=pl.CostEstimate(flops=cost, bytes_accessed=0, transcendentals=0),
            **kwargs,
        )

    gains = q_gain.reshape(1, width), k_gain.reshape(1, width)
    sent = kernel(
        functools.partial(lay_kernel, groups),
        "lay",
        56,
        out_shape=[jax.ShapeDtypeStruct((tok_rows, width + DH), BF16)] * videos,
        in_specs=[HBM] * 2,
        out_specs=[HBM] * videos,
        scratch_shapes=[
            pltpu.VMEM((videos, tok_rows, width + DH), BF16),
            pltpu.SMEM(coords.shape, jnp.int32),
            pltpu.SemaphoreType.DMA((2, videos)),
            pltpu.SemaphoreType.DMA,
        ],
    )(queries, coords)
    stale_sent, kept = lax.optimization_barrier((stale_cache, sent[0]))
    pieces = {0: stale_cache}
    bit = groups // 2
    pieces[bit] = permuted(stale_sent, bit, patches)
    query_raw = far_first(exchange([kept, *sent[1:]], groups, patches))
    value_sent = jnp.transpose(values.reshape(videos, tok_rows, width // DH, DH), (0, 2, 1, 3))
    value_got = lax.all_to_all(
        value_sent.reshape(patches, pairs_here, tok_rows, DH), "patch", split_axis=0, concat_axis=0, tiled=True
    )
    key = kernel(
        key_kernel,
        "key",
        56,
        out_shape=jax.ShapeDtypeStruct((patches, tok_rows, pairs_here * DH), BF16),
        in_specs=[HBM] * 3,
        out_specs=HBM,
        scratch_shapes=[
            pltpu.VMEM(keys.shape, BF16),
            pltpu.VMEM((1, width), F32),
            pltpu.SMEM(coords.shape, jnp.int32),
            pltpu.VMEM((patches, tok_rows, pairs_here * DH), BF16),
            pltpu.SemaphoreType.DMA((3 + videos,)),
        ],
    )(keys, gains[1], coords)
    key_sent, value_got = lax.optimization_barrier((key, value_got))
    key_got = lax.all_to_all(key_sent, "patch", split_axis=0, concat_axis=0, tiled=True)
    query_raw, pieces, key = lax.optimization_barrier((query_raw, pieces, key))
    query_got = kernel(
        turn_kernel,
        "turn",
        16,
        cost=10**12,
        out_shape=jax.ShapeDtypeStruct(queries.shape, BF16),
        in_specs=[VMEM] * (1 + videos),
        out_specs=VMEM,
    )(gains[0], *query_raw)
    pieces, query_got = lax.optimization_barrier((pieces, query_got))
    while bit > 1:
        bit //= 2
        pieces.update({t | bit: permuted(piece, bit, patches) for t, piece in list(pieces.items())})
    result = kernel(
        functools.partial(stale_kernel, groups, videos),
        "stale",
        32,
        out_shape=[jax.ShapeDtypeStruct((tok_rows, width + DH), BF16)] * videos,
        in_specs=[VMEM] * (1 + groups),
        out_specs=[VMEM] * videos,
    )(query_got, *[pieces[t] for t in range(groups)])
    result, key_late, queries_late = lax.optimization_barrier((result, key, queries))
    query = kernel(
        query_kernel,
        "query",
        16,
        out_shape=jax.ShapeDtypeStruct(queries.shape, BF16),
        in_specs=[VMEM] * 2 + [SMEM],
        out_specs=VMEM,
    )(queries_late, gains[0], coords)
    back = far_first(exchange(result, groups, patches))
    fresh_sum, fresh_log = kernel(
        functools.partial(fresh_kernel, groups, videos),
        "fresh",
        16,
        out_shape=(
            jax.ShapeDtypeStruct((videos, tok_rows, width), F32),
            jax.ShapeDtypeStruct((videos, tok_rows, DH), F32),
        ),
        in_specs=[VMEM] * 3,
        out_specs=(VMEM, VMEM),
    )(query, key_late, values)
    next_cache = kernel(
        cache_kernel,
        "cache",
        16,
        out_shape=jax.ShapeDtypeStruct((pairs_here, patches, tok_rows, 2 * DH), BF16),
        in_specs=[VMEM, VMEM],
        out_specs=HBM,
        scratch_shapes=[pltpu.SemaphoreType.DMA((2, pairs_here))],
    )(key_got, value_got)
    attended = kernel(
        functools.partial(join_kernel, groups, videos),
        "join",
        16,
        out_shape=jax.ShapeDtypeStruct(queries.shape, BF16),
        in_specs=[VMEM] * (videos + 2),
        out_specs=HBM,
        scratch_shapes=[
            pltpu.VMEM(queries.shape, BF16),
            pltpu.SemaphoreType.DMA((videos,)),
        ],
    )(*back, fresh_sum, fresh_log)
    return (attended, next_cache.reshape(stale_cache.shape))


def solution(mesh):
    in_specs = (
        P("req", "patch", None),
        P("req", "patch", None),
        P("req", "patch", None),
        P(),
        P(),
        P(("req", "patch"), None, None),
        P(None, "patch"),
    )
    out_specs = (P("req", "patch", None), P(("req", "patch"), None, None))
    return jax.shard_map(local, mesh=mesh, in_specs=in_specs, out_specs=out_specs, check_vma=False)
```

```python
import functools
import math

import jax
import jax.numpy as jnp
from jax import lax
from jax.experimental import pallas as pl
from jax.experimental.pallas import tpu as pltpu
from jax.sharding import PartitionSpec as P

DH = 128
VMEM = pl.BlockSpec(memory_space=pltpu.VMEM)
HBM = pl.BlockSpec(memory_space=pltpu.HBM)
SMEM = pl.BlockSpec(memory_space=pltpu.SMEM)
MIB = 1024 * 1024
BF16 = jnp.bfloat16
F32 = jnp.float32
TRANSPOSED = (((1,), (1,)), ((), ()))


def lane_axis(shape):
    side = DH // 6
    first = DH // 2 - 2 * side
    pair = lax.broadcasted_iota(jnp.int32, shape, 1) // 2
    return pair, (pair >= first).astype(jnp.int32) + (pair >= first + side).astype(jnp.int32)


def lane_places(coords_ref, tok_rows):
    shape = (tok_rows, DH)
    row = lax.broadcasted_iota(jnp.int32, shape, 0)
    _, axis = lane_axis(shape)
    place = jnp.zeros(shape, jnp.int32)
    for which in range(3):
        for token in range(tok_rows):
            place = jnp.where((axis == which) & (row == token), coords_ref[which, token], place)
    return place.astype(F32)


def rope_tables(place):
    side = DH // 6
    first = DH // 2 - 2 * side
    pair, axis = lane_axis(place.shape)
    step = jnp.where(axis == 0, pair, jnp.where(axis == 1, pair - first, pair - first - side))
    count = jnp.where(axis == 0, float(first), float(side))
    angle = place * jnp.exp(step.astype(F32) / count * (-math.log(10000.0)))
    sine = jnp.sin(angle)
    even = lax.broadcasted_iota(jnp.int32, place.shape, 1) % 2 == 0
    return jnp.cos(angle), jnp.where(even, -sine, 0.0), jnp.where(even, 0.0, sine)


def normed_heads(wide, gain_ref, tables):
    cosine, sine_even, sine_odd = tables
    width = wide.shape[-1]
    meansq = jnp.sum(wide * wide, axis=-1, keepdims=True) * (1.0 / width)
    inverse = lax.rsqrt(meansq + 1e-06)
    for head in range(width // DH):
        here = slice(head * DH, (head + 1) * DH)
        y = wide[:, here] * inverse * gain_ref[:, here]
        y = y * cosine + pltpu.roll(y, DH - 1, 1) * sine_even + pltpu.roll(y, 1, 1) * sine_odd
        yield head, y.astype(BF16)


def lay_kernel(groups, q_hbm, coords_hbm, *refs):
    videos, tok_rows, width = q_hbm.shape
    outs, (held, coords_ref, sems, coords_sem) = refs[:videos], refs[videos:]
    own = lax.axis_index("patch") // groups
    first = pltpu.make_async_copy(coords_hbm, coords_ref, coords_sem)
    first.start()
    reads = [
        pltpu.make_async_copy(q_hbm.at[own ^ s], held.at[s, :, pl.ds(0, width)], sems.at[0, s])
        for s in range(videos)
    ]
    writes = [pltpu.make_async_copy(held.at[s], outs[s], sems.at[1, s]) for s in range(videos)]
    for read in reads:
        read.start()
    first.wait()
    place = lane_places(coords_ref, tok_rows).astype(BF16)
    for s in range(videos):
        held[s, :, width:] = place
    for read, write in zip(reads, writes):
        read.wait()
        write.start()
    for write in writes:
        write.wait()


def key_kernel(k_hbm, v_hbm, gain_hbm, coords_hbm, out_hbm, k_ref, v_ref, gain_ref, coords_ref, done_ref, sems):
    videos, tok_rows, width = k_hbm.shape
    pairs = out_hbm.shape[2] // (2 * DH)
    groups = out_hbm.shape[0] // videos
    sources, places = (coords_hbm, k_hbm, gain_hbm, v_hbm), (coords_ref, k_ref, gain_ref, v_ref)
    reads = [
        pltpu.make_async_copy(source, place, sems.at[i])
        for i, (source, place) in enumerate(zip(sources, places))
    ]
    for read in reads:
        read.start()
    for read in reads:
        read.wait()
    tables = rope_tables(lane_places(coords_ref, tok_rows))
    writes = []
    for video in range(videos):
        for head, y in normed_heads(k_ref[video].astype(F32), gain_ref, tables):
            target, start = video * groups + head // pairs, head % pairs * 2 * DH
            done_ref[target, :, start : start + DH] = y
            done_ref[target, :, start + DH : start + 2 * DH] = v_ref[
                video, :, head * DH : (head + 1) * DH
            ]
        part = pl.ds(video * groups, groups)
        writes.append(pltpu.make_async_copy(done_ref.at[part], out_hbm.at[part], sems.at[4 + video]))
        writes[-1].start()
    for write in writes:
        write.wait()


def turn_kernel(gain_ref, *refs):
    got, out_ref = in_order(refs[:-1]), refs[-1]
    videos, tok_rows, width = out_ref.shape
    place = jnp.concatenate([ref[:, width:].astype(F32) for ref in got], axis=0)
    tables = rope_tables(place)
    for s in range(videos):
        mine = [table[s * tok_rows : (s + 1) * tok_rows] for table in tables]
        for head, y in normed_heads(got[s][:, :width].astype(F32), gain_ref, mine):
            out_ref[s, :, head * DH : (head + 1) * DH] = y


def query_kernel(q_ref, gain_ref, coords_ref, out_ref):
    videos, tok_rows, _ = q_ref.shape
    tables = rope_tables(lane_places(coords_ref, tok_rows))
    for video in range(videos):
        for head, y in normed_heads(q_ref[video].astype(F32), gain_ref, tables):
            out_ref[video, :, head * DH : (head + 1) * DH] = y


def softmax_parts(scores):
    top = jnp.max(scores, axis=-1, keepdims=True)
    weights = jnp.exp(scores - top)
    total = jnp.sum(weights, axis=-1, keepdims=True)
    return weights.astype(BF16), 1.0 / total, top + jnp.log(total)


def stacked(refs, lanes):
    rows = [ref[:, lanes].astype(F32) for ref in refs]
    return jnp.concatenate(rows, axis=0).astype(BF16)


def fresh_kernel(groups, videos, query_ref, fresh_ref, out_ref, log_ref):
    me = lax.axis_index("patch")
    own, mine = me // groups, me % groups
    queries = [query_ref.at[own ^ s] for s in range(videos)]
    _, tok_rows, width = out_ref.shape
    span = width // groups
    pairs = span // DH
    rows = videos * tok_rows
    scale = 1.0 / math.sqrt(DH)
    shape = (pairs * rows, rows)
    same = lax.broadcasted_iota(jnp.int32, shape, 0) % rows // tok_rows == (
        lax.broadcasted_iota(jnp.int32, shape, 1) // tok_rows
    )
    lane = lax.broadcasted_iota(jnp.int32, (rows, DH), 1)
    logs = jnp.zeros((rows, DH), F32)
    for t in range(groups):
        lanes = pl.ds(pl.multiple_of((mine ^ t) * span, DH), span)
        query = stacked(queries, lanes)
        fresh = stacked([fresh_ref.at[me ^ (s * groups) ^ t] for s in range(videos)], slice(None))
        scores = jnp.concatenate(
            [
                lax.dot_general(
                    query[:, pair * DH : (pair + 1) * DH],
                    fresh[:, 2 * pair * DH : (2 * pair + 1) * DH],
                    TRANSPOSED,
                    preferred_element_type=F32,
                )
                for pair in range(pairs)
            ],
            axis=0,
        )
        weights, inverse, log = softmax_parts(jnp.where(same, scores * scale, -jnp.inf))
        for pair in range(pairs):
            here = slice(pair * rows, (pair + 1) * rows)
            head = t * pairs + pair
            result = inverse[here] * jnp.dot(
                weights[here],
                fresh[:, (2 * pair + 1) * DH : (2 * pair + 2) * DH],
                preferred_element_type=F32,
            )
            logs = jnp.where(lane == head, log[here], logs)
            for s in range(videos):
                out_ref[s, :, head * DH : (head + 1) * DH] = result[s * tok_rows : (s + 1) * tok_rows]
    for s in range(videos):
        log_ref[s] = logs[s * tok_rows : (s + 1) * tok_rows]


def stale_kernel(groups, videos, query_ref, *refs):
    queries = [query_ref.at[s] for s in range(videos)]
    pieces, outs = refs[:groups], refs[groups:]
    me = lax.axis_index("patch")
    mine = me % groups
    pairs, total_rows, _ = pieces[0].shape
    tok_rows, width = queries[0].shape
    span = pairs * DH
    rows = videos * tok_rows
    scale = 1.0 / math.sqrt(DH)
    shape = (pairs * rows, total_rows)
    patch = (lax.broadcasted_iota(jnp.int32, shape, 0) % rows // tok_rows * groups) ^ me
    own = patch == lax.broadcasted_iota(jnp.int32, shape, 1) // tok_rows
    lane = lax.broadcasted_iota(jnp.int32, (rows, DH), 1)
    logs = jnp.zeros((rows, DH), F32)
    for t in range(groups):
        start = pl.multiple_of((mine ^ t) * span, DH)
        query = stacked(queries, pl.ds(start, span))
        scores = jnp.concatenate(
            [
                lax.dot_general(
                    query[:, pair * DH : (pair + 1) * DH],
                    pieces[t][pair, :, :DH],
                    TRANSPOSED,
                    preferred_element_type=F32,
                )
                for pair in range(pairs)
            ],
            axis=0,
        )
        weights, inverse, log = softmax_parts(jnp.where(own, -jnp.inf, scores * scale))
        results = []
        for pair in range(pairs):
            here = slice(pair * rows, (pair + 1) * rows)
            results.append(
                inverse[here]
                * jnp.dot(weights[here], pieces[t][pair, :, DH:], preferred_element_type=F32)
            )
            logs = jnp.where(lane == t * pairs + pair, log[here], logs)
        result = jnp.concatenate(results, axis=1).astype(BF16)
        for s in range(videos):
            outs[s][:, t * span : (t + 1) * span] = result[s * tok_rows : (s + 1) * tok_rows]
    high = logs.astype(BF16).astype(F32)
    middle = (logs - high).astype(BF16).astype(F32)
    low = (logs - high - middle).astype(BF16).astype(F32)
    heads = groups * pairs
    terms = (high + pltpu.roll(middle, heads, 1) + pltpu.roll(low, 2 * heads, 1)).astype(BF16)
    for s in range(videos):
        outs[s][:, width:] = terms[s * tok_rows : (s + 1) * tok_rows]


def join_kernel(groups, videos, *refs):
    back = in_order(refs[:videos])
    fresh_ref, log_ref, out_ref, done_ref, sems = refs[videos:]
    me = lax.axis_index("patch")
    own, mine = me // groups, me % groups
    _, tok_rows, width = fresh_ref.shape
    heads = width // DH
    pairs = heads // groups
    span = pairs * DH
    copies = []
    for s in range(videos):
        terms = back[s][:, width:].astype(F32)
        stale_log = terms + pltpu.roll(terms, DH - heads, 1) + pltpu.roll(terms, DH - 2 * heads, 1)
        share = 1.0 / (1.0 + jnp.exp(stale_log - log_ref[s]))
        for t in range(groups):
            parts = []
            for pair in range(pairs):
                head = t * pairs + pair
                here = slice(head * DH, (head + 1) * DH)
                stale = back[s][:, here].astype(F32)
                parts.append(stale + share[:, head : head + 1] * (fresh_ref[s, :, here] - stale))
            lanes = pl.ds(pl.multiple_of((mine ^ t) * span, DH), span)
            done_ref[s, :, lanes] = jnp.concatenate(parts, axis=1).astype(BF16)
        copies.append(pltpu.make_async_copy(done_ref.at[s], out_ref.at[own ^ s], sems.at[s]))
        copies[-1].start()
    for copy in copies:
        copy.wait()


def cache_kernel(got_ref, out_ref, sems):
    copies = []
    for pair in range(out_ref.shape[0]):
        lanes = pl.ds(2 * pair * DH, 2 * DH)
        copies.append(
            pltpu.make_async_copy(got_ref.at[:, :, lanes], out_ref.at[pair], sems.at[pair])
        )
        copies[-1].start()
    for copy in copies:
        copy.wait()


def permuted(array, offset, patches):
    return lax.ppermute(array, "patch", [(i, i ^ offset) for i in range(patches)])


def far_first(arrays):
    half = len(arrays) // 2
    return [*arrays[half:], *arrays[1:half], arrays[0]]


def in_order(arrays):
    half = len(arrays) // 2
    return [arrays[-1], *arrays[half:-1], *arrays[:half]]


def exchange(arrays, stride, patches):
    return [arrays[0]] + [
        permuted(arrays[s], s * stride, patches) for s in range(1, len(arrays))
    ]


def local(queries, keys, values, q_gain, k_gain, stale_cache, coords):
    videos, tok_rows, width = queries.shape
    pairs_here, total_rows, _ = stale_cache.shape
    patches = total_rows // tok_rows
    groups = patches // videos

    def kernel(body, name, limit, cost=0, **kwargs):
        return pl.pallas_call(
            body,
            name=name,
            compiler_params=pltpu.CompilerParams(vmem_limit_bytes=limit * MIB),
            cost_estimate=pl.CostEstimate(flops=cost, bytes_accessed=0, transcendentals=0),
            **kwargs,
        )

    gains = q_gain.reshape(1, width), k_gain.reshape(1, width)
    sent = kernel(
        functools.partial(lay_kernel, groups),
        "lay",
        56,
        out_shape=[jax.ShapeDtypeStruct((tok_rows, width + DH), BF16)] * videos,
        in_specs=[HBM] * 2,
        out_specs=[HBM] * videos,
        scratch_shapes=[
            pltpu.VMEM((videos, tok_rows, width + DH), BF16),
            pltpu.SMEM(coords.shape, jnp.int32),
            pltpu.SemaphoreType.DMA((2, videos)),
            pltpu.SemaphoreType.DMA,
        ],
    )(queries, coords)
    stale_sent, kept = lax.optimization_barrier((stale_cache, sent[0]))
    pieces = {0: stale_cache}
    bit = groups // 2
    pieces[bit] = permuted(stale_sent, bit, patches)
    query_raw = far_first(exchange([kept, *sent[1:]], groups, patches))
    fresh = kernel(
        key_kernel,
        "key",
        56,
        out_shape=jax.ShapeDtypeStruct((patches, tok_rows, 2 * pairs_here * DH), BF16),
        in_specs=[HBM] * 4,
        out_specs=HBM,
        scratch_shapes=[
            pltpu.VMEM(keys.shape, BF16),
            pltpu.VMEM(keys.shape, BF16),
            pltpu.VMEM((1, width), F32),
            pltpu.SMEM(coords.shape, jnp.int32),
            pltpu.VMEM((patches, tok_rows, 2 * pairs_here * DH), BF16),
            pltpu.SemaphoreType.DMA((4 + videos,)),
        ],
    )(keys, values, gains[1], coords)
    cached = lax.all_to_all(fresh, "patch", split_axis=0, concat_axis=0, tiled=True)
    query_raw, pieces, fresh = lax.optimization_barrier((query_raw, pieces, fresh))
    query_got = kernel(
        turn_kernel,
        "turn",
        16,
        cost=10**12,
        out_shape=jax.ShapeDtypeStruct(queries.shape, BF16),
        in_specs=[VMEM] * (1 + videos),
        out_specs=VMEM,
    )(gains[0], *query_raw)
    pieces, query_got = lax.optimization_barrier((pieces, query_got))
    while bit > 1:
        bit //= 2
        pieces.update({t | bit: permuted(piece, bit, patches) for t, piece in list(pieces.items())})
    result = kernel(
        functools.partial(stale_kernel, groups, videos),
        "stale",
        32,
        out_shape=[jax.ShapeDtypeStruct((tok_rows, width + DH), BF16)] * videos,
        in_specs=[VMEM] * (1 + groups),
        out_specs=[VMEM] * videos,
    )(query_got, *[pieces[t] for t in range(groups)])
    result, fresh_late, queries_late = lax.optimization_barrier((result, fresh, queries))
    query = kernel(
        query_kernel,
        "query",
        16,
        out_shape=jax.ShapeDtypeStruct(queries.shape, BF16),
        in_specs=[VMEM] * 2 + [SMEM],
        out_specs=VMEM,
    )(queries_late, gains[0], coords)
    back = far_first(exchange(result, groups, patches))
    fresh_sum, fresh_log = kernel(
        functools.partial(fresh_kernel, groups, videos),
        "fresh",
        16,
        out_shape=(
            jax.ShapeDtypeStruct((videos, tok_rows, width), F32),
            jax.ShapeDtypeStruct((videos, tok_rows, DH), F32),
        ),
        in_specs=[VMEM] * 2,
        out_specs=(VMEM, VMEM),
    )(query, fresh_late)
    fresh_sum, cached = lax.optimization_barrier((fresh_sum, cached))
    next_cache = kernel(
        cache_kernel,
        "cache",
        16,
        out_shape=jax.ShapeDtypeStruct((pairs_here, patches, tok_rows, 2 * DH), BF16),
        in_specs=[VMEM],
        out_specs=HBM,
        scratch_shapes=[pltpu.SemaphoreType.DMA((pairs_here,))],
    )(cached)
    attended = kernel(
        functools.partial(join_kernel, groups, videos),
        "join",
        16,
        out_shape=jax.ShapeDtypeStruct(queries.shape, BF16),
        in_specs=[VMEM] * (videos + 2),
        out_specs=HBM,
        scratch_shapes=[
            pltpu.VMEM(queries.shape, BF16),
            pltpu.SemaphoreType.DMA((videos,)),
        ],
    )(*back, fresh_sum, fresh_log)
    return (attended, next_cache.reshape(stale_cache.shape))


def solution(mesh):
    in_specs = (
        P("req", "patch", None),
        P("req", "patch", None),
        P("req", "patch", None),
        P(),
        P(),
        P(("req", "patch"), None, None),
        P(None, "patch"),
    )
    out_specs = (P("req", "patch", None), P(("req", "patch"), None, None))
    return jax.shard_map(local, mesh=mesh, in_specs=in_specs, out_specs=out_specs, check_vma=False)
```

```python
import functools
import math

import jax
import jax.numpy as jnp
from jax import lax
from jax.experimental import pallas as pl
from jax.experimental.pallas import tpu as pltpu
from jax.sharding import PartitionSpec as P

DH = 128
VMEM = pl.BlockSpec(memory_space=pltpu.VMEM)
HBM = pl.BlockSpec(memory_space=pltpu.HBM)
SMEM = pl.BlockSpec(memory_space=pltpu.SMEM)
MIB = 1024 * 1024
BF16 = jnp.bfloat16
F32 = jnp.float32
TRANSPOSED = (((1,), (1,)), ((), ()))


def lane_axis(shape):
    side = DH // 6
    first = DH // 2 - 2 * side
    pair = lax.broadcasted_iota(jnp.int32, shape, 1) // 2
    return pair, (pair >= first).astype(jnp.int32) + (pair >= first + side).astype(jnp.int32)


def lane_places(coords_ref, tok_rows):
    shape = (tok_rows, DH)
    row = lax.broadcasted_iota(jnp.int32, shape, 0)
    _, axis = lane_axis(shape)
    place = jnp.zeros(shape, jnp.int32)
    for which in range(3):
        for token in range(tok_rows):
            place = jnp.where((axis == which) & (row == token), coords_ref[which, token], place)
    return place.astype(F32)


def rope_tables(place):
    side = DH // 6
    first = DH // 2 - 2 * side
    pair, axis = lane_axis(place.shape)
    step = jnp.where(axis == 0, pair, jnp.where(axis == 1, pair - first, pair - first - side))
    count = jnp.where(axis == 0, float(first), float(side))
    angle = place * jnp.exp(step.astype(F32) / count * (-math.log(10000.0)))
    sine = jnp.sin(angle)
    even = lax.broadcasted_iota(jnp.int32, place.shape, 1) % 2 == 0
    return jnp.cos(angle), jnp.where(even, -sine, 0.0), jnp.where(even, 0.0, sine)


def normed_heads(wide, gain_ref, tables):
    cosine, sine_even, sine_odd = tables
    width = wide.shape[-1]
    meansq = jnp.sum(wide * wide, axis=-1, keepdims=True) * (1.0 / width)
    inverse = lax.rsqrt(meansq + 1e-06)
    for head in range(width // DH):
        here = slice(head * DH, (head + 1) * DH)
        y = wide[:, here] * inverse * gain_ref[:, here]
        y = y * cosine + pltpu.roll(y, DH - 1, 1) * sine_even + pltpu.roll(y, 1, 1) * sine_odd
        yield head, y.astype(BF16)


def lay_kernel(groups, q_hbm, coords_hbm, *refs):
    videos, tok_rows, width = q_hbm.shape
    outs, (held, coords_ref, sems, coords_sem) = refs[:videos], refs[videos:]
    own = lax.axis_index("patch") // groups
    first = pltpu.make_async_copy(coords_hbm, coords_ref, coords_sem)
    first.start()
    reads = [
        pltpu.make_async_copy(q_hbm.at[own ^ s], held.at[s, :, pl.ds(0, width)], sems.at[0, s])
        for s in range(videos)
    ]
    writes = [pltpu.make_async_copy(held.at[s], outs[s], sems.at[1, s]) for s in range(videos)]
    for read in reads:
        read.start()
    first.wait()
    place = lane_places(coords_ref, tok_rows).astype(BF16)
    for s in range(videos):
        held[s, :, width:] = place
    for read, write in zip(reads, writes):
        read.wait()
        write.start()
    for write in writes:
        write.wait()


def key_kernel(k_hbm, v_hbm, gain_hbm, coords_hbm, out_hbm, k_ref, v_ref, gain_ref, coords_ref, done_ref, sems):
    videos, tok_rows, width = k_hbm.shape
    pairs = out_hbm.shape[2] // (2 * DH)
    groups = out_hbm.shape[0] // videos
    sources, places = (coords_hbm, k_hbm, gain_hbm, v_hbm), (coords_ref, k_ref, gain_ref, v_ref)
    reads = [
        pltpu.make_async_copy(source, place, sems.at[i])
        for i, (source, place) in enumerate(zip(sources, places))
    ]
    for read in reads:
        read.start()
    for read in reads:
        read.wait()
    tables = rope_tables(lane_places(coords_ref, tok_rows))
    writes = []
    for video in range(videos):
        for head, y in normed_heads(k_ref[video].astype(F32), gain_ref, tables):
            target, start = video * groups + head // pairs, head % pairs * 2 * DH
            done_ref[target, :, start : start + DH] = y
            done_ref[target, :, start + DH : start + 2 * DH] = v_ref[
                video, :, head * DH : (head + 1) * DH
            ]
        part = pl.ds(video * groups, groups)
        writes.append(pltpu.make_async_copy(done_ref.at[part], out_hbm.at[part], sems.at[4 + video]))
        writes[-1].start()
    for write in writes:
        write.wait()


def turn_kernel(gain_ref, *refs):
    got, out_ref = in_order(refs[:-1]), refs[-1]
    videos, tok_rows, width = out_ref.shape
    place = jnp.concatenate([ref[:, width:].astype(F32) for ref in got], axis=0)
    tables = rope_tables(place)
    for s in range(videos):
        mine = [table[s * tok_rows : (s + 1) * tok_rows] for table in tables]
        for head, y in normed_heads(got[s][:, :width].astype(F32), gain_ref, mine):
            out_ref[s, :, head * DH : (head + 1) * DH] = y


def query_kernel(q_ref, gain_ref, coords_ref, out_ref):
    videos, tok_rows, _ = q_ref.shape
    tables = rope_tables(lane_places(coords_ref, tok_rows))
    for video in range(videos):
        for head, y in normed_heads(q_ref[video].astype(F32), gain_ref, tables):
            out_ref[video, :, head * DH : (head + 1) * DH] = y


def softmax_parts(scores):
    top = jnp.max(scores, axis=-1, keepdims=True)
    weights = jnp.exp(scores - top)
    total = jnp.sum(weights, axis=-1, keepdims=True)
    return weights.astype(BF16), 1.0 / total, top + jnp.log(total)


def stacked(refs, lanes):
    rows = [ref[:, lanes].astype(F32) for ref in refs]
    return jnp.concatenate(rows, axis=0).astype(BF16)


def fresh_kernel(groups, videos, query_ref, fresh_ref, out_ref, log_ref):
    me = lax.axis_index("patch")
    own, mine = me // groups, me % groups
    queries = [query_ref.at[own ^ s] for s in range(videos)]
    _, tok_rows, width = out_ref.shape
    span = width // groups
    pairs = span // DH
    rows = videos * tok_rows
    scale = 1.0 / math.sqrt(DH)
    shape = (pairs * rows, rows)
    same = lax.broadcasted_iota(jnp.int32, shape, 0) % rows // tok_rows == (
        lax.broadcasted_iota(jnp.int32, shape, 1) // tok_rows
    )
    lane = lax.broadcasted_iota(jnp.int32, (rows, DH), 1)
    logs = jnp.zeros((rows, DH), F32)
    for t in range(groups):
        lanes = pl.ds(pl.multiple_of((mine ^ t) * span, DH), span)
        query = stacked(queries, lanes)
        fresh = stacked([fresh_ref.at[me ^ (s * groups) ^ t] for s in range(videos)], slice(None))
        scores = jnp.concatenate(
            [
                lax.dot_general(
                    query[:, pair * DH : (pair + 1) * DH],
                    fresh[:, 2 * pair * DH : (2 * pair + 1) * DH],
                    TRANSPOSED,
                    preferred_element_type=F32,
                )
                for pair in range(pairs)
            ],
            axis=0,
        )
        weights, inverse, log = softmax_parts(jnp.where(same, scores * scale, -jnp.inf))
        for pair in range(pairs):
            here = slice(pair * rows, (pair + 1) * rows)
            head = t * pairs + pair
            result = inverse[here] * jnp.dot(
                weights[here],
                fresh[:, (2 * pair + 1) * DH : (2 * pair + 2) * DH],
                preferred_element_type=F32,
            )
            logs = jnp.where(lane == head, log[here], logs)
            for s in range(videos):
                out_ref[s, :, head * DH : (head + 1) * DH] = result[s * tok_rows : (s + 1) * tok_rows]
    for s in range(videos):
        log_ref[s] = logs[s * tok_rows : (s + 1) * tok_rows]


def stale_kernel(groups, videos, query_ref, *refs):
    queries = [query_ref.at[s] for s in range(videos)]
    pieces, outs = refs[:groups], refs[groups:]
    me = lax.axis_index("patch")
    mine = me % groups
    pairs, total_rows, _ = pieces[0].shape
    tok_rows, width = queries[0].shape
    span = pairs * DH
    rows = videos * tok_rows
    scale = 1.0 / math.sqrt(DH)
    shape = (pairs * rows, total_rows)
    patch = (lax.broadcasted_iota(jnp.int32, shape, 0) % rows // tok_rows * groups) ^ me
    own = patch == lax.broadcasted_iota(jnp.int32, shape, 1) // tok_rows
    lane = lax.broadcasted_iota(jnp.int32, (rows, DH), 1)
    logs = jnp.zeros((rows, DH), F32)
    for t in range(groups):
        start = pl.multiple_of((mine ^ t) * span, DH)
        query = stacked(queries, pl.ds(start, span))
        scores = jnp.concatenate(
            [
                lax.dot_general(
                    query[:, pair * DH : (pair + 1) * DH],
                    pieces[t][pair, :, :DH],
                    TRANSPOSED,
                    preferred_element_type=F32,
                )
                for pair in range(pairs)
            ],
            axis=0,
        )
        weights, inverse, log = softmax_parts(jnp.where(own, -jnp.inf, scores * scale))
        results = []
        for pair in range(pairs):
            here = slice(pair * rows, (pair + 1) * rows)
            results.append(
                inverse[here]
                * jnp.dot(weights[here], pieces[t][pair, :, DH:], preferred_element_type=F32)
            )
            logs = jnp.where(lane == t * pairs + pair, log[here], logs)
        result = jnp.concatenate(results, axis=1).astype(BF16)
        for s in range(videos):
            outs[s][:, t * span : (t + 1) * span] = result[s * tok_rows : (s + 1) * tok_rows]
    high = logs.astype(BF16).astype(F32)
    middle = (logs - high).astype(BF16).astype(F32)
    low = (logs - high - middle).astype(BF16).astype(F32)
    heads = groups * pairs
    terms = (high + pltpu.roll(middle, heads, 1) + pltpu.roll(low, 2 * heads, 1)).astype(BF16)
    for s in range(videos):
        outs[s][:, width:] = terms[s * tok_rows : (s + 1) * tok_rows]


def join_kernel(groups, videos, *refs):
    back = in_order(refs[:videos])
    fresh_ref, log_ref, out_ref, done_ref, sems = refs[videos:]
    me = lax.axis_index("patch")
    own, mine = me // groups, me % groups
    _, tok_rows, width = fresh_ref.shape
    heads = width // DH
    pairs = heads // groups
    span = pairs * DH
    copies = []
    for s in range(videos):
        terms = back[s][:, width:].astype(F32)
        stale_log = terms + pltpu.roll(terms, DH - heads, 1) + pltpu.roll(terms, DH - 2 * heads, 1)
        share = 1.0 / (1.0 + jnp.exp(stale_log - log_ref[s]))
        for t in range(groups):
            parts = []
            for pair in range(pairs):
                head = t * pairs + pair
                here = slice(head * DH, (head + 1) * DH)
                stale = back[s][:, here].astype(F32)
                parts.append(stale + share[:, head : head + 1] * (fresh_ref[s, :, here] - stale))
            lanes = pl.ds(pl.multiple_of((mine ^ t) * span, DH), span)
            done_ref[s, :, lanes] = jnp.concatenate(parts, axis=1).astype(BF16)
        copies.append(pltpu.make_async_copy(done_ref.at[s], out_ref.at[own ^ s], sems.at[s]))
        copies[-1].start()
    for copy in copies:
        copy.wait()


def cache_kernel(got_ref, out_ref, sems):
    copies = []
    for pair in range(out_ref.shape[0]):
        lanes = pl.ds(2 * pair * DH, 2 * DH)
        copies.append(
            pltpu.make_async_copy(got_ref.at[:, :, lanes], out_ref.at[pair], sems.at[pair])
        )
        copies[-1].start()
    for copy in copies:
        copy.wait()


def permuted(array, offset, patches):
    return lax.ppermute(array, "patch", [(i, i ^ offset) for i in range(patches)])


def far_first(arrays):
    half = len(arrays) // 2
    return [*arrays[half:], *arrays[1:half], arrays[0]]


def in_order(arrays):
    half = len(arrays) // 2
    return [arrays[-1], *arrays[half:-1], *arrays[:half]]


def exchange(arrays, stride, patches):
    return [arrays[0]] + [
        permuted(arrays[s], s * stride, patches) for s in range(1, len(arrays))
    ]


def local(queries, keys, values, q_gain, k_gain, stale_cache, coords):
    videos, tok_rows, width = queries.shape
    pairs_here, total_rows, _ = stale_cache.shape
    patches = total_rows // tok_rows
    groups = patches // videos

    def kernel(body, name, limit, cost=0, **kwargs):
        return pl.pallas_call(
            body,
            name=name,
            compiler_params=pltpu.CompilerParams(vmem_limit_bytes=limit * MIB),
            cost_estimate=pl.CostEstimate(flops=cost, bytes_accessed=0, transcendentals=0),
            **kwargs,
        )

    gains = q_gain.reshape(1, width), k_gain.reshape(1, width)
    sent = kernel(
        functools.partial(lay_kernel, groups),
        "lay",
        56,
        out_shape=[jax.ShapeDtypeStruct((tok_rows, width + DH), BF16)] * videos,
        in_specs=[HBM] * 2,
        out_specs=[HBM] * videos,
        scratch_shapes=[
            pltpu.VMEM((videos, tok_rows, width + DH), BF16),
            pltpu.SMEM(coords.shape, jnp.int32),
            pltpu.SemaphoreType.DMA((2, videos)),
            pltpu.SemaphoreType.DMA,
        ],
    )(queries, coords)
    stale_sent, kept = lax.optimization_barrier((stale_cache, sent[0]))
    pieces = {0: stale_cache}
    bit = groups // 2
    pieces[bit] = permuted(stale_sent, bit, patches)
    query_raw = far_first(exchange([kept, *sent[1:]], groups, patches))
    fresh = kernel(
        key_kernel,
        "key",
        56,
        out_shape=jax.ShapeDtypeStruct((patches, tok_rows, 2 * pairs_here * DH), BF16),
        in_specs=[HBM] * 4,
        out_specs=HBM,
        scratch_shapes=[
            pltpu.VMEM(keys.shape, BF16),
            pltpu.VMEM(keys.shape, BF16),
            pltpu.VMEM((1, width), F32),
            pltpu.SMEM(coords.shape, jnp.int32),
            pltpu.VMEM((patches, tok_rows, 2 * pairs_here * DH), BF16),
            pltpu.SemaphoreType.DMA((4 + videos,)),
        ],
    )(keys, values, gains[1], coords)
    cached = lax.all_to_all(fresh, "patch", split_axis=0, concat_axis=0, tiled=True)
    query_raw, pieces, fresh = lax.optimization_barrier((query_raw, pieces, fresh))
    query_got = kernel(
        turn_kernel,
        "turn",
        16,
        cost=10**11,
        out_shape=jax.ShapeDtypeStruct(queries.shape, BF16),
        in_specs=[VMEM] * (1 + videos),
        out_specs=VMEM,
    )(gains[0], *query_raw)
    pieces, query_got = lax.optimization_barrier((pieces, query_got))
    while bit > 1:
        bit //= 2
        pieces.update({t | bit: permuted(piece, bit, patches) for t, piece in list(pieces.items())})
    result = kernel(
        functools.partial(stale_kernel, groups, videos),
        "stale",
        32,
        out_shape=[jax.ShapeDtypeStruct((tok_rows, width + DH), BF16)] * videos,
        in_specs=[VMEM] * (1 + groups),
        out_specs=[VMEM] * videos,
    )(query_got, *[pieces[t] for t in range(groups)])
    result, fresh_late, queries_late = lax.optimization_barrier((result, fresh, queries))
    query = kernel(
        query_kernel,
        "query",
        16,
        out_shape=jax.ShapeDtypeStruct(queries.shape, BF16),
        in_specs=[VMEM] * 2 + [SMEM],
        out_specs=VMEM,
    )(queries_late, gains[0], coords)
    back = far_first(exchange(result, groups, patches))
    fresh_sum, fresh_log = kernel(
        functools.partial(fresh_kernel, groups, videos),
        "fresh",
        16,
        out_shape=(
            jax.ShapeDtypeStruct((videos, tok_rows, width), F32),
            jax.ShapeDtypeStruct((videos, tok_rows, DH), F32),
        ),
        in_specs=[VMEM] * 2,
        out_specs=(VMEM, VMEM),
    )(query, fresh_late)
    fresh_sum, cached = lax.optimization_barrier((fresh_sum, cached))
    next_cache = kernel(
        cache_kernel,
        "cache",
        16,
        out_shape=jax.ShapeDtypeStruct((pairs_here, patches, tok_rows, 2 * DH), BF16),
        in_specs=[VMEM],
        out_specs=HBM,
        scratch_shapes=[pltpu.SemaphoreType.DMA((pairs_here,))],
    )(cached)
    attended = kernel(
        functools.partial(join_kernel, groups, videos),
        "join",
        16,
        out_shape=jax.ShapeDtypeStruct(queries.shape, BF16),
        in_specs=[VMEM] * (videos + 2),
        out_specs=HBM,
        scratch_shapes=[
            pltpu.VMEM(queries.shape, BF16),
            pltpu.SemaphoreType.DMA((videos,)),
        ],
    )(*back, fresh_sum, fresh_log)
    return (attended, next_cache.reshape(stale_cache.shape))


def solution(mesh):
    in_specs = (
        P("req", "patch", None),
        P("req", "patch", None),
        P("req", "patch", None),
        P(),
        P(),
        P(("req", "patch"), None, None),
        P(None, "patch"),
    )
    out_specs = (P("req", "patch", None), P(("req", "patch"), None, None))
    return jax.shard_map(local, mesh=mesh, in_specs=in_specs, out_specs=out_specs, check_vma=False)
```

```python
import functools
import math

import jax
import jax.numpy as jnp
from jax import lax
from jax.experimental import pallas as pl
from jax.experimental.pallas import tpu as pltpu
from jax.sharding import PartitionSpec as P

DH = 128
VMEM = pl.BlockSpec(memory_space=pltpu.VMEM)
HBM = pl.BlockSpec(memory_space=pltpu.HBM)
SMEM = pl.BlockSpec(memory_space=pltpu.SMEM)
MIB = 1024 * 1024
BF16 = jnp.bfloat16
F32 = jnp.float32
TRANSPOSED = (((1,), (1,)), ((), ()))


def lane_axis(shape):
    side = DH // 6
    first = DH // 2 - 2 * side
    pair = lax.broadcasted_iota(jnp.int32, shape, 1) // 2
    return pair, (pair >= first).astype(jnp.int32) + (pair >= first + side).astype(jnp.int32)


def lane_places(coords_ref, tok_rows):
    shape = (tok_rows, DH)
    row = lax.broadcasted_iota(jnp.int32, shape, 0)
    _, axis = lane_axis(shape)
    place = jnp.zeros(shape, jnp.int32)
    for which in range(3):
        for token in range(tok_rows):
            place = jnp.where((axis == which) & (row == token), coords_ref[which, token], place)
    return place.astype(F32)


def rope_tables(place):
    side = DH // 6
    first = DH // 2 - 2 * side
    pair, axis = lane_axis(place.shape)
    step = jnp.where(axis == 0, pair, jnp.where(axis == 1, pair - first, pair - first - side))
    count = jnp.where(axis == 0, float(first), float(side))
    angle = place * jnp.exp(step.astype(F32) / count * (-math.log(10000.0)))
    sine = jnp.sin(angle)
    even = lax.broadcasted_iota(jnp.int32, place.shape, 1) % 2 == 0
    return jnp.cos(angle), jnp.where(even, -sine, 0.0), jnp.where(even, 0.0, sine)


def normed_heads(wide, gain_ref, tables):
    cosine, sine_even, sine_odd = tables
    width = wide.shape[-1]
    meansq = jnp.sum(wide * wide, axis=-1, keepdims=True) * (1.0 / width)
    inverse = lax.rsqrt(meansq + 1e-06)
    for head in range(width // DH):
        here = slice(head * DH, (head + 1) * DH)
        y = wide[:, here] * inverse * gain_ref[:, here]
        y = y * cosine + pltpu.roll(y, DH - 1, 1) * sine_even + pltpu.roll(y, 1, 1) * sine_odd
        yield head, y.astype(BF16)


def lay_kernel(groups, q_hbm, coords_hbm, *refs):
    videos, tok_rows, width = q_hbm.shape
    outs, (held, coords_ref, sems, coords_sem) = refs[:videos], refs[videos:]
    own = lax.axis_index("patch") // groups
    first = pltpu.make_async_copy(coords_hbm, coords_ref, coords_sem)
    first.start()
    reads = [
        pltpu.make_async_copy(q_hbm.at[own ^ s], held.at[s, :, pl.ds(0, width)], sems.at[0, s])
        for s in range(videos)
    ]
    writes = [pltpu.make_async_copy(held.at[s], outs[s], sems.at[1, s]) for s in range(videos)]
    for read in reads:
        read.start()
    first.wait()
    place = lane_places(coords_ref, tok_rows).astype(BF16)
    for s in range(videos):
        held[s, :, width:] = place
    for read, write in zip(reads, writes):
        read.wait()
        write.start()
    for write in writes:
        write.wait()


def key_kernel(k_hbm, v_hbm, gain_hbm, coords_hbm, out_hbm, k_ref, v_ref, gain_ref, coords_ref, done_ref, sems):
    videos, tok_rows, width = k_hbm.shape
    pairs = out_hbm.shape[2] // (2 * DH)
    groups = out_hbm.shape[0] // videos
    sources, places = (coords_hbm, k_hbm, gain_hbm, v_hbm), (coords_ref, k_ref, gain_ref, v_ref)
    reads = [
        pltpu.make_async_copy(source, place, sems.at[i])
        for i, (source, place) in enumerate(zip(sources, places))
    ]
    for read in reads:
        read.start()
    for read in reads:
        read.wait()
    tables = rope_tables(lane_places(coords_ref, tok_rows))
    writes = []
    for video in range(videos):
        for head, y in normed_heads(k_ref[video].astype(F32), gain_ref, tables):
            target, start = video * groups + head // pairs, head % pairs * 2 * DH
            done_ref[target, :, start : start + DH] = y
            done_ref[target, :, start + DH : start + 2 * DH] = v_ref[
                video, :, head * DH : (head + 1) * DH
            ]
        part = pl.ds(video * groups, groups)
        writes.append(pltpu.make_async_copy(done_ref.at[part], out_hbm.at[part], sems.at[4 + video]))
        writes[-1].start()
    for write in writes:
        write.wait()


def turn_kernel(gain_ref, *refs):
    got, out_ref = in_order(refs[:-1]), refs[-1]
    videos, tok_rows, width = out_ref.shape
    place = jnp.concatenate([ref[:, width:].astype(F32) for ref in got], axis=0)
    tables = rope_tables(place)
    for s in range(videos):
        mine = [table[s * tok_rows : (s + 1) * tok_rows] for table in tables]
        for head, y in normed_heads(got[s][:, :width].astype(F32), gain_ref, mine):
            out_ref[s, :, head * DH : (head + 1) * DH] = y


def query_kernel(q_ref, gain_ref, coords_ref, out_ref):
    videos, tok_rows, _ = q_ref.shape
    tables = rope_tables(lane_places(coords_ref, tok_rows))
    for video in range(videos):
        for head, y in normed_heads(q_ref[video].astype(F32), gain_ref, tables):
            out_ref[video, :, head * DH : (head + 1) * DH] = y


def softmax_parts(scores):
    top = jnp.max(scores, axis=-1, keepdims=True)
    weights = jnp.exp(scores - top)
    total = jnp.sum(weights, axis=-1, keepdims=True)
    return weights.astype(BF16), 1.0 / total, top + jnp.log(total)


def stacked(refs, lanes):
    rows = [ref[:, lanes].astype(F32) for ref in refs]
    return jnp.concatenate(rows, axis=0).astype(BF16)


def fresh_kernel(groups, videos, query_ref, fresh_ref, out_ref, log_ref):
    me = lax.axis_index("patch")
    own, mine = me // groups, me % groups
    queries = [query_ref.at[own ^ s] for s in range(videos)]
    _, tok_rows, width = out_ref.shape
    span = width // groups
    pairs = span // DH
    rows = videos * tok_rows
    scale = 1.0 / math.sqrt(DH)
    shape = (pairs * rows, rows)
    same = lax.broadcasted_iota(jnp.int32, shape, 0) % rows // tok_rows == (
        lax.broadcasted_iota(jnp.int32, shape, 1) // tok_rows
    )
    lane = lax.broadcasted_iota(jnp.int32, (rows, DH), 1)
    logs = jnp.zeros((rows, DH), F32)
    for t in range(groups):
        lanes = pl.ds(pl.multiple_of((mine ^ t) * span, DH), span)
        query = stacked(queries, lanes)
        fresh = stacked([fresh_ref.at[me ^ (s * groups) ^ t] for s in range(videos)], slice(None))
        scores = jnp.concatenate(
            [
                lax.dot_general(
                    query[:, pair * DH : (pair + 1) * DH],
                    fresh[:, 2 * pair * DH : (2 * pair + 1) * DH],
                    TRANSPOSED,
                    preferred_element_type=F32,
                )
                for pair in range(pairs)
            ],
            axis=0,
        )
        weights, inverse, log = softmax_parts(jnp.where(same, scores * scale, -jnp.inf))
        for pair in range(pairs):
            here = slice(pair * rows, (pair + 1) * rows)
            head = t * pairs + pair
            result = inverse[here] * jnp.dot(
                weights[here],
                fresh[:, (2 * pair + 1) * DH : (2 * pair + 2) * DH],
                preferred_element_type=F32,
            )
            logs = jnp.where(lane == head, log[here], logs)
            for s in range(videos):
                out_ref[s, :, head * DH : (head + 1) * DH] = result[s * tok_rows : (s + 1) * tok_rows]
    for s in range(videos):
        log_ref[s] = logs[s * tok_rows : (s + 1) * tok_rows]


def stale_kernel(groups, videos, query_ref, *refs):
    queries = [query_ref.at[s] for s in range(videos)]
    pieces, outs = refs[:groups], refs[groups:]
    me = lax.axis_index("patch")
    mine = me % groups
    pairs, total_rows, _ = pieces[0].shape
    tok_rows, width = queries[0].shape
    span = pairs * DH
    rows = videos * tok_rows
    scale = 1.0 / math.sqrt(DH)
    shape = (pairs * rows, total_rows)
    patch = (lax.broadcasted_iota(jnp.int32, shape, 0) % rows // tok_rows * groups) ^ me
    own = patch == lax.broadcasted_iota(jnp.int32, shape, 1) // tok_rows
    lane = lax.broadcasted_iota(jnp.int32, (rows, DH), 1)
    logs = jnp.zeros((rows, DH), F32)
    for t in range(groups):
        start = pl.multiple_of((mine ^ t) * span, DH)
        query = stacked(queries, pl.ds(start, span))
        scores = jnp.concatenate(
            [
                lax.dot_general(
                    query[:, pair * DH : (pair + 1) * DH],
                    pieces[t][pair, :, :DH],
                    TRANSPOSED,
                    preferred_element_type=F32,
                )
                for pair in range(pairs)
            ],
            axis=0,
        )
        weights, inverse, log = softmax_parts(jnp.where(own, -jnp.inf, scores * scale))
        results = []
        for pair in range(pairs):
            here = slice(pair * rows, (pair + 1) * rows)
            results.append(
                inverse[here]
                * jnp.dot(weights[here], pieces[t][pair, :, DH:], preferred_element_type=F32)
            )
            logs = jnp.where(lane == t * pairs + pair, log[here], logs)
        result = jnp.concatenate(results, axis=1).astype(BF16)
        for s in range(videos):
            outs[s][:, t * span : (t + 1) * span] = result[s * tok_rows : (s + 1) * tok_rows]
    high = logs.astype(BF16).astype(F32)
    middle = (logs - high).astype(BF16).astype(F32)
    low = (logs - high - middle).astype(BF16).astype(F32)
    heads = groups * pairs
    terms = (high + pltpu.roll(middle, heads, 1) + pltpu.roll(low, 2 * heads, 1)).astype(BF16)
    for s in range(videos):
        outs[s][:, width:] = terms[s * tok_rows : (s + 1) * tok_rows]


def join_kernel(groups, videos, *refs):
    back = in_order(refs[:videos])
    fresh_ref, log_ref, out_ref, done_ref, sems = refs[videos:]
    me = lax.axis_index("patch")
    own, mine = me // groups, me % groups
    _, tok_rows, width = fresh_ref.shape
    heads = width // DH
    pairs = heads // groups
    span = pairs * DH
    copies = []
    for s in range(videos):
        terms = back[s][:, width:].astype(F32)
        stale_log = terms + pltpu.roll(terms, DH - heads, 1) + pltpu.roll(terms, DH - 2 * heads, 1)
        share = 1.0 / (1.0 + jnp.exp(stale_log - log_ref[s]))
        for t in range(groups):
            parts = []
            for pair in range(pairs):
                head = t * pairs + pair
                here = slice(head * DH, (head + 1) * DH)
                stale = back[s][:, here].astype(F32)
                parts.append(stale + share[:, head : head + 1] * (fresh_ref[s, :, here] - stale))
            lanes = pl.ds(pl.multiple_of((mine ^ t) * span, DH), span)
            done_ref[s, :, lanes] = jnp.concatenate(parts, axis=1).astype(BF16)
        copies.append(pltpu.make_async_copy(done_ref.at[s], out_ref.at[own ^ s], sems.at[s]))
        copies[-1].start()
    for copy in copies:
        copy.wait()


def cache_kernel(got_ref, out_ref, sems):
    copies = []
    for pair in range(out_ref.shape[0]):
        lanes = pl.ds(2 * pair * DH, 2 * DH)
        copies.append(
            pltpu.make_async_copy(got_ref.at[:, :, lanes], out_ref.at[pair], sems.at[pair])
        )
        copies[-1].start()
    for copy in copies:
        copy.wait()


def permuted(array, offset, patches):
    return lax.ppermute(array, "patch", [(i, i ^ offset) for i in range(patches)])


def far_first(arrays):
    return [*arrays[:0:-1], arrays[0]]


def in_order(arrays):
    return [arrays[-1], *arrays[-2::-1]]


def exchange(arrays, stride, patches):
    return [arrays[0]] + [
        permuted(arrays[s], s * stride, patches) for s in range(1, len(arrays))
    ]


def local(queries, keys, values, q_gain, k_gain, stale_cache, coords):
    videos, tok_rows, width = queries.shape
    pairs_here, total_rows, _ = stale_cache.shape
    patches = total_rows // tok_rows
    groups = patches // videos

    def kernel(body, name, limit, cost=0, **kwargs):
        return pl.pallas_call(
            body,
            name=name,
            compiler_params=pltpu.CompilerParams(vmem_limit_bytes=limit * MIB),
            cost_estimate=pl.CostEstimate(flops=cost, bytes_accessed=0, transcendentals=0),
            **kwargs,
        )

    gains = q_gain.reshape(1, width), k_gain.reshape(1, width)
    sent = kernel(
        functools.partial(lay_kernel, groups),
        "lay",
        56,
        out_shape=[jax.ShapeDtypeStruct((tok_rows, width + DH), BF16)] * videos,
        in_specs=[HBM] * 2,
        out_specs=[HBM] * videos,
        scratch_shapes=[
            pltpu.VMEM((videos, tok_rows, width + DH), BF16),
            pltpu.SMEM(coords.shape, jnp.int32),
            pltpu.SemaphoreType.DMA((2, videos)),
            pltpu.SemaphoreType.DMA,
        ],
    )(queries, coords)
    stale_sent, kept = lax.optimization_barrier((stale_cache, sent[0]))
    pieces = {0: stale_cache}
    bit = groups // 2
    pieces[bit] = permuted(stale_sent, bit, patches)
    query_raw = far_first(exchange([kept, *sent[1:]], groups, patches))
    fresh = kernel(
        key_kernel,
        "key",
        56,
        out_shape=jax.ShapeDtypeStruct((patches, tok_rows, 2 * pairs_here * DH), BF16),
        in_specs=[HBM] * 4,
        out_specs=HBM,
        scratch_shapes=[
            pltpu.VMEM(keys.shape, BF16),
            pltpu.VMEM(keys.shape, BF16),
            pltpu.VMEM((1, width), F32),
            pltpu.SMEM(coords.shape, jnp.int32),
            pltpu.VMEM((patches, tok_rows, 2 * pairs_here * DH), BF16),
            pltpu.SemaphoreType.DMA((4 + videos,)),
        ],
    )(keys, values, gains[1], coords)
    cached = lax.all_to_all(fresh, "patch", split_axis=0, concat_axis=0, tiled=True)
    query_raw, pieces, fresh = lax.optimization_barrier((query_raw, pieces, fresh))
    query_got = kernel(
        turn_kernel,
        "turn",
        16,
        cost=10**11,
        out_shape=jax.ShapeDtypeStruct(queries.shape, BF16),
        in_specs=[VMEM] * (1 + videos),
        out_specs=VMEM,
    )(gains[0], *query_raw)
    pieces, query_got = lax.optimization_barrier((pieces, query_got))
    while bit > 1:
        bit //= 2
        pieces.update({t | bit: permuted(piece, bit, patches) for t, piece in list(pieces.items())})
    result = kernel(
        functools.partial(stale_kernel, groups, videos),
        "stale",
        32,
        out_shape=[jax.ShapeDtypeStruct((tok_rows, width + DH), BF16)] * videos,
        in_specs=[VMEM] * (1 + groups),
        out_specs=[VMEM] * videos,
    )(query_got, *[pieces[t] for t in range(groups)])
    result, fresh_late, queries_late = lax.optimization_barrier((result, fresh, queries))
    query = kernel(
        query_kernel,
        "query",
        16,
        out_shape=jax.ShapeDtypeStruct(queries.shape, BF16),
        in_specs=[VMEM] * 2 + [SMEM],
        out_specs=VMEM,
    )(queries_late, gains[0], coords)
    back = far_first(exchange(result, groups, patches))
    fresh_sum, fresh_log = kernel(
        functools.partial(fresh_kernel, groups, videos),
        "fresh",
        16,
        out_shape=(
            jax.ShapeDtypeStruct((videos, tok_rows, width), F32),
            jax.ShapeDtypeStruct((videos, tok_rows, DH), F32),
        ),
        in_specs=[VMEM] * 2,
        out_specs=(VMEM, VMEM),
    )(query, fresh_late)
    fresh_sum, cached = lax.optimization_barrier((fresh_sum, cached))
    next_cache = kernel(
        cache_kernel,
        "cache",
        16,
        out_shape=jax.ShapeDtypeStruct((pairs_here, patches, tok_rows, 2 * DH), BF16),
        in_specs=[VMEM],
        out_specs=HBM,
        scratch_shapes=[pltpu.SemaphoreType.DMA((pairs_here,))],
    )(cached)
    attended = kernel(
        functools.partial(join_kernel, groups, videos),
        "join",
        16,
        out_shape=jax.ShapeDtypeStruct(queries.shape, BF16),
        in_specs=[VMEM] * (videos + 2),
        out_specs=HBM,
        scratch_shapes=[
            pltpu.VMEM(queries.shape, BF16),
            pltpu.SemaphoreType.DMA((videos,)),
        ],
    )(*back, fresh_sum, fresh_log)
    return (attended, next_cache.reshape(stale_cache.shape))


def solution(mesh):
    in_specs = (
        P("req", "patch", None),
        P("req", "patch", None),
        P("req", "patch", None),
        P(),
        P(),
        P(("req", "patch"), None, None),
        P(None, "patch"),
    )
    out_specs = (P("req", "patch", None), P(("req", "patch"), None, None))
    return jax.shard_map(local, mesh=mesh, in_specs=in_specs, out_specs=out_specs, check_vma=False)
```

```python
import functools
import math

import jax
import jax.numpy as jnp
from jax import lax
from jax.experimental import pallas as pl
from jax.experimental.pallas import tpu as pltpu
from jax.sharding import PartitionSpec as P

DH = 128
VMEM = pl.BlockSpec(memory_space=pltpu.VMEM)
HBM = pl.BlockSpec(memory_space=pltpu.HBM)
SMEM = pl.BlockSpec(memory_space=pltpu.SMEM)
MIB = 1024 * 1024
BF16 = jnp.bfloat16
F32 = jnp.float32
TRANSPOSED = (((1,), (1,)), ((), ()))


def lane_axis(shape):
    side = DH // 6
    first = DH // 2 - 2 * side
    pair = lax.broadcasted_iota(jnp.int32, shape, 1) // 2
    return pair, (pair >= first).astype(jnp.int32) + (pair >= first + side).astype(jnp.int32)


def lane_places(coords_ref, tok_rows):
    shape = (tok_rows, DH)
    row = lax.broadcasted_iota(jnp.int32, shape, 0)
    _, axis = lane_axis(shape)
    place = jnp.zeros(shape, jnp.int32)
    for which in range(3):
        for token in range(tok_rows):
            place = jnp.where((axis == which) & (row == token), coords_ref[which, token], place)
    return place.astype(F32)


def rope_tables(place):
    side = DH // 6
    first = DH // 2 - 2 * side
    pair, axis = lane_axis(place.shape)
    step = jnp.where(axis == 0, pair, jnp.where(axis == 1, pair - first, pair - first - side))
    count = jnp.where(axis == 0, float(first), float(side))
    angle = place * jnp.exp(step.astype(F32) / count * (-math.log(10000.0)))
    sine = jnp.sin(angle)
    even = lax.broadcasted_iota(jnp.int32, place.shape, 1) % 2 == 0
    return jnp.cos(angle), jnp.where(even, -sine, 0.0), jnp.where(even, 0.0, sine)


def normed_heads(wide, gain_ref, tables):
    cosine, sine_even, sine_odd = tables
    width = wide.shape[-1]
    meansq = jnp.sum(wide * wide, axis=-1, keepdims=True) * (1.0 / width)
    inverse = lax.rsqrt(meansq + 1e-06)
    for head in range(width // DH):
        here = slice(head * DH, (head + 1) * DH)
        y = wide[:, here] * inverse * gain_ref[:, here]
        y = y * cosine + pltpu.roll(y, DH - 1, 1) * sine_even + pltpu.roll(y, 1, 1) * sine_odd
        yield head, y.astype(BF16)


def lay_kernel(groups, q_hbm, coords_hbm, *refs):
    videos, tok_rows, width = q_hbm.shape
    outs, (held, coords_ref, sems, coords_sem) = refs[:videos], refs[videos:]
    own = lax.axis_index("patch") // groups
    first = pltpu.make_async_copy(coords_hbm, coords_ref, coords_sem)
    first.start()
    reads = [
        pltpu.make_async_copy(q_hbm.at[own ^ s], held.at[s, :, pl.ds(0, width)], sems.at[0, s])
        for s in range(videos)
    ]
    writes = [pltpu.make_async_copy(held.at[s], outs[s], sems.at[1, s]) for s in range(videos)]
    for read in reads:
        read.start()
    first.wait()
    place = lane_places(coords_ref, tok_rows).astype(BF16)
    for s in range(videos):
        held[s, :, width:] = place
    for read, write in zip(reads, writes):
        read.wait()
        write.start()
    for write in writes:
        write.wait()


def key_kernel(k_hbm, v_hbm, gain_hbm, coords_hbm, out_hbm, k_ref, gain_ref, coords_ref, done_ref, sems, value_sems):
    videos, tok_rows, width = k_hbm.shape
    span = out_hbm.shape[2] // 2
    pairs = span // DH
    groups = out_hbm.shape[0] // videos
    reads = [
        pltpu.make_async_copy(source, place, sems.at[i])
        for i, (source, place) in enumerate(
            ((coords_hbm, coords_ref), (k_hbm, k_ref), (gain_hbm, gain_ref))
        )
    ]
    for read in reads:
        read.start()
    values = [
        pltpu.make_async_copy(
            v_hbm.at[target // groups, :, pl.ds(target % groups * span, span)],
            done_ref.at[target, :, pl.ds(span, span)],
            value_sems.at[target],
        )
        for target in range(videos * groups)
    ]
    for value in values:
        value.start()
    for read in reads:
        read.wait()
    tables = rope_tables(lane_places(coords_ref, tok_rows))
    writes = []
    for video in range(videos):
        for head, y in normed_heads(k_ref[video].astype(F32), gain_ref, tables):
            start = head % pairs * DH
            done_ref[video * groups + head // pairs, :, start : start + DH] = y
        for value in values[video * groups : (video + 1) * groups]:
            value.wait()
        part = pl.ds(video * groups, groups)
        writes.append(pltpu.make_async_copy(done_ref.at[part], out_hbm.at[part], sems.at[3 + video]))
        writes[-1].start()
    for write in writes:
        write.wait()


def turn_kernel(gain_ref, *refs):
    got, out_ref = in_order(refs[:-1]), refs[-1]
    videos, tok_rows, width = out_ref.shape
    place = jnp.concatenate([ref[:, width:].astype(F32) for ref in got], axis=0)
    tables = rope_tables(place)
    for s in range(videos):
        mine = [table[s * tok_rows : (s + 1) * tok_rows] for table in tables]
        for head, y in normed_heads(got[s][:, :width].astype(F32), gain_ref, mine):
            out_ref[s, :, head * DH : (head + 1) * DH] = y


def query_kernel(q_ref, gain_ref, coords_ref, out_ref):
    videos, tok_rows, _ = q_ref.shape
    tables = rope_tables(lane_places(coords_ref, tok_rows))
    for video in range(videos):
        for head, y in normed_heads(q_ref[video].astype(F32), gain_ref, tables):
            out_ref[video, :, head * DH : (head + 1) * DH] = y


def softmax_parts(scores):
    top = jnp.max(scores, axis=-1, keepdims=True)
    weights = jnp.exp(scores - top)
    total = jnp.sum(weights, axis=-1, keepdims=True)
    return weights.astype(BF16), 1.0 / total, top + jnp.log(total)


def stacked(refs, lanes):
    rows = [ref[:, lanes].astype(F32) for ref in refs]
    return jnp.concatenate(rows, axis=0).astype(BF16)


def fresh_kernel(groups, videos, query_ref, fresh_ref, out_ref, log_ref):
    me = lax.axis_index("patch")
    own, mine = me // groups, me % groups
    queries = [query_ref.at[own ^ s] for s in range(videos)]
    _, tok_rows, width = out_ref.shape
    span = width // groups
    pairs = span // DH
    rows = videos * tok_rows
    scale = 1.0 / math.sqrt(DH)
    shape = (pairs * rows, rows)
    same = lax.broadcasted_iota(jnp.int32, shape, 0) % rows // tok_rows == (
        lax.broadcasted_iota(jnp.int32, shape, 1) // tok_rows
    )
    lane = lax.broadcasted_iota(jnp.int32, (rows, DH), 1)
    logs = jnp.zeros((rows, DH), F32)
    for t in range(groups):
        lanes = pl.ds(pl.multiple_of((mine ^ t) * span, DH), span)
        query = stacked(queries, lanes)
        fresh = stacked([fresh_ref.at[me ^ (s * groups) ^ t] for s in range(videos)], slice(None))
        scores = jnp.concatenate(
            [
                lax.dot_general(
                    query[:, pair * DH : (pair + 1) * DH],
                    fresh[:, pair * DH : (pair + 1) * DH],
                    TRANSPOSED,
                    preferred_element_type=F32,
                )
                for pair in range(pairs)
            ],
            axis=0,
        )
        weights, inverse, log = softmax_parts(jnp.where(same, scores * scale, -jnp.inf))
        for pair in range(pairs):
            here = slice(pair * rows, (pair + 1) * rows)
            head = t * pairs + pair
            result = inverse[here] * jnp.dot(
                weights[here],
                fresh[:, span + pair * DH : span + (pair + 1) * DH],
                preferred_element_type=F32,
            )
            logs = jnp.where(lane == head, log[here], logs)
            for s in range(videos):
                out_ref[s, :, head * DH : (head + 1) * DH] = result[s * tok_rows : (s + 1) * tok_rows]
    for s in range(videos):
        log_ref[s] = logs[s * tok_rows : (s + 1) * tok_rows]


def stale_kernel(groups, videos, query_ref, *refs):
    queries = [query_ref.at[s] for s in range(videos)]
    pieces, outs = refs[:groups], refs[groups:]
    me = lax.axis_index("patch")
    mine = me % groups
    pairs, total_rows, _ = pieces[0].shape
    tok_rows, width = queries[0].shape
    span = pairs * DH
    rows = videos * tok_rows
    scale = 1.0 / math.sqrt(DH)
    shape = (pairs * rows, total_rows)
    patch = (lax.broadcasted_iota(jnp.int32, shape, 0) % rows // tok_rows * groups) ^ me
    own = patch == lax.broadcasted_iota(jnp.int32, shape, 1) // tok_rows
    lane = lax.broadcasted_iota(jnp.int32, (rows, DH), 1)
    logs = jnp.zeros((rows, DH), F32)
    for t in range(groups):
        start = pl.multiple_of((mine ^ t) * span, DH)
        query = stacked(queries, pl.ds(start, span))
        scores = jnp.concatenate(
            [
                lax.dot_general(
                    query[:, pair * DH : (pair + 1) * DH],
                    pieces[t][pair, :, :DH],
                    TRANSPOSED,
                    preferred_element_type=F32,
                )
                for pair in range(pairs)
            ],
            axis=0,
        )
        weights, inverse, log = softmax_parts(jnp.where(own, -jnp.inf, scores * scale))
        results = []
        for pair in range(pairs):
            here = slice(pair * rows, (pair + 1) * rows)
            results.append(
                inverse[here]
                * jnp.dot(weights[here], pieces[t][pair, :, DH:], preferred_element_type=F32)
            )
            logs = jnp.where(lane == t * pairs + pair, log[here], logs)
        result = jnp.concatenate(results, axis=1).astype(BF16)
        for s in range(videos):
            outs[s][:, t * span : (t + 1) * span] = result[s * tok_rows : (s + 1) * tok_rows]
    high = logs.astype(BF16).astype(F32)
    middle = (logs - high).astype(BF16).astype(F32)
    low = (logs - high - middle).astype(BF16).astype(F32)
    heads = groups * pairs
    terms = (high + pltpu.roll(middle, heads, 1) + pltpu.roll(low, 2 * heads, 1)).astype(BF16)
    for s in range(videos):
        outs[s][:, width:] = terms[s * tok_rows : (s + 1) * tok_rows]


def join_kernel(groups, videos, *refs):
    back = in_order(refs[:videos])
    fresh_ref, log_ref, out_ref, done_ref, sems = refs[videos:]
    me = lax.axis_index("patch")
    own, mine = me // groups, me % groups
    _, tok_rows, width = fresh_ref.shape
    heads = width // DH
    pairs = heads // groups
    span = pairs * DH
    copies = []
    for s in range(videos):
        terms = back[s][:, width:].astype(F32)
        stale_log = terms + pltpu.roll(terms, DH - heads, 1) + pltpu.roll(terms, DH - 2 * heads, 1)
        share = 1.0 / (1.0 + jnp.exp(stale_log - log_ref[s]))
        for t in range(groups):
            parts = []
            for pair in range(pairs):
                head = t * pairs + pair
                here = slice(head * DH, (head + 1) * DH)
                stale = back[s][:, here].astype(F32)
                parts.append(stale + share[:, head : head + 1] * (fresh_ref[s, :, here] - stale))
            lanes = pl.ds(pl.multiple_of((mine ^ t) * span, DH), span)
            done_ref[s, :, lanes] = jnp.concatenate(parts, axis=1).astype(BF16)
        copies.append(pltpu.make_async_copy(done_ref.at[s], out_ref.at[own ^ s], sems.at[s]))
        copies[-1].start()
    for copy in copies:
        copy.wait()


def cache_kernel(got_ref, out_ref, sems):
    copies = []
    for pair in range(out_ref.shape[0]):
        for part in range(2):
            source = got_ref.at[:, :, pl.ds((part * out_ref.shape[0] + pair) * DH, DH)]
            target = out_ref.at[pair, :, :, pl.ds(part * DH, DH)]
            copies.append(pltpu.make_async_copy(source, target, sems.at[part, pair]))
            copies[-1].start()
    for copy in copies:
        copy.wait()


def permuted(array, offset, patches):
    return lax.ppermute(array, "patch", [(i, i ^ offset) for i in range(patches)])


def far_first(arrays):
    half = len(arrays) // 2
    return [*arrays[half:], *arrays[1:half], arrays[0]]


def in_order(arrays):
    half = len(arrays) // 2
    return [arrays[-1], *arrays[half:-1], *arrays[:half]]


def exchange(arrays, stride, patches):
    return [arrays[0]] + [
        permuted(arrays[s], s * stride, patches) for s in range(1, len(arrays))
    ]


def local(queries, keys, values, q_gain, k_gain, stale_cache, coords):
    videos, tok_rows, width = queries.shape
    pairs_here, total_rows, _ = stale_cache.shape
    patches = total_rows // tok_rows
    groups = patches // videos

    def kernel(body, name, limit, cost=0, **kwargs):
        return pl.pallas_call(
            body,
            name=name,
            compiler_params=pltpu.CompilerParams(vmem_limit_bytes=limit * MIB),
            cost_estimate=pl.CostEstimate(flops=cost, bytes_accessed=0, transcendentals=0),
            **kwargs,
        )

    gains = q_gain.reshape(1, width), k_gain.reshape(1, width)
    sent = kernel(
        functools.partial(lay_kernel, groups),
        "lay",
        56,
        out_shape=[jax.ShapeDtypeStruct((tok_rows, width + DH), BF16)] * videos,
        in_specs=[HBM] * 2,
        out_specs=[HBM] * videos,
        scratch_shapes=[
            pltpu.VMEM((videos, tok_rows, width + DH), BF16),
            pltpu.SMEM(coords.shape, jnp.int32),
            pltpu.SemaphoreType.DMA((2, videos)),
            pltpu.SemaphoreType.DMA,
        ],
    )(queries, coords)
    stale_sent, kept = lax.optimization_barrier((stale_cache, sent[0]))
    pieces = {0: stale_cache}
    bit = groups // 2
    pieces[bit] = permuted(stale_sent, bit, patches)
    query_raw = far_first(exchange([kept, *sent[1:]], groups, patches))
    fresh = kernel(
        key_kernel,
        "key",
        56,
        out_shape=jax.ShapeDtypeStruct((patches, tok_rows, 2 * pairs_here * DH), BF16),
        in_specs=[HBM] * 4,
        out_specs=HBM,
        scratch_shapes=[
            pltpu.VMEM(keys.shape, BF16),
            pltpu.VMEM((1, width), F32),
            pltpu.SMEM(coords.shape, jnp.int32),
            pltpu.VMEM((patches, tok_rows, 2 * pairs_here * DH), BF16),
            pltpu.SemaphoreType.DMA((3 + videos,)),
            pltpu.SemaphoreType.DMA((patches,)),
        ],
    )(keys, values, gains[1], coords)
    cached = lax.all_to_all(fresh, "patch", split_axis=0, concat_axis=0, tiled=True)
    query_raw, pieces, fresh = lax.optimization_barrier((query_raw, pieces, fresh))
    query_got = kernel(
        turn_kernel,
        "turn",
        16,
        cost=10**11,
        out_shape=jax.ShapeDtypeStruct(queries.shape, BF16),
        in_specs=[VMEM] * (1 + videos),
        out_specs=VMEM,
    )(gains[0], *query_raw)
    pieces, query_got = lax.optimization_barrier((pieces, query_got))
    while bit > 1:
        bit //= 2
        pieces.update({t | bit: permuted(piece, bit, patches) for t, piece in list(pieces.items())})
    result = kernel(
        functools.partial(stale_kernel, groups, videos),
        "stale",
        32,
        out_shape=[jax.ShapeDtypeStruct((tok_rows, width + DH), BF16)] * videos,
        in_specs=[VMEM] * (1 + groups),
        out_specs=[VMEM] * videos,
    )(query_got, *[pieces[t] for t in range(groups)])
    result, fresh_late, queries_late = lax.optimization_barrier((result, fresh, queries))
    query = kernel(
        query_kernel,
        "query",
        16,
        out_shape=jax.ShapeDtypeStruct(queries.shape, BF16),
        in_specs=[VMEM] * 2 + [SMEM],
        out_specs=VMEM,
    )(queries_late, gains[0], coords)
    back = far_first(exchange(result, groups, patches))
    fresh_sum, fresh_log = kernel(
        functools.partial(fresh_kernel, groups, videos),
        "fresh",
        16,
        out_shape=(
            jax.ShapeDtypeStruct((videos, tok_rows, width), F32),
            jax.ShapeDtypeStruct((videos, tok_rows, DH), F32),
        ),
        in_specs=[VMEM] * 2,
        out_specs=(VMEM, VMEM),
    )(query, fresh_late)
    fresh_sum, cached = lax.optimization_barrier((fresh_sum, cached))
    next_cache = kernel(
        cache_kernel,
        "cache",
        16,
        out_shape=jax.ShapeDtypeStruct((pairs_here, patches, tok_rows, 2 * DH), BF16),
        in_specs=[VMEM],
        out_specs=HBM,
        scratch_shapes=[pltpu.SemaphoreType.DMA((2, pairs_here))],
    )(cached)
    attended = kernel(
        functools.partial(join_kernel, groups, videos),
        "join",
        16,
        out_shape=jax.ShapeDtypeStruct(queries.shape, BF16),
        in_specs=[VMEM] * (videos + 2),
        out_specs=HBM,
        scratch_shapes=[
            pltpu.VMEM(queries.shape, BF16),
            pltpu.SemaphoreType.DMA((videos,)),
        ],
    )(*back, fresh_sum, fresh_log)
    return (attended, next_cache.reshape(stale_cache.shape))


def solution(mesh):
    in_specs = (
        P("req", "patch", None),
        P("req", "patch", None),
        P("req", "patch", None),
        P(),
        P(),
        P(("req", "patch"), None, None),
        P(None, "patch"),
    )
    out_specs = (P("req", "patch", None), P(("req", "patch"), None, None))
    return jax.shard_map(local, mesh=mesh, in_specs=in_specs, out_specs=out_specs, check_vma=False)
```

```python
import functools
import math

import jax
import jax.numpy as jnp
from jax import lax
from jax.experimental import pallas as pl
from jax.experimental.pallas import tpu as pltpu
from jax.sharding import PartitionSpec as P

DH = 128
VMEM = pl.BlockSpec(memory_space=pltpu.VMEM)
HBM = pl.BlockSpec(memory_space=pltpu.HBM)
SMEM = pl.BlockSpec(memory_space=pltpu.SMEM)
MIB = 1024 * 1024
BF16 = jnp.bfloat16
F32 = jnp.float32
TRANSPOSED = (((1,), (1,)), ((), ()))


def lane_axis(shape):
    side = DH // 6
    first = DH // 2 - 2 * side
    pair = lax.broadcasted_iota(jnp.int32, shape, 1) // 2
    return pair, (pair >= first).astype(jnp.int32) + (pair >= first + side).astype(jnp.int32)


def lane_places(coords_ref, tok_rows):
    shape = (tok_rows, DH)
    row = lax.broadcasted_iota(jnp.int32, shape, 0)
    _, axis = lane_axis(shape)
    place = jnp.zeros(shape, jnp.int32)
    for which in range(3):
        for token in range(tok_rows):
            place = jnp.where((axis == which) & (row == token), coords_ref[which, token], place)
    return place.astype(F32)


def rope_tables(place):
    side = DH // 6
    first = DH // 2 - 2 * side
    pair, axis = lane_axis(place.shape)
    step = jnp.where(axis == 0, pair, jnp.where(axis == 1, pair - first, pair - first - side))
    count = jnp.where(axis == 0, float(first), float(side))
    angle = place * jnp.exp(step.astype(F32) / count * (-math.log(10000.0)))
    sine = jnp.sin(angle)
    even = lax.broadcasted_iota(jnp.int32, place.shape, 1) % 2 == 0
    return jnp.cos(angle), jnp.where(even, -sine, 0.0), jnp.where(even, 0.0, sine)


def normed_heads(wide, gain_ref, tables):
    cosine, sine_even, sine_odd = tables
    width = wide.shape[-1]
    meansq = jnp.sum(wide * wide, axis=-1, keepdims=True) * (1.0 / width)
    inverse = lax.rsqrt(meansq + 1e-06)
    for head in range(width // DH):
        here = slice(head * DH, (head + 1) * DH)
        y = wide[:, here] * inverse * gain_ref[:, here]
        y = y * cosine + pltpu.roll(y, DH - 1, 1) * sine_even + pltpu.roll(y, 1, 1) * sine_odd
        yield head, y.astype(BF16)


def lay_kernel(groups, q_hbm, coords_hbm, *refs):
    videos, tok_rows, width = q_hbm.shape
    outs, (held, coords_ref, sems, coords_sem) = refs[:videos], refs[videos:]
    own = lax.axis_index("patch") // groups
    first = pltpu.make_async_copy(coords_hbm, coords_ref, coords_sem)
    first.start()
    read = pltpu.make_async_copy(q_hbm, held.at[:, :, pl.ds(0, width)], sems.at[0, 0])
    writes = [pltpu.make_async_copy(held.at[own ^ s], outs[s], sems.at[1, s]) for s in range(videos)]
    read.start()
    first.wait()
    place = lane_places(coords_ref, tok_rows).astype(BF16)
    for s in range(videos):
        held[s, :, width:] = place
    read.wait()
    for write in writes:
        write.start()
    for write in writes:
        write.wait()


def key_kernel(k_hbm, v_hbm, gain_hbm, coords_hbm, out_hbm, k_ref, v_ref, gain_ref, coords_ref, done_ref, sems):
    videos, tok_rows, width = k_hbm.shape
    pairs = out_hbm.shape[2] // (2 * DH)
    groups = out_hbm.shape[0] // videos
    sources, places = (coords_hbm, k_hbm, gain_hbm, v_hbm), (coords_ref, k_ref, gain_ref, v_ref)
    reads = [
        pltpu.make_async_copy(source, place, sems.at[i])
        for i, (source, place) in enumerate(zip(sources, places))
    ]
    for read in reads:
        read.start()
    for read in reads:
        read.wait()
    tables = rope_tables(lane_places(coords_ref, tok_rows))
    writes = []
    for video in range(videos):
        for head, y in normed_heads(k_ref[video].astype(F32), gain_ref, tables):
            target, start = video * groups + head // pairs, head % pairs * 2 * DH
            done_ref[target, :, start : start + DH] = y
            done_ref[target, :, start + DH : start + 2 * DH] = v_ref[
                video, :, head * DH : (head + 1) * DH
            ]
        part = pl.ds(video * groups, groups)
        writes.append(pltpu.make_async_copy(done_ref.at[part], out_hbm.at[part], sems.at[4 + video]))
        writes[-1].start()
    for write in writes:
        write.wait()


def turn_kernel(gain_ref, *refs):
    got, out_ref = in_order(refs[:-1]), refs[-1]
    videos, tok_rows, width = out_ref.shape
    place = jnp.concatenate([ref[:, width:].astype(F32) for ref in got], axis=0)
    tables = rope_tables(place)
    for s in range(videos):
        mine = [table[s * tok_rows : (s + 1) * tok_rows] for table in tables]
        for head, y in normed_heads(got[s][:, :width].astype(F32), gain_ref, mine):
            out_ref[s, :, head * DH : (head + 1) * DH] = y


def query_kernel(q_ref, gain_ref, coords_ref, out_ref):
    videos, tok_rows, _ = q_ref.shape
    tables = rope_tables(lane_places(coords_ref, tok_rows))
    for video in range(videos):
        for head, y in normed_heads(q_ref[video].astype(F32), gain_ref, tables):
            out_ref[video, :, head * DH : (head + 1) * DH] = y


def softmax_parts(scores):
    top = jnp.max(scores, axis=-1, keepdims=True)
    weights = jnp.exp(scores - top)
    total = jnp.sum(weights, axis=-1, keepdims=True)
    return weights.astype(BF16), 1.0 / total, top + jnp.log(total)


def stacked(refs, lanes):
    rows = [ref[:, lanes].astype(F32) for ref in refs]
    return jnp.concatenate(rows, axis=0).astype(BF16)


def fresh_kernel(groups, videos, query_ref, fresh_ref, out_ref, log_ref):
    me = lax.axis_index("patch")
    own, mine = me // groups, me % groups
    queries = [query_ref.at[own ^ s] for s in range(videos)]
    _, tok_rows, width = out_ref.shape
    span = width // groups
    pairs = span // DH
    rows = videos * tok_rows
    scale = 1.0 / math.sqrt(DH)
    shape = (pairs * rows, rows)
    same = lax.broadcasted_iota(jnp.int32, shape, 0) % rows // tok_rows == (
        lax.broadcasted_iota(jnp.int32, shape, 1) // tok_rows
    )
    lane = lax.broadcasted_iota(jnp.int32, (rows, DH), 1)
    logs = jnp.zeros((rows, DH), F32)
    for t in range(groups):
        lanes = pl.ds(pl.multiple_of((mine ^ t) * span, DH), span)
        query = stacked(queries, lanes)
        fresh = stacked([fresh_ref.at[me ^ (s * groups) ^ t] for s in range(videos)], slice(None))
        scores = jnp.concatenate(
            [
                lax.dot_general(
                    query[:, pair * DH : (pair + 1) * DH],
                    fresh[:, 2 * pair * DH : (2 * pair + 1) * DH],
                    TRANSPOSED,
                    preferred_element_type=F32,
                )
                for pair in range(pairs)
            ],
            axis=0,
        )
        weights, inverse, log = softmax_parts(jnp.where(same, scores * scale, -jnp.inf))
        for pair in range(pairs):
            here = slice(pair * rows, (pair + 1) * rows)
            head = t * pairs + pair
            result = inverse[here] * jnp.dot(
                weights[here],
                fresh[:, (2 * pair + 1) * DH : (2 * pair + 2) * DH],
                preferred_element_type=F32,
            )
            logs = jnp.where(lane == head, log[here], logs)
            for s in range(videos):
                out_ref[s, :, head * DH : (head + 1) * DH] = result[s * tok_rows : (s + 1) * tok_rows]
    for s in range(videos):
        log_ref[s] = logs[s * tok_rows : (s + 1) * tok_rows]


def stale_kernel(groups, videos, query_ref, *refs):
    queries = [query_ref.at[s] for s in range(videos)]
    pieces, outs = refs[:groups], refs[groups:]
    me = lax.axis_index("patch")
    mine = me % groups
    pairs, total_rows, _ = pieces[0].shape
    tok_rows, width = queries[0].shape
    span = pairs * DH
    rows = videos * tok_rows
    scale = 1.0 / math.sqrt(DH)
    shape = (pairs * rows, total_rows)
    patch = (lax.broadcasted_iota(jnp.int32, shape, 0) % rows // tok_rows * groups) ^ me
    own = patch == lax.broadcasted_iota(jnp.int32, shape, 1) // tok_rows
    lane = lax.broadcasted_iota(jnp.int32, (rows, DH), 1)
    logs = jnp.zeros((rows, DH), F32)
    for t in range(groups):
        start = pl.multiple_of((mine ^ t) * span, DH)
        query = stacked(queries, pl.ds(start, span))
        scores = jnp.concatenate(
            [
                lax.dot_general(
                    query[:, pair * DH : (pair + 1) * DH],
                    pieces[t][pair, :, :DH],
                    TRANSPOSED,
                    preferred_element_type=F32,
                )
                for pair in range(pairs)
            ],
            axis=0,
        )
        weights, inverse, log = softmax_parts(jnp.where(own, -jnp.inf, scores * scale))
        results = []
        for pair in range(pairs):
            here = slice(pair * rows, (pair + 1) * rows)
            results.append(
                inverse[here]
                * jnp.dot(weights[here], pieces[t][pair, :, DH:], preferred_element_type=F32)
            )
            logs = jnp.where(lane == t * pairs + pair, log[here], logs)
        result = jnp.concatenate(results, axis=1).astype(BF16)
        for s in range(videos):
            outs[s][:, t * span : (t + 1) * span] = result[s * tok_rows : (s + 1) * tok_rows]
    high = logs.astype(BF16).astype(F32)
    middle = (logs - high).astype(BF16).astype(F32)
    low = (logs - high - middle).astype(BF16).astype(F32)
    heads = groups * pairs
    terms = (high + pltpu.roll(middle, heads, 1) + pltpu.roll(low, 2 * heads, 1)).astype(BF16)
    for s in range(videos):
        outs[s][:, width:] = terms[s * tok_rows : (s + 1) * tok_rows]


def join_kernel(groups, videos, *refs):
    back = in_order(refs[:videos])
    fresh_ref, log_ref, out_ref, done_ref, sems = refs[videos:]
    me = lax.axis_index("patch")
    own, mine = me // groups, me % groups
    _, tok_rows, width = fresh_ref.shape
    heads = width // DH
    pairs = heads // groups
    span = pairs * DH
    copies = []
    for s in range(videos):
        terms = back[s][:, width:].astype(F32)
        stale_log = terms + pltpu.roll(terms, DH - heads, 1) + pltpu.roll(terms, DH - 2 * heads, 1)
        share = 1.0 / (1.0 + jnp.exp(stale_log - log_ref[s]))
        for t in range(groups):
            parts = []
            for pair in range(pairs):
                head = t * pairs + pair
                here = slice(head * DH, (head + 1) * DH)
                stale = back[s][:, here].astype(F32)
                parts.append(stale + share[:, head : head + 1] * (fresh_ref[s, :, here] - stale))
            lanes = pl.ds(pl.multiple_of((mine ^ t) * span, DH), span)
            done_ref[s, :, lanes] = jnp.concatenate(parts, axis=1).astype(BF16)
        copies.append(pltpu.make_async_copy(done_ref.at[s], out_ref.at[own ^ s], sems.at[s]))
        copies[-1].start()
    for copy in copies:
        copy.wait()


def cache_kernel(got_ref, out_ref, sems):
    copies = []
    for pair in range(out_ref.shape[0]):
        lanes = pl.ds(2 * pair * DH, 2 * DH)
        copies.append(
            pltpu.make_async_copy(got_ref.at[:, :, lanes], out_ref.at[pair], sems.at[pair])
        )
        copies[-1].start()
    for copy in copies:
        copy.wait()


def permuted(array, offset, patches):
    return lax.ppermute(array, "patch", [(i, i ^ offset) for i in range(patches)])


def far_first(arrays):
    half = len(arrays) // 2
    return [*arrays[half:], *arrays[1:half], arrays[0]]


def in_order(arrays):
    half = len(arrays) // 2
    return [arrays[-1], *arrays[half:-1], *arrays[:half]]


def exchange(arrays, stride, patches):
    return [arrays[0]] + [
        permuted(arrays[s], s * stride, patches) for s in range(1, len(arrays))
    ]


def local(queries, keys, values, q_gain, k_gain, stale_cache, coords):
    videos, tok_rows, width = queries.shape
    pairs_here, total_rows, _ = stale_cache.shape
    patches = total_rows // tok_rows
    groups = patches // videos

    def kernel(body, name, limit, cost=0, **kwargs):
        return pl.pallas_call(
            body,
            name=name,
            compiler_params=pltpu.CompilerParams(vmem_limit_bytes=limit * MIB),
            cost_estimate=pl.CostEstimate(flops=cost, bytes_accessed=0, transcendentals=0),
            **kwargs,
        )

    gains = q_gain.reshape(1, width), k_gain.reshape(1, width)
    sent = kernel(
        functools.partial(lay_kernel, groups),
        "lay",
        56,
        out_shape=[jax.ShapeDtypeStruct((tok_rows, width + DH), BF16)] * videos,
        in_specs=[HBM] * 2,
        out_specs=[HBM] * videos,
        scratch_shapes=[
            pltpu.VMEM((videos, tok_rows, width + DH), BF16),
            pltpu.SMEM(coords.shape, jnp.int32),
            pltpu.SemaphoreType.DMA((2, videos)),
            pltpu.SemaphoreType.DMA,
        ],
    )(queries, coords)
    stale_sent, kept = lax.optimization_barrier((stale_cache, sent[0]))
    pieces = {0: stale_cache}
    bit = groups // 2
    pieces[bit] = permuted(stale_sent, bit, patches)
    query_raw = far_first(exchange([kept, *sent[1:]], groups, patches))
    fresh = kernel(
        key_kernel,
        "key",
        56,
        out_shape=jax.ShapeDtypeStruct((patches, tok_rows, 2 * pairs_here * DH), BF16),
        in_specs=[HBM] * 4,
        out_specs=HBM,
        scratch_shapes=[
            pltpu.VMEM(keys.shape, BF16),
            pltpu.VMEM(keys.shape, BF16),
            pltpu.VMEM((1, width), F32),
            pltpu.SMEM(coords.shape, jnp.int32),
            pltpu.VMEM((patches, tok_rows, 2 * pairs_here * DH), BF16),
            pltpu.SemaphoreType.DMA((4 + videos,)),
        ],
    )(keys, values, gains[1], coords)
    cached = lax.all_to_all(fresh, "patch", split_axis=0, concat_axis=0, tiled=True)
    query_raw, pieces, fresh = lax.optimization_barrier((query_raw, pieces, fresh))
    query_got = kernel(
        turn_kernel,
        "turn",
        16,
        cost=10**11,
        out_shape=jax.ShapeDtypeStruct(queries.shape, BF16),
        in_specs=[VMEM] * (1 + videos),
        out_specs=VMEM,
    )(gains[0], *query_raw)
    pieces, query_got = lax.optimization_barrier((pieces, query_got))
    while bit > 1:
        bit //= 2
        pieces.update({t | bit: permuted(piece, bit, patches) for t, piece in list(pieces.items())})
    result = kernel(
        functools.partial(stale_kernel, groups, videos),
        "stale",
        32,
        out_shape=[jax.ShapeDtypeStruct((tok_rows, width + DH), BF16)] * videos,
        in_specs=[VMEM] * (1 + groups),
        out_specs=[VMEM] * videos,
    )(query_got, *[pieces[t] for t in range(groups)])
    result, fresh_late, queries_late = lax.optimization_barrier((result, fresh, queries))
    query = kernel(
        query_kernel,
        "query",
        16,
        out_shape=jax.ShapeDtypeStruct(queries.shape, BF16),
        in_specs=[VMEM] * 2 + [SMEM],
        out_specs=VMEM,
    )(queries_late, gains[0], coords)
    back = far_first(exchange(result, groups, patches))
    fresh_sum, fresh_log = kernel(
        functools.partial(fresh_kernel, groups, videos),
        "fresh",
        16,
        out_shape=(
            jax.ShapeDtypeStruct((videos, tok_rows, width), F32),
            jax.ShapeDtypeStruct((videos, tok_rows, DH), F32),
        ),
        in_specs=[VMEM] * 2,
        out_specs=(VMEM, VMEM),
    )(query, fresh_late)
    fresh_sum, cached = lax.optimization_barrier((fresh_sum, cached))
    next_cache = kernel(
        cache_kernel,
        "cache",
        16,
        out_shape=jax.ShapeDtypeStruct((pairs_here, patches, tok_rows, 2 * DH), BF16),
        in_specs=[VMEM],
        out_specs=HBM,
        scratch_shapes=[pltpu.SemaphoreType.DMA((pairs_here,))],
    )(cached)
    attended = kernel(
        functools.partial(join_kernel, groups, videos),
        "join",
        16,
        out_shape=jax.ShapeDtypeStruct(queries.shape, BF16),
        in_specs=[VMEM] * (videos + 2),
        out_specs=HBM,
        scratch_shapes=[
            pltpu.VMEM(queries.shape, BF16),
            pltpu.SemaphoreType.DMA((videos,)),
        ],
    )(*back, fresh_sum, fresh_log)
    return (attended, next_cache.reshape(stale_cache.shape))


def solution(mesh):
    in_specs = (
        P("req", "patch", None),
        P("req", "patch", None),
        P("req", "patch", None),
        P(),
        P(),
        P(("req", "patch"), None, None),
        P(None, "patch"),
    )
    out_specs = (P("req", "patch", None), P(("req", "patch"), None, None))
    return jax.shard_map(local, mesh=mesh, in_specs=in_specs, out_specs=out_specs, check_vma=False)
```
